256 devices in a mesh: gx: 16 (over y, x), gy: 16 (over z, core).
Axes of the slice: x: 4, y: 4, z: 8, core: 2. Of those that a mesh axis runs over, the one named last changes fastest.
Arguments:
- field: float32 [3, 16, 1024, 2048], P(None, None, 'gx', 'gy'), may hold values from -6 to 6
- masks: int32 [2, 7, 32, 64], P(None, None, 'gx', 'gy'), may hold values 0 or 1
Outputs:
- restored: float32 [3, 16, 1024, 2048], P(None, None, 'gx', 'gy')
- coarse: float32 [3, 4, 256, 512], replicated
The draws below stay inside these ranges and needn't reach their ends.
All inputs are finite; a program needn't handle non-finite values. No bound on the sum of `masks` on one device may be relied on, other than what follows from the above.
Results may differ from the reference program's by a relative error of at most 0.00002.
Values sent between devices are 32-bit elements; how exact they have to be, the bound alone decides.
A program may use at most 128 MiB of HBM per device.

```python
import jax
import jax.numpy as jnp
from jax import lax

VARS = 3
NZ = 16
BLOCK = 32
LEVELS = 2
NX = 1024
NY = 2048


def with_ends(array, stream_key, smallest, largest):
    place = [jax.random.randint(jax.random.fold_in(stream_key, axis), (), 0, length) for axis, length in enumerate(array.shape)]
    longest = array.shape.index(max(array.shape))
    beside = place[:longest] + [(place[longest] + 1) % array.shape[longest]] + place[longest + 1:]
    return array.at[tuple(place)].set(smallest).at[tuple(beside)].set(largest)


def shard_levels(stream_key, shape, cuts, low, largest):
    loudness = 1.0
    for dim, shards_of in cuts:
        heights = jax.random.uniform(jax.random.fold_in(jax.random.fold_in(stream_key, 6), dim), (shards_of,), jnp.float32, low / len(cuts), largest / len(cuts))
        loudness = loudness * jnp.repeat(jnp.exp(heights), shape[dim] // shards_of).reshape((-1,) + (1,) * (len(shape) - 1 - dim))
    return loudness


def bell_draw(rng, shape, scale, limit, split=(), held_as=jnp.bfloat16):
    result = jax.random.normal(rng, shape, jnp.float32) * scale
    if len(split) > 0:
        result = shard_levels(rng, shape, split, -0.22, 0.18) * result
    return jnp.clip(result, min=-limit, max=limit).astype(held_as)


def setup_inputs(seed: int = 0) -> dict:
    seeds = jax.random.split(jax.random.key(seed), 3)
    field = bell_draw(seeds[0], (VARS, NZ, NX, NY), 1.0, 6.0, ((2, 16), (3, 16)), jnp.float32)
    masks = with_ends((jax.random.randint(seeds[1], (LEVELS, 7, NX // BLOCK, NY // BLOCK), 0, 2) < 1).astype(jnp.int32), jax.random.fold_in(seeds[1], 1), 0, 1)
    return {"field": field, "masks": masks}


def take_slice(volume, start, stop, stride, direction):
    return lax.slice_in_dim(volume, start, stop, stride, direction)


def lift_forward(padded, direction):
    length = padded.shape[direction] - 4
    even_cells = take_slice(padded, 2, length + 2, 2, direction)
    odd_cells = take_slice(padded, 3, length + 3, 2, direction)
    next_even = take_slice(padded, 4, length + 4, 2, direction)
    detail = odd_cells - 0.5 * (even_cells + next_even)
    first_detail = take_slice(padded, 1, 2, 1, direction) - 0.5 * (take_slice(padded, 0, 1, 1, direction) + take_slice(padded, 2, 3, 1, direction))
    previous = jnp.concatenate([first_detail, take_slice(detail, 0, length // 2 - 1, 1, direction)], direction)
    smooth = even_cells + 0.25 * (previous + detail)
    return jnp.concatenate([smooth, detail], 0)


def lift_inverse(padded, direction):
    middle = padded.shape[0] // 2
    smooth_pad = padded[:middle]
    detail_pad = padded[middle:]
    length = padded.shape[direction] - 2
    even_ext = take_slice(smooth_pad, 1, length + 2, 1, direction) - 0.25 * (take_slice(detail_pad, 0, length + 1, 1, direction) + take_slice(detail_pad, 1, length + 2, 1, direction))
    even_cells = take_slice(even_ext, 0, length, 1, direction)
    next_even = take_slice(even_ext, 1, length + 1, 1, direction)
    odd_cells = take_slice(detail_pad, 1, length + 1, 1, direction) + 0.5 * (even_cells + next_even)
    target_shape = list(even_cells.shape)
    target_shape[direction] = 2 * length
    return jnp.stack([even_cells, odd_cells], direction + 1).reshape(target_shape)


def wrap_local(volume, direction, margin):
    length = volume.shape[direction]
    return jnp.concatenate([take_slice(volume, length - margin, length, 1, direction), volume, take_slice(volume, 0, margin, 1, direction)], direction)


def mirror_forward(volume, direction):
    length = volume.shape[direction]
    return jnp.concatenate([take_slice(volume, 2, 3, 1, direction), take_slice(volume, 1, 2, 1, direction), volume, take_slice(volume, length - 2, length - 1, 1, direction), take_slice(volume, length - 3, length - 2, 1, direction)], direction)


def mirror_inverse(volume, direction):
    middle = volume.shape[0] // 2
    length = volume.shape[direction]
    smooth = volume[:middle]
    detail = volume[middle:]
    smooth_pad = jnp.concatenate([take_slice(smooth, 0, 1, 1, direction), smooth, take_slice(smooth, length - 1, length, 1, direction)], direction)
    detail_pad = jnp.concatenate([take_slice(detail, 0, 1, 1, direction), detail, take_slice(detail, length - 2, length - 1, 1, direction)], direction)
    return jnp.concatenate([smooth_pad, detail_pad], 0)


def expand_mask(mask_block, block_width):
    return jnp.repeat(jnp.repeat(mask_block, block_width, 1), block_width, 2).astype(jnp.float32)


def forward_level(volume):
    volume = lift_forward(wrap_local(volume, 3, 2), 3)
    volume = lift_forward(wrap_local(volume, 4, 2), 4)
    return lift_forward(mirror_forward(volume, 2), 2)


def inverse_level(volume):
    volume = lift_inverse(mirror_inverse(volume, 2), 2)
    volume = lift_inverse(wrap_local(volume, 4, 1), 4)
    return lift_inverse(wrap_local(volume, 3, 1), 3)


def reference(field, masks):
    def one_variable(values):
        volume = values[None, None]
        detail_list = []
        for level_index in range(LEVELS):
            volume = forward_level(volume)
            kept_mask = expand_mask(masks[level_index], BLOCK >> (level_index + 1))
            detail_list.append(volume[1:] * kept_mask[:, None, None, :, :])
            volume = volume[:1]
        coarse = volume[0, 0]
        for level_index in range(LEVELS - 1, -1, -1):
            volume = inverse_level(jnp.concatenate([volume, detail_list[level_index]], 0))
        return volume[0, 0], coarse

    restored, coarse = lax.map(one_variable, field)
    return restored, coarse
```

```python
import jax
import jax.numpy as jnp
import numpy as np
from jax import lax
from jax.experimental import pallas as pl
from jax.experimental.pallas import tpu as pltpu
from jax.sharding import PartitionSpec as P

MESH = pl.DeviceIdType.MESH
F32 = jnp.float32
BF16 = jnp.bfloat16
VARS, NZ, ROWS, COLS = 3, 16, 64, 128
PLANES = VARS * NZ
CLASS = 12
MESSAGES = 80

SMOOTH = {0: 0.75, -2: -0.125, 2: -0.125, -1: 0.25, 1: 0.25}
DETAIL = {0: -0.5, 1: 1.0, 2: -0.5}


def lane_filters():
    def cell(x):
        return x if x >= 0 else 144 + x

    first = np.zeros((256, 256), np.float32)
    for k in range(-2, 67):
        for t, w in SMOOTH.items():
            first[cell(2 * k + t), k + 2] += w
        for t, w in DETAIL.items():
            first[cell(2 * k + t), 128 + k + 2] += w
    second = np.zeros((128, 128), np.float32)
    for m in range(0, 33):
        for t, w in SMOOTH.items():
            second[2 * m + t + 2, m + 2] += w
    for m in range(-1, 33):
        for t, w in DETAIL.items():
            second[2 * m + t + 2, 64 + m + 2] += w

    def inverse(count, out, offset, smooth, detail):
        matrix = np.zeros((2 * smooth(-2) + 2 * detail(-2), out), np.float32)
        for x in range(count):
            k, odd = divmod(x, 2)
            col = x + offset
            if odd:
                matrix[smooth(k), col] += 0.5
                matrix[smooth(k + 1), col] += 0.5
                matrix[detail(k), col] += 0.75
                matrix[detail(k - 1), col] -= 0.125
                matrix[detail(k + 1), col] -= 0.125
            else:
                matrix[smooth(k), col] += 1.0
                matrix[detail(k - 1), col] -= 0.25
                matrix[detail(k), col] -= 0.25
        return matrix

    back_first = inverse(128, 128, 0, lambda k: k + 2, lambda k: 128 + k + 2)
    back_second = inverse(65, 128, 2, lambda k: k + 2, lambda k: 64 + k + 2)
    packed = np.zeros((512, 256), np.float32)
    packed[:256] = first
    packed[256:, :128] = back_first
    packed[256:384, 128:] = second
    packed[384:, 128:] = back_second
    return packed.astype(BF16)


def halves(x):
    high = x.astype(BF16)
    low = (x - high.astype(F32)).astype(BF16)
    return high, low


def split_dot(x, filters):
    high, low = halves(x)
    return jnp.dot(high, filters, preferred_element_type=F32) + jnp.dot(low, filters, preferred_element_type=F32)


def forward_planes(x):
    count = len(x) // 2
    detail = []
    for k in range(count):
        after = x[2 * k + 2] if k + 1 < count else x[2 * count - 2]
        detail.append(x[2 * k + 1] - 0.5 * (x[2 * k] + after))
    smooth = [x[2 * k] + 0.25 * (detail[max(k - 1, 0)] + detail[k]) for k in range(count)]
    return smooth, detail


def inverse_planes(smooth, detail):
    count = len(smooth)
    even = [smooth[k] - 0.25 * (detail[max(k - 1, 0)] + detail[k]) for k in range(count)]
    out = []
    for k in range(count):
        out += [even[k], detail[k] + 0.5 * (even[k] + even[min(k + 1, count - 1)])]
    return out


def plane_slots(var):
    smooth = [4 * var + k for k in range(4)]
    middle = [12 + 4 * var + k for k in range(4)]
    fine = [24 + 8 * var + k for k in range(8)]
    return smooth, middle, fine


def kernel(
    field_ref, mk_ref, filt_ref, restored_ref, g_ref,
    x_ref, w_ref, t_ref, rp_ref, lp_ref, hl_ref, hr_ref, nk_ref, lhs_ref, y_ref, c_ref, s1_ref, s1l_ref, c2_ref,
    u_ref, m1_ref, m2_ref, own_ref, parts_ref, lhsi_ref, zr_ref, load_sem, send_sem, recv_sem,
):
    gx = lax.axis_index("gx")
    gy = lax.axis_index("gy")
    yy, xx = gx // 4, gx % 4
    zz, core = gy // 2, gy % 2
    group, low = gy // 4, zz % 2
    side = 2 * low - 1

    up, down = (gx + 15) % 16, (gx + 1) % 16
    left, right = (gy + 15) % 16, (gy + 1) % 16
    around = [(up, gy), (down, gy), (gx, left), (gx, right), (up, left), (up, right), (down, left), (down, right)]
    flip1 = gy + 1 - 2 * core
    flip2 = gy + 2 - 4 * low
    flip3 = flip2 + 1 - 2 * core
    sibling = (gx, flip1)
    pair = (gx, flip2)
    cross = (gx, (gy + 2 * side + 16) % 16)

    def along_x(k):
        return (yy * 4 + (xx + k) % 4, gy)

    def along_y(k):
        return (((yy + k) % 4) * 4 + xx, gy)

    def along_z(k):
        return (gx, (gy + 2 * side * k + 16) % 16)

    greeted = around + [(gx, flip1), (gx, flip2), (gx, flip3)]
    greeted += [along_x(k) for k in (1, 2, 3)] + [along_y(k) for k in (1, 2, 3)]
    greeted += [along_z(k) for k in (1, 2, -2, 3)]

    loads = [
        pltpu.make_async_copy(field_ref, x_ref, load_sem.at[0]),
        pltpu.make_async_copy(filt_ref, w_ref, load_sem.at[1]),
    ]
    for copy in loads:
        copy.start()
    barrier = pltpu.get_barrier_semaphore()
    for device in greeted:
        pl.semaphore_signal(barrier, inc=1, device_id=device, device_id_type=MESH)

    sent = []

    def send(src, dst, device):
        i = len(sent)
        copy = pltpu.make_async_remote_copy(
            src_ref=src, dst_ref=dst, send_sem=send_sem.at[i], recv_sem=recv_sem.at[i],
            device_id=device, device_id_type=MESH,
        )
        copy.start()
        sent.append(copy)
        return copy

    lane = lax.broadcasted_iota(jnp.int32, (1, 128), 1)

    loads[0].wait()
    for var in range(VARS):
        slots = plane_slots(var)

        def lift(tile, _, var=var, slots=slots):
            rows = pl.ds(pl.multiple_of(tile * 8, 8), 8)
            x = [x_ref[var * NZ + k, rows, :] for k in range(NZ)]
            smooth, fine = forward_planes(x)
            smooth, middle = forward_planes(smooth)
            ext = pl.ds(pl.multiple_of(tile * 8 + 8, 8), 8)
            for slot, value in zip(slots[0] + slots[1] + slots[2], smooth + middle + fine):
                t_ref[slot, ext, :] = value
            return _

        lax.fori_loop(0, 8, lift, None)

    def pack(q):
        rightward = jnp.zeros((ROWS, 128), F32)
        leftward = jnp.zeros((ROWS, 128), F32)
        for j in range(CLASS):
            plane = t_ref[q * CLASS + j, 8:72, :]
            here = (lane >= 8 * j) & (lane < 8 * j + 8)
            rightward = jnp.where(here, pltpu.roll(plane, (8 * j + 8) % 128, 1), rightward)
            leftward = jnp.where(here, pltpu.roll(plane, 8 * j, 1) if j else plane, leftward)
        rp_ref[q] = rightward
        lp_ref[q] = leftward

    def send_halo(q, n):
        p = pl.ds(q * CLASS, n * CLASS)
        c = pl.ds(q, n)
        return [
            send(rp_ref.at[c], hl_ref.at[c, 8:72], (gx, right)),
            send(lp_ref.at[c], hr_ref.at[c, 8:72], (gx, left)),
            send(t_ref.at[p, 64:72], t_ref.at[p, 0:8], (down, gy)),
            send(t_ref.at[p, 8:16], t_ref.at[p, 72:80], (up, gy)),
            send(rp_ref.at[c, 56:64], hl_ref.at[c, 0:8], (down, right)),
            send(rp_ref.at[c, 0:8], hl_ref.at[c, 72:80], (up, right)),
            send(lp_ref.at[c, 56:64], hr_ref.at[c, 0:8], (down, left)),
            send(lp_ref.at[c, 0:8], hr_ref.at[c, 72:80], (up, left)),
        ]

    pack(0)
    pl.semaphore_wait(barrier, len(greeted))
    halo0 = send_halo(0, 1)
    masks_in = [send(mk_ref, nk_ref.at[n], device) for n, device in enumerate(around)]
    for q in (1, 2, 3):
        pack(q)
    halo1 = send_halo(1, 3)
    loads[1].wait()

    def expand_masks():
        for copy in masks_in:
            copy.wait_recv()
        below, above, from_right, from_left, below_right, below_left, above_right, above_left = (
            nk_ref.at[n] for n in range(8)
        )
        bands = [(above_left, above, above_right, 1), (from_left, mk_ref, from_right, 0),
                 (from_left, mk_ref, from_right, 1), (below_left, below, below_right, 0)]
        wide = [[], []]
        for a, b, c, i in bands:
            wide[0].append(jnp.where(
                lane < 2, pltpu.roll(a[0, i], 66, 1),
                jnp.where(lane < 66, pltpu.roll(b[0, i], 2, 1), pltpu.roll(c[0, i], 66, 1))))
            base = jnp.where(
                lane < 2, pltpu.roll(a[1, i], 98, 1),
                jnp.where(lane < 34, pltpu.roll(b[1, i], 2, 1), pltpu.roll(c[1, i], 34, 1)))
            wide[1].append((base, pltpu.roll(base, 64, 1)))
        row = lax.broadcasted_iota(jnp.int32, (40, 128), 0)

        def by_rows(values, edges, count):
            out = jnp.broadcast_to(values[0], (count, 128))
            for value, edge in zip(values[1:], edges):
                out = jnp.where(row[:count] >= edge, jnp.broadcast_to(value, (count, 128)), out)
            return out

        for bz in range(2):
            for rd in range(2):
                for ld in range(2):
                    b = 4 * bz + 2 * ld + rd
                    m1_ref[bz, rd, :, 128 * ld:128 * ld + 128] = by_rows(
                        [v[b:b + 1] for v in wide[0]], (3, 19, 35), 40)
                b = 4 * bz + rd
                values = [jnp.where(lane < 64, v[b:b + 1], w[b + 2:b + 3]) for v, w in wide[1]]
                m2_ref[bz, rd] = by_rows(values, (rd, 8 + rd, 16 + rd), 24)

    def lanes1(q):
        for j in range(CLASS):
            sides = jnp.where(
                lane < 8, pltpu.roll(hr_ref[q], (128 - 8 * j) % 128, 1) if j else hr_ref[q],
                pltpu.roll(hl_ref[q], (136 - 8 * j) % 128, 1))
            for col, value in ((0, t_ref[q * CLASS + j]), (128, sides)):
                high, low_part = halves(value)
                lhs_ref[80 * j:80 * j + 80, col:col + 128] = high
                lhs_ref[80 * j:80 * j + 80, 256 + col:384 + col] = low_part
        filters = w_ref[0:256, :]
        both = jnp.concatenate([filters, filters], 0)

        def step(i, _):
            rows = pl.ds(pl.multiple_of(i * 320, 320), 320)
            out = jnp.dot(lhs_ref[rows, :], both, preferred_element_type=F32)
            for half in range(2):
                y_ref[pl.ds(q * CLASS + 4 * i, 4), half, 0:80, :] = out[:, 128 * half:128 * half + 128].reshape(4, 80, 128)
            return _

        lax.fori_loop(0, 3, step, None)

    def rows1(q):
        bz = 0 if q < 2 else 1

        def one(p):
            for half in range(2):
                cols = slice(128 * half, 128 * half + 128)
                even0, even1, even2 = (y_ref[p, half, pl.ds(s, 40, stride=2), :] for s in (0, 2, 4))
                odd0, odd1 = (y_ref[p, half, pl.ds(s, 40, stride=2), :] for s in (1, 3))
                detail = odd1 - 0.5 * (even1 + even2)
                before = odd0 - 0.5 * (even0 + even1)
                smooth = even1 + 0.25 * (before + detail)
                c_ref[p, 1, 0:40, cols] = detail * m1_ref[bz, 1, :, cols]
                if q < 2 and half == 0:
                    s1_ref[p] = smooth
                else:
                    c_ref[p, 0, 0:40, cols] = smooth * m1_ref[bz, 0, :, cols]

        def step(i, _):
            one(q * CLASS + 2 * i)
            one(q * CLASS + 2 * i + 1)
            return _

        lax.fori_loop(0, CLASS // 2, step, None)

    def lanes2(q):
        x = s1_ref[q * CLASS:(q + 1) * CLASS].reshape(CLASS * 40, 128)
        s1l_ref[q * CLASS:(q + 1) * CLASS, 0:40, :] = split_dot(x, w_ref[256:384, 128:256]).reshape(CLASS, 40, 128)

    def rows2(q):
        for p in range(q * CLASS, (q + 1) * CLASS):
            even0, even1, even2 = (s1l_ref[p, pl.ds(s, 24, stride=2), :] for s in (1, 3, 5))
            odd0, odd1 = (s1l_ref[p, pl.ds(s, 24, stride=2), :] for s in (2, 4))
            before = odd0 - 0.5 * (even0 + even1)
            detail = odd1 - 0.5 * (even1 + even2)
            smooth = even1 + 0.25 * (before + detail)
            if q == 0:
                local = jnp.where((lane >= 2) & (lane < 34), smooth[0:16], 0.0)
                own_ref[p] = pltpu.roll(local, (32 * (gy % 4) + 126) % 128, 1)
            c2_ref[p, 0, 0:24] = smooth * m2_ref[q, 0]
            c2_ref[p, 1, 0:24] = before * m2_ref[q, 1]

    def back2(q):
        for p in range(q * CLASS, (q + 1) * CLASS):
            smooth0, smooth1 = (c2_ref[p, 0, s:s + 24, :] for s in (0, 1))
            detail0, detail1, detail2 = (c2_ref[p, 1, s:s + 24, :] for s in (0, 1, 2))
            even = smooth0 - 0.25 * (detail0 + detail1)
            after = smooth1 - 0.25 * (detail1 + detail2)
            u_ref[p, pl.ds(3, 24, stride=2), :] = even
            u_ref[p, pl.ds(4, 24, stride=2), :] = detail1 + 0.5 * (even + after)
        x = u_ref[q * CLASS:(q + 1) * CLASS, 0:40, :].reshape(CLASS * 40, 128)
        c_ref[q * CLASS:(q + 1) * CLASS, 0, 0:40, 0:128] = split_dot(x, w_ref[384:512, 128:256]).reshape(CLASS, 40, 128)

    def back1(q):
        def one(p, j):
            for half in range(2):
                cols = slice(128 * half, 128 * half + 128)
                smooth0, smooth1 = (c_ref[p, 0, s:s + 32, cols] for s in (3, 4))
                detail0, detail1, detail2 = (c_ref[p, 1, s:s + 32, cols] for s in (2, 3, 4))
                even = smooth0 - 0.25 * (detail0 + detail1)
                after = smooth1 - 0.25 * (detail1 + detail2)
                odd = detail1 + 0.5 * (even + after)
                for which, value in ((0, even), (1, odd)):
                    rows = pl.ds(pl.multiple_of(j * 64 + 32 * which, 32), 32)
                    high, low_part = halves(value)
                    lhsi_ref[rows, cols] = high
                    lhsi_ref[rows, slice(256 + 128 * half, 384 + 128 * half)] = low_part

        def step(i, _):
            one(q * CLASS + 2 * i, 2 * i)
            one(q * CLASS + 2 * i + 1, 2 * i + 1)
            return _

        lax.fori_loop(0, CLASS // 2, step, None)
        filters = w_ref[256:512, 0:128]
        both = jnp.concatenate([filters, filters], 0)

        def multiply(i, _):
            rows = pl.ds(pl.multiple_of(i * 256, 256), 256)
            out = jnp.dot(lhsi_ref[rows, :], both, preferred_element_type=F32)
            zr_ref[pl.ds(q * CLASS + 4 * i, 4)] = out.reshape(4, 64, 128)
            return _

        lax.fori_loop(0, 3, multiply, None)

    def finish():
        for var in range(VARS):
            slots = plane_slots(var)
            for odd in range(2):
                for tile in range(4):
                    rows = slice(32 * odd + 8 * tile, 32 * odd + 8 * tile + 8)
                    smooth, middle, fine = ([zr_ref[p, rows, :] for p in part] for part in slots)
                    out = inverse_planes(inverse_planes(smooth, middle), fine)
                    for k in range(NZ):
                        restored_ref[var * NZ + k, pl.ds(16 * tile + odd, 8, stride=2), :] = out[k]

    def lanes_of(block):
        return pl.ds(pl.multiple_of(128 * ((block + 4) % 4), 128), 128)

    base = 6 * core
    p0, p1, p2 = (pl.ds(base + 2 * r, 2) for r in range(3))

    def both_ways(view, step):
        src = view(0)
        return send(src, src, step(1)), send(src, src, step(3))

    def pass_on(view, half_view, step, came):
        came[0].wait_recv()
        a = half_view(0, -1)
        first = send(a, a, step(1))
        came[1].wait_recv()
        b = half_view(1, 1)
        return first, send(b, b, step(3))

    def to_sibling(ref):
        return send(ref, ref, sibling)

    expand_masks()
    for copy in halo0:
        copy.wait_recv()
    lanes1(0)
    rows1(0)
    lanes2(0)
    rows2(0)
    other = 1 - core
    pre = [
        send(own_ref.at[pl.ds(6 * other, 6)], parts_ref.at[0], (gx, flip1)),
        send(own_ref.at[pl.ds(6 * core, 6)], parts_ref.at[1], (gx, flip2)),
        send(own_ref.at[pl.ds(6 * other, 6)], parts_ref.at[2], (gx, flip3)),
    ]
    for copy in halo1:
        copy.wait_recv()
    for copy in pre:
        copy.wait_recv()
    block = own_ref[pl.ds(base, 6)] + parts_ref[0] + parts_ref[1] + parts_ref[2]
    g_ref[pl.ds(base, 6), yy, xx, :, lanes_of(group)] = block

    mine0 = g_ref.at[p0, yy, xx, :, lanes_of(group)]
    xs = [send(mine0, mine0, along_x(k)) for k in (1, 3, 2)]
    mine12 = g_ref.at[pl.ds(base + 2, 4), yy, xx, :, lanes_of(group)]
    zs = [send(mine12, mine12, along_z(k)) for k in (1, 2, 3)]

    lanes1(1)
    rows1(1)

    def y0(k):
        return g_ref.at[p0, (yy + k + 4) % 4, :, :, lanes_of(group)]

    def y0_half(h, k):
        return g_ref.at[base + h, (yy + k + 4) % 4, :, :, lanes_of(group)]

    def x1(k):
        return g_ref.at[p1, yy, (xx + k + 4) % 4]

    def x1_half(h, k):
        return g_ref.at[base + 2 + h, yy, (xx + k + 4) % 4]

    def y2(k):
        return g_ref.at[p2, (yy + k + 4) % 4, xx]

    def y2_half(h, k):
        return g_ref.at[base + 4 + h, (yy + k + 4) % 4, xx]

    for copy in xs:
        copy.wait_recv()
    a0 = both_ways(y0, along_y)
    for copy in zs:
        copy.wait_recv()
    a1 = both_ways(x1, along_x)
    a2 = both_ways(y2, along_y)
    lanes2(1)
    rows2(1)
    f0 = pass_on(y0, y0_half, along_y, a0)
    f1 = pass_on(x1, x1_half, along_x, a1)
    f2 = pass_on(y2, y2_half, along_y, a2)
    back2(0)

    def z0(k):
        return g_ref.at[p0, :, :, :, lanes_of(group + k)]

    def z0_half(h, k):
        return g_ref.at[base + h, :, :, :, lanes_of(group + k)]

    def y1(k):
        return g_ref.at[p1, (yy + k + 4) % 4]

    def y1_half(h, k):
        return g_ref.at[base + 2 + h, (yy + k + 4) % 4]

    def x2(k):
        return g_ref.at[p2, :, (xx + k + 4) % 4]

    def x2_half(h, k):
        return g_ref.at[base + 4 + h, :, (xx + k + 4) % 4]

    for copy in f0:
        copy.wait_recv()
    c1 = send(z0(0), z0(0), cross)
    for copy in f1:
        copy.wait_recv()
    b1 = both_ways(y1, along_y)
    for copy in f2:
        copy.wait_recv()
    b2 = both_ways(x2, along_x)
    sib = [to_sibling(z0(0)), to_sibling(y1(0)), to_sibling(x2(0))]
    back2(1)
    lanes1(2)
    rows1(2)
    c1.wait_recv()
    c2 = send(z0(side), z0(side), pair)
    sib.append(to_sibling(z0(side)))
    e1 = pass_on(y1, y1_half, along_y, b1)
    e2 = pass_on(x2, x2_half, along_x, b2)
    for view in (y1, x2):
        sib += [to_sibling(view(-1)), to_sibling(view(1))]
    lanes1(3)
    rows1(3)
    c2.wait_recv()
    c3 = send(z0_half(1 - low, -side), z0_half(1 - low, -side), cross)
    sib.append(to_sibling(z0(-side)))
    back1(0)
    back1(1)
    c3.wait_recv()
    c4 = send(z0_half(low, 2), z0_half(low, 2), pair)
    for copy in e1:
        copy.wait_recv()
    sib.append(to_sibling(y1(2)))
    for copy in e2:
        copy.wait_recv()
    sib.append(to_sibling(x2(2)))
    back1(2)
    back1(3)
    c4.wait_recv()
    sib.append(to_sibling(z0(2)))
    finish()
    for copy in sib:
        copy.wait_recv()
    for copy in sent:
        copy.wait_send()


def body(field, masks):
    flags = masks.astype(F32)
    level1 = jnp.pad(jnp.repeat(flags[0], 16, 2), ((1, 0), (0, 0), (0, 64)), constant_values=1.0)
    level2 = jnp.pad(jnp.repeat(flags[1], 8, 2), ((1, 0), (0, 0), (0, 96)), constant_values=1.0)
    mk = jnp.stack([level1, level2]).transpose(0, 2, 1, 3)
    anywhere = pl.BlockSpec(memory_space=pl.ANY)
    in_vmem = pl.BlockSpec(memory_space=pltpu.VMEM)
    restored, coarse = pl.pallas_call(
        kernel,
        out_shape=(
            jax.ShapeDtypeStruct((PLANES, ROWS, COLS), F32),
            jax.ShapeDtypeStruct((12, 4, 4, 16, 512), F32),
        ),
        in_specs=[anywhere, in_vmem, anywhere],
        out_specs=(in_vmem, in_vmem),
        scratch_shapes=[
            pltpu.VMEM((PLANES, ROWS, COLS), F32),
            pltpu.VMEM((512, 256), BF16),
            pltpu.VMEM((PLANES, 80, 128), F32),
            pltpu.VMEM((4, ROWS, 128), F32),
            pltpu.VMEM((4, ROWS, 128), F32),
            pltpu.VMEM((4, 80, 128), F32),
            pltpu.VMEM((4, 80, 128), F32),
            pltpu.VMEM((8, 2, 2, 8, 128), F32),
            pltpu.VMEM((CLASS * 80, 512), BF16),
            pltpu.VMEM((PLANES, 2, 88, 128), F32),
            pltpu.VMEM((PLANES, 2, 40, 256), F32),
            pltpu.VMEM((2 * CLASS, 40, 128), F32),
            pltpu.VMEM((2 * CLASS, 56, 128), F32),
            pltpu.VMEM((2 * CLASS, 2, 32, 128), F32),
            pltpu.VMEM((2 * CLASS, 56, 128), F32),
            pltpu.VMEM((2, 2, 40, 256), F32),
            pltpu.VMEM((2, 2, 24, 128), F32),
            pltpu.VMEM((CLASS, 16, 128), F32),
            pltpu.VMEM((3, 6, 16, 128), F32),
            pltpu.VMEM((CLASS * 64, 512), BF16),
            pltpu.VMEM((PLANES, 64, 128), F32),
            pltpu.SemaphoreType.DMA((2,)),
            pltpu.SemaphoreType.DMA((MESSAGES,)),
            pltpu.SemaphoreType.DMA((MESSAGES,)),
        ],
        compiler_params=pltpu.CompilerParams(
            collective_id=0, has_side_effects=True, vmem_limit_bytes=48 * 1024 * 1024
        ),
        cost_estimate=pl.CostEstimate(flops=2_000_000_000, bytes_accessed=10_000_000, transcendentals=0),
    )(field.reshape(PLANES, ROWS, COLS), mk, jnp.asarray(lane_filters()))
    return restored.reshape(VARS, NZ, ROWS, COLS), coarse.reshape(VARS, 4, 256, 512)


def solution(mesh):
    placed = (P(None, None, "gx", "gy"), P(None, None, "gx", "gy"))
    return jax.shard_map(
        body,
        mesh=mesh,
        in_specs=placed,
        out_specs=(P(None, None, "gx", "gy"), P()),
        check_vma=False,
    )
```

```python
import jax
import jax.numpy as jnp
from jax import lax
from jax.experimental import pallas as pl
from jax.experimental.pallas import tpu as pltpu
from jax.sharding import PartitionSpec as P

MESH = pl.DeviceIdType.MESH
F32 = jnp.float32
BF16 = jnp.bfloat16
VARS, NZ, ROWS, COLS = 3, 16, 64, 128
PLANES = VARS * NZ
CLASS = 12
MESSAGES = 128
VMEM_LIMIT = 32 * 1024 * 1024


def by_distance(distance, taps):
    out = jnp.zeros(distance.shape, F32)
    for at, weight in taps.items():
        out = jnp.where(distance == at, weight, out)
    return out


FORWARD_SMOOTH = {0: 0.75, -2: -0.125, 2: -0.125, -1: 0.25, 1: 0.25}
FORWARD_DETAIL = {0: -0.5, 1: 1.0, 2: -0.5}
INVERSE_SMOOTH = {0: 1.0, -1: 0.5, 1: 0.5}
INVERSE_DETAIL = {1: 0.75, 0: -0.25, 2: -0.25, -1: -0.125, 3: -0.125}


def write_filters(w_ref):
    row = lax.broadcasted_iota(jnp.int32, (256, 128), 0)
    col = lax.broadcasted_iota(jnp.int32, (256, 128), 1)
    cell = jnp.where(row < 136, row, jnp.where(row < 144, row - 144, 4096))
    w_ref[0:256, 0:128] = by_distance(cell - 2 * (col - 2), FORWARD_SMOOTH).astype(BF16)
    w_ref[0:256, 128:256] = by_distance(cell - 2 * (col - 2), FORWARD_DETAIL).astype(BF16)
    w_ref[256:384, 0:128] = by_distance(col[:128] - 2 * (row[:128] - 2), INVERSE_SMOOTH).astype(BF16)
    w_ref[384:512, 0:128] = by_distance(col[:128] - 2 * (row[:128] - 2), INVERSE_DETAIL).astype(BF16)
    row, col = row[:128], col[:128]
    ahead = row - 2 - 2 * (jnp.where(col < 64, col, col - 64) - 2)
    w_ref[256:384, 128:256] = jnp.where(
        col < 64, by_distance(ahead, FORWARD_SMOOTH), by_distance(ahead, FORWARD_DETAIL)).astype(BF16)
    ahead = col - 2 - 2 * (jnp.where(row < 64, row, row - 64) - 2)
    w_ref[384:512, 128:256] = jnp.where(
        row < 64, by_distance(ahead, INVERSE_SMOOTH), by_distance(ahead, INVERSE_DETAIL)).astype(BF16)


def halves(x):
    high = x.astype(BF16)
    low = (x - high.astype(F32)).astype(BF16)
    return high, low


def split_dot(x, filters):
    high, low = halves(x)
    return jnp.dot(high, filters, preferred_element_type=F32) + jnp.dot(low, filters, preferred_element_type=F32)


def forward_planes(x):
    count = len(x) // 2
    detail = []
    for k in range(count):
        after = x[2 * k + 2] if k + 1 < count else x[2 * count - 2]
        detail.append(x[2 * k + 1] - 0.5 * (x[2 * k] + after))
    smooth = [x[2 * k] + 0.25 * (detail[max(k - 1, 0)] + detail[k]) for k in range(count)]
    return smooth, detail


def inverse_planes(smooth, detail):
    count = len(smooth)
    even = [smooth[k] - 0.25 * (detail[max(k - 1, 0)] + detail[k]) for k in range(count)]
    out = []
    for k in range(count):
        out += [even[k], detail[k] + 0.5 * (even[k] + even[min(k + 1, count - 1)])]
    return out


def plane_slots(var):
    smooth = [4 * var + k for k in range(4)]
    middle = [12 + 4 * var + k for k in range(4)]
    fine = [24 + 8 * var + k for k in range(8)]
    return smooth, middle, fine


def kernel(
    field_ref, masks_ref, restored_ref, g_ref,
    x_ref, mk_ref, w_ref, t_ref, rp_ref, lp_ref, hl_ref, hr_ref, nk_ref, lhs_ref, y_ref, c_ref, s1_ref, s1l_ref, c2_ref,
    u_ref, m1_ref, m2_ref, own_ref, parts_ref, lhsi_ref, zr_ref, j_ref, load_sem, send_sem, recv_sem,
):
    gx = lax.axis_index("gx")
    gy = lax.axis_index("gy")
    yy, xx = gx // 4, gx % 4
    zz, core = gy // 2, gy % 2
    group, low = gy // 4, zz % 2
    side = 2 * low - 1

    up, down = (gx + 15) % 16, (gx + 1) % 16
    left, right = (gy + 15) % 16, (gy + 1) % 16
    around = [(up, gy), (down, gy), (gx, left), (gx, right), (up, left), (up, right), (down, left), (down, right)]
    flip1 = gy + 1 - 2 * core
    flip2 = gy + 2 - 4 * low
    flip3 = flip2 + 1 - 2 * core
    sibling = (gx, flip1)
    pair = (gx, flip2)
    cross = (gx, (gy + 2 * side + 16) % 16)

    def along_x(k):
        return (yy * 4 + (xx + k) % 4, gy)

    def along_y(k):
        return (((yy + k) % 4) * 4 + xx, gy)

    def along_z(k):
        return (gx, (gy + 2 * side * k + 16) % 16)

    greeted = around + [(gx, flip1), (gx, flip2), (gx, flip3)]
    greeted += [along_x(k) for k in (1, 2, 3)] + [along_y(k) for k in (1, 2, 3)]
    greeted += [along_z(k) for k in (1, 2, -2, 3)]

    loads = [
        pltpu.make_async_copy(field_ref.at[NZ * v:NZ * v + NZ], x_ref.at[NZ * v:NZ * v + NZ], load_sem.at[v])
        for v in range(VARS)
    ]
    loads.append(pltpu.make_async_copy(masks_ref, mk_ref, load_sem.at[VARS]))
    for copy in loads:
        copy.start()
    barrier = pltpu.get_barrier_semaphore()
    for device in greeted:
        pl.semaphore_signal(barrier, inc=1, device_id=device, device_id_type=MESH)

    write_filters(w_ref)
    sent = []

    def send(src, dst, device):
        i = len(sent)
        copy = pltpu.make_async_remote_copy(
            src_ref=src, dst_ref=dst, send_sem=send_sem.at[i], recv_sem=recv_sem.at[i],
            device_id=device, device_id_type=MESH,
        )
        copy.start()
        sent.append(copy)
        return copy

    lane = lax.broadcasted_iota(jnp.int32, (1, 128), 1)

    for var in range(VARS):
        slots = plane_slots(var)
        loads[var].wait()

        def lift(tile, _, var=var, slots=slots):
            rows = pl.ds(pl.multiple_of(tile * 8, 8), 8)
            x = [x_ref[var * NZ + k, rows, :] for k in range(NZ)]
            smooth, fine = forward_planes(x)
            smooth, middle = forward_planes(smooth)
            ext = pl.ds(pl.multiple_of(tile * 8 + 8, 8), 8)
            for slot, value in zip(slots[0] + slots[1] + slots[2], smooth + middle + fine):
                t_ref[slot, ext, :] = value
            return _

        lax.fori_loop(0, 8, lift, None)

    def pack(q):
        rightward = jnp.zeros((ROWS, 128), F32)
        leftward = jnp.zeros((ROWS, 128), F32)
        for j in range(CLASS):
            plane = t_ref[q * CLASS + j, 8:72, :]
            here = (lane >= 8 * j) & (lane < 8 * j + 8)
            rightward = jnp.where(here, pltpu.roll(plane, (8 * j + 8) % 128, 1), rightward)
            leftward = jnp.where(here, pltpu.roll(plane, 8 * j, 1) if j else plane, leftward)
        rp_ref[q] = rightward
        lp_ref[q] = leftward

    def send_halo(q, n):
        p = pl.ds(q * CLASS, n * CLASS)
        c = pl.ds(q, n)
        return [
            send(rp_ref.at[c], hl_ref.at[c, 8:72], (gx, right)),
            send(lp_ref.at[c], hr_ref.at[c, 8:72], (gx, left)),
            send(t_ref.at[p, 64:72], t_ref.at[p, 0:8], (down, gy)),
            send(t_ref.at[p, 8:16], t_ref.at[p, 72:80], (up, gy)),
            send(rp_ref.at[c, 56:64], hl_ref.at[c, 0:8], (down, right)),
            send(rp_ref.at[c, 0:8], hl_ref.at[c, 72:80], (up, right)),
            send(lp_ref.at[c, 56:64], hr_ref.at[c, 0:8], (down, left)),
            send(lp_ref.at[c, 0:8], hr_ref.at[c, 72:80], (up, left)),
        ]

    pack(0)
    pl.semaphore_wait(barrier, len(greeted))
    halo0 = send_halo(0, 1)
    loads[VARS].wait()
    masks_in = [send(mk_ref, nk_ref.at[n], device) for n, device in enumerate(around)]
    for q in (1, 2, 3):
        pack(q)
    halo1 = send_halo(1, 3)

    def expand_masks():
        for copy in masks_in:
            copy.wait_recv()
        below, above, from_right, from_left, below_right, below_left, above_right, above_left = (
            nk_ref.at[n] for n in range(8)
        )
        bands = [(above_left, above, above_right, 1), (from_left, mk_ref, from_right, 0),
                 (from_left, mk_ref, from_right, 1), (below_left, below, below_right, 0)]
        block = lax.broadcasted_iota(jnp.int32, (8, 128), 0)
        place = lax.broadcasted_iota(jnp.int32, (8, 128), 1)
        wide = [[], []]
        for level, spread_out in enumerate(((place + 14) // 16 == block, (place % 64 + 6) // 8 == block)):
            spread_out = jnp.where(spread_out, 1.0, 0.0)
            for n, (a, b, c, i) in enumerate(bands):
                j_ref[level, n] = jnp.zeros((8, 128), F32)
                j_ref[level, n, 0:1, 0:7] = a[level, i, 3:4].astype(F32)
                j_ref[level, n, 1:5, 0:7] = b[level, i].astype(F32)
                j_ref[level, n, 5:6, 0:7] = c[level, i, 0:1].astype(F32)
                wide[level].append(lax.dot_general(
                    j_ref[level, n], spread_out, (((0,), (0,)), ((), ())), preferred_element_type=F32))
        row = lax.broadcasted_iota(jnp.int32, (40, 128), 0)

        def by_rows(values, edges, count):
            out = jnp.broadcast_to(values[0], (count, 128))
            for value, edge in zip(values[1:], edges):
                out = jnp.where(row[:count] >= edge, jnp.broadcast_to(value, (count, 128)), out)
            return out

        for bz in range(2):
            for rd in range(2):
                for ld in range(2):
                    b = 4 * bz + 2 * ld + rd - 1
                    if b >= 0:
                        m1_ref[bz, rd, :, 128 * ld:128 * ld + 128] = by_rows(
                            [v[b:b + 1] for v in wide[0]], (3, 19, 35), 40)
                b = 4 * bz + rd - 1
                values = [jnp.where(lane < 64, v[b:b + 1] if b >= 0 else 1.0, v[b + 2:b + 3]) for v in wide[1]]
                m2_ref[bz, rd] = by_rows(values, (rd, 8 + rd, 16 + rd), 24)

    def sides_and_halves(q):
        for j in range(CLASS):
            sides = jnp.where(
                lane < 8, pltpu.roll(hr_ref[q], (128 - 8 * j) % 128, 1) if j else hr_ref[q],
                pltpu.roll(hl_ref[q], (136 - 8 * j) % 128, 1))
            for col, value in ((0, t_ref[q * CLASS + j]), (128, sides)):
                high, low_part = halves(value)
                lhs_ref[80 * j:80 * j + 80, col:col + 128] = high
                lhs_ref[80 * j:80 * j + 80, 256 + col:384 + col] = low_part

    def lanes1(q, parts=(0, 1)):
        cols = slice(128 * parts[0], 128 * parts[-1] + 128)
        filters = w_ref[0:256, cols]
        both = jnp.concatenate([filters, filters], 0)

        def step(i, _):
            rows = pl.ds(pl.multiple_of(i * 320, 320), 320)
            out = jnp.dot(lhs_ref[rows, :], both, preferred_element_type=F32)
            for n, half in enumerate(parts):
                y_ref[pl.ds(q * CLASS + 4 * i, 4), half, 0:80, :] = out[:, 128 * n:128 * n + 128].reshape(4, 80, 128)
            return _

        lax.fori_loop(0, 3, step, None)

    def smooth_rows1(q):
        def one(p):
            even0, even1, even2 = (y_ref[p, 0, pl.ds(s, 40, stride=2), :] for s in (0, 2, 4))
            odd0, odd1 = (y_ref[p, 0, pl.ds(s, 40, stride=2), :] for s in (1, 3))
            detail = odd1 - 0.5 * (even1 + even2)
            before = odd0 - 0.5 * (even0 + even1)
            s1_ref[p] = even1 + 0.25 * (before + detail)

        def step(i, _):
            for n in range(4):
                one(q * CLASS + 4 * i + n)
            return _

        lax.fori_loop(0, CLASS // 4, step, None)

    def coarse_rows2():
        for p in range(CLASS):
            even0, even1, even2 = (s1l_ref[p, pl.ds(s, 16, stride=2), :] for s in (1, 3, 5))
            odd0, odd1 = (s1l_ref[p, pl.ds(s, 16, stride=2), :] for s in (2, 4))
            detail = odd1 - 0.5 * (even1 + even2)
            before = odd0 - 0.5 * (even0 + even1)
            smooth = even1 + 0.25 * (before + detail)
            local = jnp.where((lane >= 2) & (lane < 34), smooth, 0.0)
            own_ref[p] = pltpu.roll(local, (32 * (gy % 4) + 126) % 128, 1)

    def rows1(q):
        bz = 0 if q < 2 else 1

        def one(p):
            for half in range(2):
                cols = slice(128 * half, 128 * half + 128)
                even0, even1, even2 = (y_ref[p, half, pl.ds(s, 40, stride=2), :] for s in (0, 2, 4))
                odd0, odd1 = (y_ref[p, half, pl.ds(s, 40, stride=2), :] for s in (1, 3))
                detail = odd1 - 0.5 * (even1 + even2)
                before = odd0 - 0.5 * (even0 + even1)
                smooth = even1 + 0.25 * (before + detail)
                c_ref[p, 1, 0:40, cols] = detail * m1_ref[bz, 1, :, cols]
                if q == 1 and half == 0:
                    s1_ref[p] = smooth
                elif q > 1 or half == 1:
                    c_ref[p, 0, 0:40, cols] = smooth * m1_ref[bz, 0, :, cols]

        def step(i, _):
            one(q * CLASS + 2 * i)
            one(q * CLASS + 2 * i + 1)
            return _

        lax.fori_loop(0, CLASS // 2, step, None)

    def lanes2(q):
        x = s1_ref[q * CLASS:(q + 1) * CLASS].reshape(CLASS * 40, 128)
        s1l_ref[q * CLASS:(q + 1) * CLASS, 0:40, :] = split_dot(x, w_ref[256:384, 128:256]).reshape(CLASS, 40, 128)

    def rows2(q):
        for p in range(q * CLASS, (q + 1) * CLASS):
            even0, even1, even2 = (s1l_ref[p, pl.ds(s, 24, stride=2), :] for s in (1, 3, 5))
            odd0, odd1 = (s1l_ref[p, pl.ds(s, 24, stride=2), :] for s in (2, 4))
            before = odd0 - 0.5 * (even0 + even1)
            detail = odd1 - 0.5 * (even1 + even2)
            smooth = even1 + 0.25 * (before + detail)
            c2_ref[p, 0, 0:24] = smooth * m2_ref[q, 0]
            c2_ref[p, 1, 0:24] = before * m2_ref[q, 1]

    def back2(q):
        for p in range(q * CLASS, (q + 1) * CLASS):
            smooth0, smooth1 = (c2_ref[p, 0, s:s + 24, :] for s in (0, 1))
            detail0, detail1, detail2 = (c2_ref[p, 1, s:s + 24, :] for s in (0, 1, 2))
            even = smooth0 - 0.25 * (detail0 + detail1)
            after = smooth1 - 0.25 * (detail1 + detail2)
            u_ref[p, pl.ds(3, 24, stride=2), :] = even
            u_ref[p, pl.ds(4, 24, stride=2), :] = detail1 + 0.5 * (even + after)
        x = u_ref[q * CLASS:(q + 1) * CLASS, 0:40, :].reshape(CLASS * 40, 128)
        c_ref[q * CLASS:(q + 1) * CLASS, 0, 0:40, 0:128] = split_dot(x, w_ref[384:512, 128:256]).reshape(CLASS, 40, 128)

    def back1(q):
        def one(p, j):
            for half in range(2):
                cols = slice(128 * half, 128 * half + 128)
                smooth0, smooth1 = (c_ref[p, 0, s:s + 32, cols] for s in (3, 4))
                detail0, detail1, detail2 = (c_ref[p, 1, s:s + 32, cols] for s in (2, 3, 4))
                even = smooth0 - 0.25 * (detail0 + detail1)
                after = smooth1 - 0.25 * (detail1 + detail2)
                odd = detail1 + 0.5 * (even + after)
                for which, value in ((0, even), (1, odd)):
                    rows = pl.ds(pl.multiple_of(j * 64 + 32 * which, 32), 32)
                    high, low_part = halves(value)
                    lhsi_ref[rows, cols] = high
                    lhsi_ref[rows, slice(256 + 128 * half, 384 + 128 * half)] = low_part

        def step(i, _):
            one(q * CLASS + 2 * i, 2 * i)
            one(q * CLASS + 2 * i + 1, 2 * i + 1)
            return _

        lax.fori_loop(0, CLASS // 2, step, None)
        filters = w_ref[256:512, 0:128]
        both = jnp.concatenate([filters, filters], 0)

        def multiply(i, _):
            rows = pl.ds(pl.multiple_of(i * 256, 256), 256)
            out = jnp.dot(lhsi_ref[rows, :], both, preferred_element_type=F32)
            zr_ref[pl.ds(q * CLASS + 4 * i, 4)] = out.reshape(4, 64, 128)
            return _

        lax.fori_loop(0, 3, multiply, None)

    def finish():
        for var in range(VARS):
            slots = plane_slots(var)
            for odd in range(2):
                for tile in range(4):
                    rows = slice(32 * odd + 8 * tile, 32 * odd + 8 * tile + 8)
                    smooth, middle, fine = ([zr_ref[p, rows, :] for p in part] for part in slots)
                    out = inverse_planes(inverse_planes(smooth, middle), fine)
                    for k in range(NZ):
                        restored_ref[var * NZ + k, pl.ds(16 * tile + odd, 8, stride=2), :] = out[k]

    def lanes_of(block):
        return pl.ds(pl.multiple_of(128 * ((block + 4) % 4), 128), 128)

    base = 6 * core
    p0, p1, p2 = (pl.ds(base + 2 * r, 2) for r in range(3))
    order = (1, 3, 2)

    def strip0(ky, kz, plane=p0):
        return g_ref.at[plane, (yy + ky + 4) % 4, :, :, lanes_of(group + kz)]

    def strip1(kx, ky=0):
        return g_ref.at[p1, (yy + ky + 4) % 4, (xx + kx + 4) % 4]

    def strip2(ky, kx=0):
        return g_ref.at[p2, (yy + ky + 4) % 4, (xx + kx + 4) % 4]

    def spread(view, axis):
        return [send(view, view, axis(k)) for k in order]

    def ship0(ky):
        whole = strip0(ky, 0)
        half = strip0(ky, 0, base + low)
        return send(whole, whole, cross), send(half, half, along_z(3))

    def relay0(ky, came):
        came[0].wait_recv()
        whole = strip0(ky, side)
        first = send(whole, whole, pair)
        came[1].wait_recv()
        half = strip0(ky, 2, base + 1 - low)
        return first, send(half, half, pair)

    def to_sibling(ref):
        return send(ref, ref, sibling)

    def arrived(copies):
        for copy in copies:
            copy.wait_recv()

    arrived(halo0)
    sides_and_halves(0)
    lanes1(0, (0,))
    smooth_rows1(0)
    lanes2(0)
    coarse_rows2()
    other = 1 - core
    pre = [
        send(own_ref.at[pl.ds(6 * other, 6)], parts_ref.at[0], (gx, flip1)),
        send(own_ref.at[pl.ds(6 * core, 6)], parts_ref.at[1], (gx, flip2)),
        send(own_ref.at[pl.ds(6 * other, 6)], parts_ref.at[2], (gx, flip3)),
    ]
    lanes1(0, (1,))
    expand_masks()
    arrived(pre)
    block = own_ref[pl.ds(base, 6)] + parts_ref[0] + parts_ref[1] + parts_ref[2]
    g_ref[pl.ds(base, 6), yy, xx, :, lanes_of(group)] = block

    xs = spread(g_ref.at[p0, yy, xx, :, lanes_of(group)], along_x)
    zs = spread(g_ref.at[pl.ds(base + 2, 4), yy, xx, :, lanes_of(group)], along_z)
    rows1(0)
    arrived(halo1)
    sides_and_halves(1)
    lanes1(1)

    arrived(xs)
    ys0 = spread(strip0(0, 0), along_y)
    s0 = ship0(0)
    rows1(1)
    lanes2(1)

    arrived(zs)
    xs1 = spread(strip1(0), along_x)
    ys2 = spread(strip2(0), along_y)
    ys1 = {0: spread(strip1(0), along_y)}
    xs2 = {0: spread(strip2(0), along_x)}
    rows2(0)
    rows2(1)

    s0 = {0: s0}
    for n, k in enumerate(order):
        ys0[n].wait_recv()
        s0[-k] = ship0(-k)
    back2(0)
    r0 = {0: relay0(0, s0[0])}
    for n, k in enumerate(order):
        xs1[n].wait_recv()
        ys1[-k] = spread(strip1(-k), along_y)
        ys2[n].wait_recv()
        xs2[-k] = spread(strip2(-k), along_x)
    back2(1)
    sides_and_halves(2)
    lanes1(2)
    rows1(2)
    for k in order:
        r0[-k] = relay0(-k, s0[-k])
    sib = []

    def complete(which):
        arrived(ys1[which])
        sib.append(to_sibling(g_ref.at[p1, :, (xx + which + 4) % 4]))
        arrived(xs2[which])
        sib.append(to_sibling(g_ref.at[p2, (yy + which + 4) % 4]))

    def complete0(which):
        arrived(r0[which])
        sib.append(to_sibling(g_ref.at[p0, (yy + which + 4) % 4]))

    complete(0)
    sides_and_halves(3)
    lanes1(3)
    rows1(3)
    complete0(0)
    back1(0)
    back1(1)
    complete(-1)
    back1(2)
    complete0(-1)
    back1(3)
    complete(-3)
    complete0(-3)
    finish()
    complete(-2)
    complete0(-2)
    arrived(sib)
    for copy in sent:
        copy.wait_send()


def store(restored_ref, coarse_ref, restored_out, coarse_out, sem):
    copies = [
        pltpu.make_async_copy(coarse_ref.at[p], coarse_out.at[p], sem.at[p]) for p in range(12)
    ] + [
        pltpu.make_async_copy(restored_ref.at[NZ * v:NZ * v + NZ], restored_out.at[NZ * v:NZ * v + NZ], sem.at[12 + v])
        for v in range(VARS)
    ]
    for copy in copies:
        copy.start()
    for copy in copies:
        copy.wait()


def body(field, masks):
    mk = pltpu.with_memory_space_constraint(masks.transpose(0, 2, 3, 1), pltpu.HBM)
    field = pltpu.with_memory_space_constraint(field.reshape(PLANES, ROWS, COLS), pltpu.HBM)
    anywhere = pl.BlockSpec(memory_space=pl.ANY)
    in_hbm = pl.BlockSpec(memory_space=pltpu.HBM)
    in_vmem = pl.BlockSpec(memory_space=pltpu.VMEM)
    restored, coarse = pl.pallas_call(
        kernel,
        out_shape=(
            jax.ShapeDtypeStruct((PLANES, ROWS, COLS), F32),
            jax.ShapeDtypeStruct((12, 4, 4, 16, 512), F32),
        ),
        in_specs=[in_hbm, in_hbm],
        out_specs=(in_vmem, in_vmem),
        scratch_shapes=[
            pltpu.VMEM((PLANES, ROWS, COLS), F32),
            pltpu.VMEM((2, 2, 4, 7), jnp.int32),
            pltpu.VMEM((512, 256), BF16),
            pltpu.VMEM((PLANES, 80, 128), F32),
            pltpu.VMEM((4, ROWS, 128), F32),
            pltpu.VMEM((4, ROWS, 128), F32),
            pltpu.VMEM((4, 80, 128), F32),
            pltpu.VMEM((4, 80, 128), F32),
            pltpu.VMEM((8, 2, 2, 4, 7), jnp.int32),
            pltpu.VMEM((CLASS * 80, 512), BF16),
            pltpu.VMEM((PLANES, 2, 88, 128), F32),
            pltpu.VMEM((PLANES, 2, 40, 256), F32),
            pltpu.VMEM((2 * CLASS, 40, 128), F32),
            pltpu.VMEM((2 * CLASS, 56, 128), F32),
            pltpu.VMEM((2 * CLASS, 2, 32, 128), F32),
            pltpu.VMEM((2 * CLASS, 56, 128), F32),
            pltpu.VMEM((2, 2, 40, 256), F32),
            pltpu.VMEM((2, 2, 24, 128), F32),
            pltpu.VMEM((CLASS, 16, 128), F32),
            pltpu.VMEM((3, 6, 16, 128), F32),
            pltpu.VMEM((CLASS * 64, 512), BF16),
            pltpu.VMEM((PLANES, 64, 128), F32),
            pltpu.VMEM((2, 4, 8, 128), F32),
            pltpu.SemaphoreType.DMA((VARS + 1,)),
            pltpu.SemaphoreType.DMA((MESSAGES,)),
            pltpu.SemaphoreType.DMA((MESSAGES,)),
        ],
        compiler_params=pltpu.CompilerParams(
            collective_id=0, has_side_effects=True, vmem_limit_bytes=VMEM_LIMIT
        ),
        cost_estimate=pl.CostEstimate(flops=2_000_000_000, bytes_accessed=10_000_000, transcendentals=0),
    )(field, mk)
    restored, coarse = pl.pallas_call(
        store,
        out_shape=(
            jax.ShapeDtypeStruct(restored.shape, F32),
            jax.ShapeDtypeStruct(coarse.shape, F32),
        ),
        in_specs=[anywhere, anywhere],
        out_specs=(in_hbm, in_hbm),
        scratch_shapes=[pltpu.SemaphoreType.DMA((12 + VARS,))],
        compiler_params=pltpu.CompilerParams(vmem_limit_bytes=1024 * 1024),
    )(restored, coarse)
    return restored.reshape(VARS, NZ, ROWS, COLS), coarse.reshape(VARS, 4, 256, 512)


def solution(mesh):
    placed = (P(None, None, "gx", "gy"), P(None, None, "gx", "gy"))
    return jax.shard_map(
        body,
        mesh=mesh,
        in_specs=placed,
        out_specs=(P(None, None, "gx", "gy"), P()),
        check_vma=False,
    )
```

```python
import math

import jax
import jax.numpy as jnp
from jax import lax
from jax.experimental import pallas as pl
from jax.experimental.pallas import tpu as pltpu
from jax.sharding import PartitionSpec as P

MESH = pl.DeviceIdType.MESH
F32 = jnp.float32
BF16 = jnp.bfloat16
VARS, NZ, ROWS, COLS = 3, 16, 64, 128
PLANES = VARS * NZ
CLASS = 12
BATCHES = 32
VMEM_LIMIT = 32 * 1024 * 1024


def by_distance(distance, taps):
    out = jnp.zeros(distance.shape, F32)
    for at, weight in taps.items():
        out = jnp.where(distance == at, weight, out)
    return out


FORWARD_SMOOTH = {0: 0.75, -2: -0.125, 2: -0.125, -1: 0.25, 1: 0.25}
FORWARD_DETAIL = {0: -0.5, 1: 1.0, 2: -0.5}
INVERSE_SMOOTH = {0: 1.0, -1: 0.5, 1: 0.5}
INVERSE_DETAIL = {1: 0.75, 0: -0.25, 2: -0.25, -1: -0.125, 3: -0.125}


def write_filters(w_ref):
    row = lax.broadcasted_iota(jnp.int32, (256, 128), 0)
    col = lax.broadcasted_iota(jnp.int32, (256, 128), 1)
    cell = jnp.where(row < 136, row, jnp.where(row < 144, row - 144, 4096))
    w_ref[0:256, 0:128] = by_distance(cell - 2 * (col - 2), FORWARD_SMOOTH).astype(BF16)
    w_ref[0:256, 128:256] = by_distance(cell - 2 * (col - 2), FORWARD_DETAIL).astype(BF16)
    w_ref[256:384, 0:128] = by_distance(col[:128] - 2 * (row[:128] - 2), INVERSE_SMOOTH).astype(BF16)
    w_ref[384:512, 0:128] = by_distance(col[:128] - 2 * (row[:128] - 2), INVERSE_DETAIL).astype(BF16)
    row, col = row[:128], col[:128]
    ahead = row - 2 - 2 * (jnp.where(col < 64, col, col - 64) - 2)
    w_ref[256:384, 128:256] = jnp.where(
        col < 64, by_distance(ahead, FORWARD_SMOOTH), by_distance(ahead, FORWARD_DETAIL)).astype(BF16)
    ahead = col - 2 - 2 * (jnp.where(row < 64, row, row - 64) - 2)
    w_ref[384:512, 128:256] = jnp.where(
        row < 64, by_distance(ahead, INVERSE_SMOOTH), by_distance(ahead, INVERSE_DETAIL)).astype(BF16)


def halves(x):
    high = x.astype(BF16)
    low = (x - high.astype(F32)).astype(BF16)
    return high, low


def split_dot(x, filters):
    high, low = halves(x)
    return jnp.dot(high, filters, preferred_element_type=F32) + jnp.dot(low, filters, preferred_element_type=F32)


def forward_planes(x):
    count = len(x) // 2
    detail = []
    for k in range(count):
        after = x[2 * k + 2] if k + 1 < count else x[2 * count - 2]
        detail.append(x[2 * k + 1] - 0.5 * (x[2 * k] + after))
    smooth = [x[2 * k] + 0.25 * (detail[max(k - 1, 0)] + detail[k]) for k in range(count)]
    return smooth, detail


def inverse_planes(smooth, detail):
    count = len(smooth)
    even = [smooth[k] - 0.25 * (detail[max(k - 1, 0)] + detail[k]) for k in range(count)]
    out = []
    for k in range(count):
        out += [even[k], detail[k] + 0.5 * (even[k] + even[min(k + 1, count - 1)])]
    return out


def plane_slots(var):
    smooth = [4 * var + k for k in range(4)]
    middle = [12 + 4 * var + k for k in range(4)]
    fine = [24 + 8 * var + k for k in range(8)]
    return smooth, middle, fine


def kernel(
    field_ref, masks_ref, zr_ref, g_ref,
    x_ref, mk_ref, w_ref, t_ref, rp_ref, lp_ref, hl_ref, hr_ref, nk_ref, lhs_ref, y_ref, c_ref, s1_ref, s1l_ref, c2_ref,
    u_ref, m1_ref, m2_ref, own_ref, parts_ref, lhsi_ref, j_ref, load_sem, send_sem, recv_sem,
):
    gx = lax.axis_index("gx")
    gy = lax.axis_index("gy")
    yy, xx = gx // 4, gx % 4
    zz, core = gy // 2, gy % 2
    group, low = gy // 4, zz % 2
    side = 2 * low - 1

    up, down = (gx + 15) % 16, (gx + 1) % 16
    left, right = (gy + 15) % 16, (gy + 1) % 16
    around = [(up, gy), (down, gy), (gx, left), (gx, right), (up, left), (up, right), (down, left), (down, right)]
    flip1 = gy + 1 - 2 * core
    flip2 = gy + 2 - 4 * low
    flip3 = flip2 + 1 - 2 * core
    sibling = (gx, flip1)
    pair = (gx, flip2)
    cross = (gx, (gy + 2 * side + 16) % 16)

    def along_x(k):
        return (yy * 4 + (xx + k) % 4, gy)

    def along_y(k):
        return (((yy + k) % 4) * 4 + xx, gy)

    def in_plane(ky, kx):
        return (((yy + ky) % 4) * 4 + (xx + kx) % 4, gy)

    def along_z(k):
        return (gx, (gy + 2 * side * k + 16) % 16)

    greeted = around + [(gx, flip1), (gx, flip2), (gx, flip3)]
    greeted += [along_x(k) for k in (1, 2, 3)] + [along_y(k) for k in (1, 2, 3)]
    greeted += [along_z(k) for k in (1, 2, -2, 3)]
    greeted += [in_plane(ky, kx) for ky in (1, 2, 3) for kx in (1, 2, 3)]

    loads = [
        pltpu.make_async_copy(field_ref.at[NZ * v:NZ * v + NZ], x_ref.at[NZ * v:NZ * v + NZ], load_sem.at[v])
        for v in range(VARS)
    ]
    loads.append(pltpu.make_async_copy(masks_ref, mk_ref, load_sem.at[VARS]))
    for copy in loads:
        copy.start()
    barrier = pltpu.get_barrier_semaphore()
    for device in greeted:
        pl.semaphore_signal(barrier, inc=1, device_id=device, device_id_type=MESH)

    write_filters(w_ref)
    batches = []

    class Batch:
        def __init__(self, sized=None):
            self.at, self.tiles, self.sized = len(batches), 0, sized
            batches.append(self)

        def send(self, src, dst, device):
            pltpu.make_async_remote_copy(
                src_ref=src, dst_ref=dst, send_sem=send_sem.at[self.at], recv_sem=recv_sem.at[self.at],
                device_id=device, device_id_type=MESH,
            ).start()
            if self.sized is None:
                self.tiles += math.prod(src.shape) // 1024

        def wait(self, sem):
            size = self.sized
            if size is None and self.tiles == 768:
                size = g_ref.at[0:6]
            elif size is None:
                high = max(h for h in range(1, 9) if self.tiles % h == 0)
                size = x_ref.at[0:self.tiles // high, 0:8 * high]
            pltpu.make_async_copy(size, size, sem.at[self.at]).wait()

        def arrived(self):
            self.wait(recv_sem)

    def batch(*copies):
        out = Batch()
        for copy in copies:
            out.send(*copy)
        return out

    lane = lax.broadcasted_iota(jnp.int32, (1, 128), 1)

    for var in range(VARS):
        slots = plane_slots(var)
        loads[var].wait()

        def lift(tile, _, var=var, slots=slots):
            rows = pl.ds(pl.multiple_of(tile * 8, 8), 8)
            x = [x_ref[var * NZ + k, rows, :] for k in range(NZ)]
            smooth, fine = forward_planes(x)
            smooth, middle = forward_planes(smooth)
            ext = pl.ds(pl.multiple_of(tile * 8 + 8, 8), 8)
            for slot, value in zip(slots[0] + slots[1] + slots[2], smooth + middle + fine):
                t_ref[slot, ext, :] = value
            return _

        lax.fori_loop(0, 8, lift, None)

    def pack(q):
        rightward = jnp.zeros((ROWS, 128), F32)
        leftward = jnp.zeros((ROWS, 128), F32)
        for j in range(CLASS):
            plane = t_ref[q * CLASS + j, 8:72, :]
            here = (lane >= 8 * j) & (lane < 8 * j + 8)
            rightward = jnp.where(here, pltpu.roll(plane, (8 * j + 8) % 128, 1), rightward)
            leftward = jnp.where(here, pltpu.roll(plane, 8 * j, 1) if j else plane, leftward)
        rp_ref[q] = rightward
        lp_ref[q] = leftward

    def send_halo(q, n):
        p = pl.ds(q * CLASS, n * CLASS)
        c = pl.ds(q, n)
        return batch(
            (rp_ref.at[c], hl_ref.at[c, 8:72], (gx, right)),
            (lp_ref.at[c], hr_ref.at[c, 8:72], (gx, left)),
            (t_ref.at[p, 64:72], t_ref.at[p, 0:8], (down, gy)),
            (t_ref.at[p, 8:16], t_ref.at[p, 72:80], (up, gy)),
            (rp_ref.at[c, 56:64], hl_ref.at[c, 0:8], (down, right)),
            (rp_ref.at[c, 0:8], hl_ref.at[c, 72:80], (up, right)),
            (lp_ref.at[c, 56:64], hr_ref.at[c, 0:8], (down, left)),
            (lp_ref.at[c, 0:8], hr_ref.at[c, 72:80], (up, left)),
        )

    pack(0)
    pl.semaphore_wait(barrier, len(greeted))
    halo0 = send_halo(0, 1)
    loads[VARS].wait()
    for q in (1, 2, 3):
        pack(q)
    halo1 = send_halo(1, 3)
    masks_in = Batch(nk_ref)
    for n, device in enumerate(around):
        masks_in.send(mk_ref, nk_ref.at[n], device)

    def expand_masks():
        below, above, from_right, from_left, below_right, below_left, above_right, above_left = (
            nk_ref.at[n] for n in range(8)
        )
        bands = [(above_left, above, above_right, 1), (from_left, mk_ref, from_right, 0),
                 (from_left, mk_ref, from_right, 1), (below_left, below, below_right, 0)]
        block = lax.broadcasted_iota(jnp.int32, (8, 128), 0)
        place = lax.broadcasted_iota(jnp.int32, (8, 128), 1)
        wide = [[], []]
        for level, spread_out in enumerate(((place + 14) // 16 == block, (place % 64 + 6) // 8 == block)):
            spread_out = jnp.where(spread_out, 1.0, 0.0)
            for n, (a, b, c, i) in enumerate(bands):
                j_ref[level, n] = jnp.zeros((8, 128), F32)
                j_ref[level, n, 0:1, 0:7] = a[level, i, 3:4].astype(F32)
                j_ref[level, n, 1:5, 0:7] = b[level, i].astype(F32)
                j_ref[level, n, 5:6, 0:7] = c[level, i, 0:1].astype(F32)
                wide[level].append(lax.dot_general(
                    j_ref[level, n], spread_out, (((0,), (0,)), ((), ())), preferred_element_type=F32))
        row = lax.broadcasted_iota(jnp.int32, (40, 128), 0)

        def by_rows(values, edges, count):
            out = jnp.broadcast_to(values[0], (count, 128))
            for value, edge in zip(values[1:], edges):
                out = jnp.where(row[:count] >= edge, jnp.broadcast_to(value, (count, 128)), out)
            return out

        for bz in range(2):
            for rd in range(2):
                for ld in range(2):
                    b = 4 * bz + 2 * ld + rd - 1
                    if b >= 0:
                        m1_ref[bz, rd, :, 128 * ld:128 * ld + 128] = by_rows(
                            [v[b:b + 1] for v in wide[0]], (3, 19, 35), 40)
                b = 4 * bz + rd - 1
                values = [jnp.where(lane < 64, v[b:b + 1] if b >= 0 else 1.0, v[b + 2:b + 3]) for v in wide[1]]
                m2_ref[bz, rd] = by_rows(values, (rd, 8 + rd, 16 + rd), 24)

    def sides_and_halves(q):
        for j in range(CLASS):
            sides = jnp.where(
                lane < 8, pltpu.roll(hr_ref[q], (128 - 8 * j) % 128, 1) if j else hr_ref[q],
                pltpu.roll(hl_ref[q], (136 - 8 * j) % 128, 1))
            for col, value in ((0, t_ref[q * CLASS + j]), (128, sides)):
                high, low_part = halves(value)
                lhs_ref[80 * j:80 * j + 80, col:col + 128] = high
                lhs_ref[80 * j:80 * j + 80, 256 + col:384 + col] = low_part

    def lanes1(q, parts=(0, 1)):
        cols = slice(128 * parts[0], 128 * parts[-1] + 128)
        filters = w_ref[0:256, cols]
        both = jnp.concatenate([filters, filters], 0)

        def step(i, _):
            rows = pl.ds(pl.multiple_of(i * 320, 320), 320)
            out = jnp.dot(lhs_ref[rows, :], both, preferred_element_type=F32)
            for n, half in enumerate(parts):
                y_ref[pl.ds(q * CLASS + 4 * i, 4), half, 0:80, :] = out[:, 128 * n:128 * n + 128].reshape(4, 80, 128)
            return _

        lax.fori_loop(0, 3, step, None)

    def smooth_rows1(q):
        def one(p):
            even0, even1, even2 = (y_ref[p, 0, pl.ds(s, 40, stride=2), :] for s in (0, 2, 4))
            odd0, odd1 = (y_ref[p, 0, pl.ds(s, 40, stride=2), :] for s in (1, 3))
            detail = odd1 - 0.5 * (even1 + even2)
            before = odd0 - 0.5 * (even0 + even1)
            s1_ref[p] = even1 + 0.25 * (before + detail)

        def step(i, _):
            for n in range(4):
                one(q * CLASS + 4 * i + n)
            return _

        lax.fori_loop(0, CLASS // 4, step, None)

    def coarse_rows2():
        for p in range(CLASS):
            even0, even1, even2 = (s1l_ref[p, pl.ds(s, 16, stride=2), :] for s in (1, 3, 5))
            odd0, odd1 = (s1l_ref[p, pl.ds(s, 16, stride=2), :] for s in (2, 4))
            detail = odd1 - 0.5 * (even1 + even2)
            before = odd0 - 0.5 * (even0 + even1)
            smooth = even1 + 0.25 * (before + detail)
            local = jnp.where((lane >= 2) & (lane < 34), smooth, 0.0)
            own_ref[p] = pltpu.roll(local, (32 * (gy % 4) + 126) % 128, 1)

    def rows1(q):
        bz = 0 if q < 2 else 1

        def one(p):
            for half in range(2):
                cols = slice(128 * half, 128 * half + 128)
                even0, even1, even2 = (y_ref[p, half, pl.ds(s, 40, stride=2), :] for s in (0, 2, 4))
                odd0, odd1 = (y_ref[p, half, pl.ds(s, 40, stride=2), :] for s in (1, 3))
                detail = odd1 - 0.5 * (even1 + even2)
                before = odd0 - 0.5 * (even0 + even1)
                smooth = even1 + 0.25 * (before + detail)
                c_ref[p, 1, 0:40, cols] = detail * m1_ref[bz, 1, :, cols]
                if q == 1 and half == 0:
                    s1_ref[p] = smooth
                elif q > 1 or half == 1:
                    c_ref[p, 0, 0:40, cols] = smooth * m1_ref[bz, 0, :, cols]

        def step(i, _):
            one(q * CLASS + 2 * i)
            one(q * CLASS + 2 * i + 1)
            return _

        lax.fori_loop(0, CLASS // 2, step, None)

    def lanes2(q):
        x = s1_ref[q * CLASS:(q + 1) * CLASS].reshape(CLASS * 40, 128)
        s1l_ref[q * CLASS:(q + 1) * CLASS, 0:40, :] = split_dot(x, w_ref[256:384, 128:256]).reshape(CLASS, 40, 128)

    def rows2(q):
        for p in range(q * CLASS, (q + 1) * CLASS):
            even0, even1, even2 = (s1l_ref[p, pl.ds(s, 24, stride=2), :] for s in (1, 3, 5))
            odd0, odd1 = (s1l_ref[p, pl.ds(s, 24, stride=2), :] for s in (2, 4))
            before = odd0 - 0.5 * (even0 + even1)
            detail = odd1 - 0.5 * (even1 + even2)
            smooth = even1 + 0.25 * (before + detail)
            c2_ref[p, 0, 0:24] = smooth * m2_ref[q, 0]
            c2_ref[p, 1, 0:24] = before * m2_ref[q, 1]

    def back2(q):
        for p in range(q * CLASS, (q + 1) * CLASS):
            smooth0, smooth1 = (c2_ref[p, 0, s:s + 24, :] for s in (0, 1))
            detail0, detail1, detail2 = (c2_ref[p, 1, s:s + 24, :] for s in (0, 1, 2))
            even = smooth0 - 0.25 * (detail0 + detail1)
            after = smooth1 - 0.25 * (detail1 + detail2)
            u_ref[p, pl.ds(3, 24, stride=2), :] = even
            u_ref[p, pl.ds(4, 24, stride=2), :] = detail1 + 0.5 * (even + after)
        x = u_ref[q * CLASS:(q + 1) * CLASS, 0:40, :].reshape(CLASS * 40, 128)
        c_ref[q * CLASS:(q + 1) * CLASS, 0, 0:40, 0:128] = split_dot(x, w_ref[384:512, 128:256]).reshape(CLASS, 40, 128)

    def back1(q):
        def one(p, j):
            for half in range(2):
                cols = slice(128 * half, 128 * half + 128)
                smooth0, smooth1 = (c_ref[p, 0, s:s + 32, cols] for s in (3, 4))
                detail0, detail1, detail2 = (c_ref[p, 1, s:s + 32, cols] for s in (2, 3, 4))
                even = smooth0 - 0.25 * (detail0 + detail1)
                after = smooth1 - 0.25 * (detail1 + detail2)
                odd = detail1 + 0.5 * (even + after)
                for which, value in ((0, even), (1, odd)):
                    rows = pl.ds(pl.multiple_of(j * 64 + 32 * which, 32), 32)
                    high, low_part = halves(value)
                    lhsi_ref[rows, cols] = high
                    lhsi_ref[rows, slice(256 + 128 * half, 384 + 128 * half)] = low_part

        def step(i, _):
            one(q * CLASS + 2 * i, 2 * i)
            one(q * CLASS + 2 * i + 1, 2 * i + 1)
            return _

        lax.fori_loop(0, CLASS // 2, step, None)
        filters = w_ref[256:512, 0:128]
        both = jnp.concatenate([filters, filters], 0)

        def multiply(i, _):
            rows = pl.ds(pl.multiple_of(i * 256, 256), 256)
            out = jnp.dot(lhsi_ref[rows, :], both, preferred_element_type=F32)
            zr_ref[pl.ds(q * CLASS + 4 * i, 4)] = out.reshape(4, 64, 128)
            return _

        lax.fori_loop(0, 3, multiply, None)

    def lanes_of(block):
        return pl.ds(pl.multiple_of(128 * ((block + 4) % 4), 128), 128)

    base = 6 * core
    p0, p1, p2 = (pl.ds(base + 2 * r, 2) for r in range(3))
    order = (1, 3, 2)

    def strip0(ky, kz, plane=p0):
        return g_ref.at[plane, (yy + ky + 4) % 4, :, :, lanes_of(group + kz)]

    def strip1(kx, ky=0):
        return g_ref.at[p1, (yy + ky + 4) % 4, (xx + kx + 4) % 4]

    def strip2(ky, kx=0):
        return g_ref.at[p2, (yy + ky + 4) % 4, (xx + kx + 4) % 4]

    def spread(view, axis):
        return batch(*((view, view, axis(k)) for k in order))

    def ship0(ky):
        whole = strip0(ky, 0)
        half = strip0(ky, 0, base + low)
        return batch((whole, whole, cross), (half, half, along_z(3)))

    def relay0(ky, came):
        came.arrived()
        whole = strip0(ky, side)
        half = strip0(ky, 2, base + 1 - low)
        return batch((whole, whole, pair), (half, half, pair))

    def arrived(came):
        came.arrived()

    arrived(halo0)
    sides_and_halves(0)
    lanes1(0, (0,))
    smooth_rows1(0)
    lanes2(0)
    coarse_rows2()
    other = 1 - core
    pre = batch(
        (own_ref.at[pl.ds(6 * other, 6)], parts_ref.at[0], (gx, flip1)),
        (own_ref.at[pl.ds(6 * core, 6)], parts_ref.at[1], (gx, flip2)),
        (own_ref.at[pl.ds(6 * other, 6)], parts_ref.at[2], (gx, flip3)),
    )
    lanes1(0, (1,))
    arrived(pre)
    block = own_ref[pl.ds(base, 6)] + parts_ref[0] + parts_ref[1] + parts_ref[2]
    g_ref[pl.ds(base, 6), yy, xx, :, lanes_of(group)] = block

    zs = spread(g_ref.at[pl.ds(base + 2, 4), yy, xx, :, lanes_of(group)], along_z)
    source0 = g_ref.at[p0, yy, xx, :, lanes_of(group)]
    mine0 = g_ref.at[p0, yy, xx, :, lanes_of(group)]
    flat0 = {}
    for ky in (0, 1, 3, 2):
        flat0[-ky] = batch(*((source0, mine0, in_plane(ky, kx)) for kx in (0, 1, 3, 2) if kx or ky))
    arrived(masks_in)
    expand_masks()
    rows1(0)
    arrived(flat0[0])
    s0 = {0: ship0(0)}
    arrived(zs)
    xs1 = [batch((strip1(0), strip1(0), along_x(k))) for k in order]
    ys2 = [batch((strip2(0), strip2(0), along_y(k))) for k in order]
    ys1 = {0: spread(strip1(0), along_y)}
    xs2 = {0: spread(strip2(0), along_x)}
    for k in order:
        arrived(flat0[-k])
        s0[-k] = ship0(-k)
    arrived(halo1)
    sides_and_halves(1)
    lanes1(1)
    rows1(1)
    for n, k in enumerate(order):
        xs1[n].arrived()
        ys1[-k] = spread(strip1(-k), along_y)
        ys2[n].arrived()
        xs2[-k] = spread(strip2(-k), along_x)
    r0 = {0: relay0(0, s0[0])}
    lanes2(1)
    rows2(0)
    rows2(1)
    back2(0)
    r0[-1] = relay0(-1, s0[-1])
    back2(1)
    sides_and_halves(2)
    lanes1(2)
    r0[-3] = relay0(-3, s0[-3])
    rows1(2)
    r0[-2] = relay0(-2, s0[-2])
    sib = Batch()

    def to_sibling(ref):
        sib.send(ref, ref, sibling)

    def complete(which):
        ys1[which].arrived()
        to_sibling(g_ref.at[p1, :, (xx + which + 4) % 4])
        xs2[which].arrived()
        to_sibling(g_ref.at[p2, (yy + which + 4) % 4])

    def complete0(which):
        r0[which].arrived()
        to_sibling(g_ref.at[p0, (yy + which + 4) % 4])

    complete(0)
    sides_and_halves(3)
    lanes1(3)
    rows1(3)
    complete0(0)
    back1(0)
    back1(1)
    complete(-1)
    back1(2)
    complete0(-1)
    back1(3)
    complete(-3)
    complete0(-3)
    complete(-2)
    complete0(-2)
    arrived(sib)
    for out in batches:
        out.wait(send_sem)


def store(planes_ref, coarse_ref, restored_out, coarse_out, restored_ref, sem):
    copies = [pltpu.make_async_copy(coarse_ref.at[p], coarse_out.at[p], sem.at[p]) for p in range(12)]
    for copy in copies:
        copy.start()
    for var in range(VARS):
        slots = plane_slots(var)

        def lift(i, _, var=var, slots=slots):
            odd, tile = i // 4, i % 4
            rows = pl.ds(pl.multiple_of(8 * i, 8), 8)
            smooth, middle, fine = ([planes_ref[p, rows, :] for p in part] for part in slots)
            out = inverse_planes(inverse_planes(smooth, middle), fine)
            for k in range(NZ):
                restored_ref[var * NZ + k, pl.ds(16 * tile + odd, 8, stride=2), :] = out[k]
            return _

        lax.fori_loop(0, 8, lift, None)
        planes = pl.ds(NZ * var, NZ)
        copy = pltpu.make_async_copy(restored_ref.at[planes], restored_out.at[planes], sem.at[12 + var])
        copy.start()
        copies.append(copy)
    for copy in copies:
        copy.wait()


def body(field, masks):
    mk = pltpu.with_memory_space_constraint(masks.transpose(0, 2, 3, 1), pltpu.HBM)
    field = pltpu.with_memory_space_constraint(field.reshape(PLANES, ROWS, COLS), pltpu.HBM)
    anywhere = pl.BlockSpec(memory_space=pl.ANY)
    in_hbm = pl.BlockSpec(memory_space=pltpu.HBM)
    in_vmem = pl.BlockSpec(memory_space=pltpu.VMEM)
    planes, coarse = pl.pallas_call(
        kernel,
        out_shape=(
            jax.ShapeDtypeStruct((PLANES, ROWS, COLS), F32),
            jax.ShapeDtypeStruct((12, 4, 4, 16, 512), F32),
        ),
        in_specs=[in_hbm, in_hbm],
        out_specs=(in_vmem, in_vmem),
        scratch_shapes=[
            pltpu.VMEM((PLANES, ROWS, COLS), F32),
            pltpu.VMEM((2, 2, 4, 7), jnp.int32),
            pltpu.VMEM((512, 256), BF16),
            pltpu.VMEM((PLANES, 80, 128), F32),
            pltpu.VMEM((4, ROWS, 128), F32),
            pltpu.VMEM((4, ROWS, 128), F32),
            pltpu.VMEM((4, 80, 128), F32),
            pltpu.VMEM((4, 80, 128), F32),
            pltpu.VMEM((8, 2, 2, 4, 7), jnp.int32),
            pltpu.VMEM((CLASS * 80, 512), BF16),
            pltpu.VMEM((PLANES, 2, 88, 128), F32),
            pltpu.VMEM((PLANES, 2, 40, 256), F32),
            pltpu.VMEM((2 * CLASS, 40, 128), F32),
            pltpu.VMEM((2 * CLASS, 56, 128), F32),
            pltpu.VMEM((2 * CLASS, 2, 32, 128), F32),
            pltpu.VMEM((2 * CLASS, 56, 128), F32),
            pltpu.VMEM((2, 2, 40, 256), F32),
            pltpu.VMEM((2, 2, 24, 128), F32),
            pltpu.VMEM((CLASS, 16, 128), F32),
            pltpu.VMEM((3, 6, 16, 128), F32),
            pltpu.VMEM((CLASS * 64, 512), BF16),
            pltpu.VMEM((2, 4, 8, 128), F32),
            pltpu.SemaphoreType.DMA((VARS + 1,)),
            pltpu.SemaphoreType.DMA((BATCHES,)),
            pltpu.SemaphoreType.DMA((BATCHES,)),
        ],
        compiler_params=pltpu.CompilerParams(
            collective_id=0, has_side_effects=True, vmem_limit_bytes=VMEM_LIMIT
        ),
        cost_estimate=pl.CostEstimate(flops=2_000_000_000, bytes_accessed=10_000_000, transcendentals=0),
    )(field, mk)
    restored, coarse = pl.pallas_call(
        store,
        out_shape=(
            jax.ShapeDtypeStruct((PLANES, ROWS, COLS), F32),
            jax.ShapeDtypeStruct(coarse.shape, F32),
        ),
        in_specs=[in_vmem, anywhere],
        out_specs=(in_hbm, in_hbm),
        scratch_shapes=[pltpu.VMEM((PLANES, ROWS, COLS), F32), pltpu.SemaphoreType.DMA((12 + VARS,))],
        compiler_params=pltpu.CompilerParams(vmem_limit_bytes=4 * 1024 * 1024),
    )(planes, coarse)
    return restored.reshape(VARS, NZ, ROWS, COLS), coarse.reshape(VARS, 4, 256, 512)


def solution(mesh):
    placed = (P(None, None, "gx", "gy"), P(None, None, "gx", "gy"))
    return jax.shard_map(
        body,
        mesh=mesh,
        in_specs=placed,
        out_specs=(P(None, None, "gx", "gy"), P()),
        check_vma=False,
    )
```

```python
import math

import jax
import jax.numpy as jnp
from jax import lax
from jax.experimental import pallas as pl
from jax.experimental.pallas import tpu as pltpu
from jax.sharding import PartitionSpec as P

MESH = pl.DeviceIdType.MESH
F32 = jnp.float32
BF16 = jnp.bfloat16
VARS, NZ, ROWS, COLS = 3, 16, 64, 128
PLANES = VARS * NZ
CLASS = 12
BATCHES = 32
VMEM_LIMIT = 32 * 1024 * 1024


def by_distance(distance, taps):
    out = jnp.zeros(distance.shape, F32)
    for at, weight in taps.items():
        out = jnp.where(distance == at, weight, out)
    return out


FORWARD_SMOOTH = {0: 0.75, -2: -0.125, 2: -0.125, -1: 0.25, 1: 0.25}
FORWARD_DETAIL = {0: -0.5, 1: 1.0, 2: -0.5}
INVERSE_SMOOTH = {0: 1.0, -1: 0.5, 1: 0.5}
INVERSE_DETAIL = {1: 0.75, 0: -0.25, 2: -0.25, -1: -0.125, 3: -0.125}


def write_filters(w_ref):
    row = lax.broadcasted_iota(jnp.int32, (256, 128), 0)
    col = lax.broadcasted_iota(jnp.int32, (256, 128), 1)
    cell = jnp.where(row < 136, row, jnp.where(row < 144, row - 144, 4096))
    w_ref[0:256, 0:128] = by_distance(cell - 2 * (col - 2), FORWARD_SMOOTH).astype(BF16)
    w_ref[0:256, 128:256] = by_distance(cell - 2 * (col - 2), FORWARD_DETAIL).astype(BF16)
    w_ref[256:384, 0:128] = by_distance(col[:128] - 2 * (row[:128] - 2), INVERSE_SMOOTH).astype(BF16)
    w_ref[384:512, 0:128] = by_distance(col[:128] - 2 * (row[:128] - 2), INVERSE_DETAIL).astype(BF16)
    row, col = row[:128], col[:128]
    ahead = row - 2 - 2 * (jnp.where(col < 64, col, col - 64) - 2)
    w_ref[256:384, 128:256] = jnp.where(
        col < 64, by_distance(ahead, FORWARD_SMOOTH), by_distance(ahead, FORWARD_DETAIL)).astype(BF16)
    ahead = col - 2 - 2 * (jnp.where(row < 64, row, row - 64) - 2)
    w_ref[384:512, 128:256] = jnp.where(
        row < 64, by_distance(ahead, INVERSE_SMOOTH), by_distance(ahead, INVERSE_DETAIL)).astype(BF16)


def halves(x):
    high = x.astype(BF16)
    low = (x - high.astype(F32)).astype(BF16)
    return high, low


def split_dot(x, filters):
    high, low = halves(x)
    return jnp.dot(high, filters, preferred_element_type=F32) + jnp.dot(low, filters, preferred_element_type=F32)


def forward_planes(x):
    count = len(x) // 2
    detail = []
    for k in range(count):
        after = x[2 * k + 2] if k + 1 < count else x[2 * count - 2]
        detail.append(x[2 * k + 1] - 0.5 * (x[2 * k] + after))
    smooth = [x[2 * k] + 0.25 * (detail[max(k - 1, 0)] + detail[k]) for k in range(count)]
    return smooth, detail


def inverse_planes(smooth, detail):
    count = len(smooth)
    even = [smooth[k] - 0.25 * (detail[max(k - 1, 0)] + detail[k]) for k in range(count)]
    out = []
    for k in range(count):
        out += [even[k], detail[k] + 0.5 * (even[k] + even[min(k + 1, count - 1)])]
    return out


def plane_slots(var):
    smooth = [4 * var + k for k in range(4)]
    middle = [12 + 4 * var + k for k in range(4)]
    fine = [24 + 8 * var + k for k in range(8)]
    return smooth, middle, fine


def kernel(
    field_ref, masks_ref, zr_ref, g_ref,
    x_ref, mk_ref, w_ref, t_ref, rp_ref, lp_ref, hl_ref, hr_ref, nk_ref, lhs_ref, y_ref, c_ref, s1_ref, s1l_ref, c2_ref,
    u_ref, m1_ref, m2_ref, own_ref, parts_ref, lhsi_ref, j_ref, load_sem, send_sem, recv_sem,
):
    gx = lax.axis_index("gx")
    gy = lax.axis_index("gy")
    yy, xx = gx // 4, gx % 4
    zz, core = gy // 2, gy % 2
    group, low = gy // 4, zz % 2
    side = 2 * low - 1

    up, down = (gx + 15) % 16, (gx + 1) % 16
    left, right = (gy + 15) % 16, (gy + 1) % 16
    around = [(up, gy), (down, gy), (gx, left), (gx, right), (up, left), (up, right), (down, left), (down, right)]
    flip1 = gy + 1 - 2 * core
    flip2 = gy + 2 - 4 * low
    flip3 = flip2 + 1 - 2 * core
    sibling = (gx, flip1)
    pair = (gx, flip2)
    cross = (gx, (gy + 2 * side + 16) % 16)

    def along_x(k):
        return (yy * 4 + (xx + k) % 4, gy)

    def along_y(k):
        return (((yy + k) % 4) * 4 + xx, gy)

    def in_plane(ky, kx):
        return (((yy + ky) % 4) * 4 + (xx + kx) % 4, gy)

    def along_z(k):
        return (gx, (gy + 2 * side * k + 16) % 16)

    greeted = around + [(gx, flip1), (gx, flip2), (gx, flip3)]
    greeted += [along_x(k) for k in (1, 2, 3)] + [along_y(k) for k in (1, 2, 3)]
    greeted += [along_z(k) for k in (1, 2, -2, 3)]
    greeted += [in_plane(ky, kx) for ky in (1, 2, 3) for kx in (1, 2, 3)]

    loads = [
        pltpu.make_async_copy(field_ref.at[NZ * v:NZ * v + NZ], x_ref.at[NZ * v:NZ * v + NZ], load_sem.at[v])
        for v in range(VARS)
    ]
    loads.append(pltpu.make_async_copy(masks_ref, mk_ref, load_sem.at[VARS]))
    for copy in loads:
        copy.start()
    barrier = pltpu.get_barrier_semaphore()
    for device in greeted:
        pl.semaphore_signal(barrier, inc=1, device_id=device, device_id_type=MESH)

    write_filters(w_ref)
    batches = []

    class Batch:
        def __init__(self, sized=None):
            self.at, self.tiles, self.sized = len(batches), 0, sized
            batches.append(self)

        def send(self, src, dst, device):
            pltpu.make_async_remote_copy(
                src_ref=src, dst_ref=dst, send_sem=send_sem.at[self.at], recv_sem=recv_sem.at[self.at],
                device_id=device, device_id_type=MESH,
            ).start()
            if self.sized is None:
                self.tiles += math.prod(src.shape) // 1024

        def wait(self, sem):
            size = self.sized
            if size is None and self.tiles == 768:
                size = g_ref.at[0:6]
            elif size is None:
                high = max(h for h in range(1, 9) if self.tiles % h == 0)
                size = x_ref.at[0:self.tiles // high, 0:8 * high]
            pltpu.make_async_copy(size, size, sem.at[self.at]).wait()

        def arrived(self):
            self.wait(recv_sem)

    def batch(*copies):
        out = Batch()
        for copy in copies:
            out.send(*copy)
        return out

    lane = lax.broadcasted_iota(jnp.int32, (1, 128), 1)

    for var in range(VARS):
        slots = plane_slots(var)
        loads[var].wait()

        def lift(tile, _, var=var, slots=slots):
            rows = pl.ds(pl.multiple_of(tile * 8, 8), 8)
            x = [x_ref[var * NZ + k, rows, :] for k in range(NZ)]
            smooth, fine = forward_planes(x)
            smooth, middle = forward_planes(smooth)
            ext = pl.ds(pl.multiple_of(tile * 8 + 8, 8), 8)
            for slot, value in zip(slots[0] + slots[1] + slots[2], smooth + middle + fine):
                t_ref[slot, ext, :] = value
            return _

        lax.fori_loop(0, 8, lift, None)

    def pack(q):
        rightward = jnp.zeros((ROWS, 128), F32)
        leftward = jnp.zeros((ROWS, 128), F32)
        for j in range(CLASS):
            plane = t_ref[q * CLASS + j, 8:72, :]
            here = (lane >= 8 * j) & (lane < 8 * j + 8)
            rightward = jnp.where(here, pltpu.roll(plane, (8 * j + 8) % 128, 1), rightward)
            leftward = jnp.where(here, pltpu.roll(plane, 8 * j, 1) if j else plane, leftward)
        rp_ref[q] = rightward
        lp_ref[q] = leftward

    def send_halo(q, n):
        p = pl.ds(q * CLASS, n * CLASS)
        c = pl.ds(q, n)
        return batch(
            (rp_ref.at[c], hl_ref.at[c, 8:72], (gx, right)),
            (lp_ref.at[c], hr_ref.at[c, 8:72], (gx, left)),
            (t_ref.at[p, 64:72], t_ref.at[p, 0:8], (down, gy)),
            (t_ref.at[p, 8:16], t_ref.at[p, 72:80], (up, gy)),
            (rp_ref.at[c, 56:64], hl_ref.at[c, 0:8], (down, right)),
            (rp_ref.at[c, 0:8], hl_ref.at[c, 72:80], (up, right)),
            (lp_ref.at[c, 56:64], hr_ref.at[c, 0:8], (down, left)),
            (lp_ref.at[c, 0:8], hr_ref.at[c, 72:80], (up, left)),
        )

    pack(0)
    pl.semaphore_wait(barrier, len(greeted))
    halo0 = send_halo(0, 1)
    loads[VARS].wait()
    for q in (1, 2, 3):
        pack(q)
    halo1 = send_halo(1, 3)
    masks_in = Batch(nk_ref)
    for n, device in enumerate(around):
        masks_in.send(mk_ref, nk_ref.at[n], device)

    def expand_masks():
        below, above, from_right, from_left, below_right, below_left, above_right, above_left = (
            nk_ref.at[n] for n in range(8)
        )
        bands = [(above_left, above, above_right, 1), (from_left, mk_ref, from_right, 0),
                 (from_left, mk_ref, from_right, 1), (below_left, below, below_right, 0)]
        block = lax.broadcasted_iota(jnp.int32, (8, 128), 0)
        place = lax.broadcasted_iota(jnp.int32, (8, 128), 1)
        wide = [[], []]
        for level, spread_out in enumerate(((place + 14) // 16 == block, (place % 64 + 6) // 8 == block)):
            spread_out = jnp.where(spread_out, 1.0, 0.0)
            for n, (a, b, c, i) in enumerate(bands):
                j_ref[level, n] = jnp.zeros((8, 128), F32)
                j_ref[level, n, 0:1, 0:7] = a[level, i, 3:4].astype(F32)
                j_ref[level, n, 1:5, 0:7] = b[level, i].astype(F32)
                j_ref[level, n, 5:6, 0:7] = c[level, i, 0:1].astype(F32)
                wide[level].append(lax.dot_general(
                    j_ref[level, n], spread_out, (((0,), (0,)), ((), ())), preferred_element_type=F32))
        row = lax.broadcasted_iota(jnp.int32, (40, 128), 0)

        def by_rows(values, edges, count):
            out = jnp.broadcast_to(values[0], (count, 128))
            for value, edge in zip(values[1:], edges):
                out = jnp.where(row[:count] >= edge, jnp.broadcast_to(value, (count, 128)), out)
            return out

        for bz in range(2):
            for rd in range(2):
                for ld in range(2):
                    b = 4 * bz + 2 * ld + rd - 1
                    if b >= 0:
                        m1_ref[bz, rd, :, 128 * ld:128 * ld + 128] = by_rows(
                            [v[b:b + 1] for v in wide[0]], (3, 19, 35), 40)
                b = 4 * bz + rd - 1
                values = [jnp.where(lane < 64, v[b:b + 1] if b >= 0 else 1.0, v[b + 2:b + 3]) for v in wide[1]]
                m2_ref[bz, rd] = by_rows(values, (rd, 8 + rd, 16 + rd), 24)

    def sides_and_halves(q):
        for j in range(CLASS):
            sides = jnp.where(
                lane < 8, pltpu.roll(hr_ref[q], (128 - 8 * j) % 128, 1) if j else hr_ref[q],
                pltpu.roll(hl_ref[q], (136 - 8 * j) % 128, 1))
            for col, value in ((0, t_ref[q * CLASS + j]), (128, sides)):
                high, low_part = halves(value)
                lhs_ref[80 * j:80 * j + 80, col:col + 128] = high
                lhs_ref[80 * j:80 * j + 80, 256 + col:384 + col] = low_part

    def lanes1(q, parts=(0, 1)):
        cols = slice(128 * parts[0], 128 * parts[-1] + 128)
        filters = w_ref[0:256, cols]
        both = jnp.concatenate([filters, filters], 0)

        def step(i, _):
            rows = pl.ds(pl.multiple_of(i * 320, 320), 320)
            out = jnp.dot(lhs_ref[rows, :], both, preferred_element_type=F32)
            for n, half in enumerate(parts):
                y_ref[pl.ds(q * CLASS + 4 * i, 4), half, 0:80, :] = out[:, 128 * n:128 * n + 128].reshape(4, 80, 128)
            return _

        lax.fori_loop(0, 3, step, None)

    def smooth_rows1(q):
        def one(p):
            even0, even1, even2 = (y_ref[p, 0, pl.ds(s, 40, stride=2), :] for s in (0, 2, 4))
            odd0, odd1 = (y_ref[p, 0, pl.ds(s, 40, stride=2), :] for s in (1, 3))
            detail = odd1 - 0.5 * (even1 + even2)
            before = odd0 - 0.5 * (even0 + even1)
            s1_ref[p] = even1 + 0.25 * (before + detail)

        def step(i, _):
            for n in range(4):
                one(q * CLASS + 4 * i + n)
            return _

        lax.fori_loop(0, CLASS // 4, step, None)

    def coarse_rows2():
        for p in range(CLASS):
            even0, even1, even2 = (s1l_ref[p, pl.ds(s, 16, stride=2), :] for s in (1, 3, 5))
            odd0, odd1 = (s1l_ref[p, pl.ds(s, 16, stride=2), :] for s in (2, 4))
            detail = odd1 - 0.5 * (even1 + even2)
            before = odd0 - 0.5 * (even0 + even1)
            smooth = even1 + 0.25 * (before + detail)
            local = jnp.where((lane >= 2) & (lane < 34), smooth, 0.0)
            own_ref[p] = pltpu.roll(local, (32 * (gy % 4) + 126) % 128, 1)

    def rows1(q):
        bz = 0 if q < 2 else 1

        def one(p):
            for half in range(2):
                cols = slice(128 * half, 128 * half + 128)
                even0, even1, even2 = (y_ref[p, half, pl.ds(s, 40, stride=2), :] for s in (0, 2, 4))
                odd0, odd1 = (y_ref[p, half, pl.ds(s, 40, stride=2), :] for s in (1, 3))
                detail = odd1 - 0.5 * (even1 + even2)
                before = odd0 - 0.5 * (even0 + even1)
                smooth = even1 + 0.25 * (before + detail)
                c_ref[p, 1, 0:40, cols] = detail * m1_ref[bz, 1, :, cols]
                if q == 1 and half == 0:
                    s1_ref[p] = smooth
                elif q > 1 or half == 1:
                    c_ref[p, 0, 0:40, cols] = smooth * m1_ref[bz, 0, :, cols]

        def step(i, _):
            one(q * CLASS + 2 * i)
            one(q * CLASS + 2 * i + 1)
            return _

        lax.fori_loop(0, CLASS // 2, step, None)

    def lanes2(q):
        x = s1_ref[q * CLASS:(q + 1) * CLASS].reshape(CLASS * 40, 128)
        s1l_ref[q * CLASS:(q + 1) * CLASS, 0:40, :] = split_dot(x, w_ref[256:384, 128:256]).reshape(CLASS, 40, 128)

    def rows2(q):
        for p in range(q * CLASS, (q + 1) * CLASS):
            even0, even1, even2 = (s1l_ref[p, pl.ds(s, 24, stride=2), :] for s in (1, 3, 5))
            odd0, odd1 = (s1l_ref[p, pl.ds(s, 24, stride=2), :] for s in (2, 4))
            before = odd0 - 0.5 * (even0 + even1)
            detail = odd1 - 0.5 * (even1 + even2)
            smooth = even1 + 0.25 * (before + detail)
            c2_ref[p, 0, 0:24] = smooth * m2_ref[q, 0]
            c2_ref[p, 1, 0:24] = before * m2_ref[q, 1]

    def back2(q):
        for p in range(q * CLASS, (q + 1) * CLASS):
            smooth0, smooth1 = (c2_ref[p, 0, s:s + 24, :] for s in (0, 1))
            detail0, detail1, detail2 = (c2_ref[p, 1, s:s + 24, :] for s in (0, 1, 2))
            even = smooth0 - 0.25 * (detail0 + detail1)
            after = smooth1 - 0.25 * (detail1 + detail2)
            u_ref[p, pl.ds(3, 24, stride=2), :] = even
            u_ref[p, pl.ds(4, 24, stride=2), :] = detail1 + 0.5 * (even + after)
        x = u_ref[q * CLASS:(q + 1) * CLASS, 0:40, :].reshape(CLASS * 40, 128)
        c_ref[q * CLASS:(q + 1) * CLASS, 0, 0:40, 0:128] = split_dot(x, w_ref[384:512, 128:256]).reshape(CLASS, 40, 128)

    def back1(q):
        def one(p, j):
            for half in range(2):
                cols = slice(128 * half, 128 * half + 128)
                smooth0, smooth1 = (c_ref[p, 0, s:s + 32, cols] for s in (3, 4))
                detail0, detail1, detail2 = (c_ref[p, 1, s:s + 32, cols] for s in (2, 3, 4))
                even = smooth0 - 0.25 * (detail0 + detail1)
                after = smooth1 - 0.25 * (detail1 + detail2)
                odd = detail1 + 0.5 * (even + after)
                for which, value in ((0, even), (1, odd)):
                    rows = pl.ds(pl.multiple_of(j * 64 + 32 * which, 32), 32)
                    high, low_part = halves(value)
                    lhsi_ref[rows, cols] = high
                    lhsi_ref[rows, slice(256 + 128 * half, 384 + 128 * half)] = low_part

        def step(i, _):
            one(q * CLASS + 2 * i, 2 * i)
            one(q * CLASS + 2 * i + 1, 2 * i + 1)
            return _

        lax.fori_loop(0, CLASS // 2, step, None)
        filters = w_ref[256:512, 0:128]
        both = jnp.concatenate([filters, filters], 0)

        def multiply(i, _):
            rows = pl.ds(pl.multiple_of(i * 256, 256), 256)
            out = jnp.dot(lhsi_ref[rows, :], both, preferred_element_type=F32)
            zr_ref[pl.ds(q * CLASS + 4 * i, 4)] = out.reshape(4, 64, 128)
            return _

        lax.fori_loop(0, 3, multiply, None)

    def lanes_of(block):
        return pl.ds(pl.multiple_of(128 * ((block + 4) % 4), 128), 128)

    base = 6 * core
    p0, p1, p2 = (pl.ds(base + 2 * r, 2) for r in range(3))
    order = (1, 3, 2)

    def strip0(ky, kz, plane=p0):
        return g_ref.at[plane, (yy + ky + 4) % 4, :, :, lanes_of(group + kz)]

    def strip1(kx, ky=0):
        return g_ref.at[p1, (yy + ky + 4) % 4, (xx + kx + 4) % 4]

    def strip2(ky, kx=0):
        return g_ref.at[p2, (yy + ky + 4) % 4, (xx + kx + 4) % 4]

    def spread(view, axis):
        return batch(*((view, view, axis(k)) for k in order))

    def ship0(ky):
        whole = strip0(ky, 0)
        half = strip0(ky, 0, base + low)
        return batch((whole, whole, cross), (half, half, along_z(3)))

    def relay0(ky, came):
        came.arrived()
        whole = strip0(ky, side)
        half = strip0(ky, 2, base + 1 - low)
        return batch((whole, whole, pair), (half, half, pair))

    def arrived(came):
        came.arrived()

    arrived(halo0)
    sides_and_halves(0)
    lanes1(0, (0,))
    smooth_rows1(0)
    lanes2(0)
    coarse_rows2()
    other = 1 - core
    pre = batch(
        (own_ref.at[pl.ds(6 * other, 6)], parts_ref.at[0], (gx, flip1)),
        (own_ref.at[pl.ds(6 * core, 6)], parts_ref.at[1], (gx, flip2)),
        (own_ref.at[pl.ds(6 * other, 6)], parts_ref.at[2], (gx, flip3)),
    )
    lanes1(0, (1,))
    arrived(pre)
    block = own_ref[pl.ds(base, 6)] + parts_ref[0] + parts_ref[1] + parts_ref[2]
    g_ref[pl.ds(base, 6), yy, xx, :, lanes_of(group)] = block

    zs = spread(g_ref.at[pl.ds(base + 2, 4), yy, xx, :, lanes_of(group)], along_z)
    source0 = g_ref.at[p0, yy, xx, :, lanes_of(group)]
    mine0 = g_ref.at[p0, yy, xx, :, lanes_of(group)]
    flat0 = {}
    for ky in (0, 1, 3, 2):
        flat0[-ky] = batch(*((source0, mine0, in_plane(ky, kx)) for kx in (0, 1, 3, 2) if kx or ky))
    arrived(masks_in)
    expand_masks()
    rows1(0)
    rows2(0)
    back2(0)
    arrived(flat0[0])
    s0 = {0: ship0(0)}
    arrived(zs)
    xs1 = [batch((strip1(0), strip1(0), along_x(k))) for k in order]
    ys2 = [batch((strip2(0), strip2(0), along_y(k))) for k in order]
    ys1 = {0: spread(strip1(0), along_y)}
    xs2 = {0: spread(strip2(0), along_x)}
    for k in order:
        arrived(flat0[-k])
        s0[-k] = ship0(-k)
    arrived(halo1)
    sides_and_halves(1)
    lanes1(1)
    rows1(1)
    for n, k in enumerate(order):
        xs1[n].arrived()
        ys1[-k] = spread(strip1(-k), along_y)
        ys2[n].arrived()
        xs2[-k] = spread(strip2(-k), along_x)
    r0 = {}
    sib = Batch()

    def to_sibling(ref):
        sib.send(ref, ref, sibling)

    def complete(which):
        ys1[which].arrived()
        to_sibling(g_ref.at[p1, :, (xx + which + 4) % 4])
        xs2[which].arrived()
        to_sibling(g_ref.at[p2, (yy + which + 4) % 4])

    def complete0(which):
        r0[which].arrived()
        to_sibling(g_ref.at[p0, (yy + which + 4) % 4])

    back1(0)
    r0[0] = relay0(0, s0[0])
    lanes2(1)
    rows2(1)
    back2(1)
    back1(1)
    r0[-1] = relay0(-1, s0[-1])
    sides_and_halves(2)
    lanes1(2)
    rows1(2)
    r0[-3] = relay0(-3, s0[-3])
    complete(0)
    back1(2)
    sides_and_halves(3)
    lanes1(3)
    complete0(0)
    complete(-1)
    r0[-2] = relay0(-2, s0[-2])
    rows1(3)
    complete0(-1)
    complete(-3)
    back1(3)
    complete0(-3)
    complete(-2)
    complete0(-2)
    arrived(sib)
    for out in batches:
        out.wait(send_sem)


def store(planes_ref, coarse_ref, restored_out, coarse_out, restored_ref, sem):
    copies = [pltpu.make_async_copy(coarse_ref.at[p], coarse_out.at[p], sem.at[p]) for p in range(12)]
    for copy in copies:
        copy.start()
    for var in range(VARS):
        slots = plane_slots(var)

        def lift(i, _, var=var, slots=slots):
            odd, tile = i // 4, i % 4
            rows = pl.ds(pl.multiple_of(8 * i, 8), 8)
            smooth, middle, fine = ([planes_ref[p, rows, :] for p in part] for part in slots)
            out = inverse_planes(inverse_planes(smooth, middle), fine)
            for k in range(NZ):
                restored_ref[var * NZ + k, pl.ds(16 * tile + odd, 8, stride=2), :] = out[k]
            return _

        lax.fori_loop(0, 8, lift, None)
        planes = pl.ds(NZ * var, NZ)
        copy = pltpu.make_async_copy(restored_ref.at[planes], restored_out.at[planes], sem.at[12 + var])
        copy.start()
        copies.append(copy)
    for copy in copies:
        copy.wait()


def body(field, masks):
    mk = pltpu.with_memory_space_constraint(masks.transpose(0, 2, 3, 1), pltpu.HBM)
    field = pltpu.with_memory_space_constraint(field.reshape(PLANES, ROWS, COLS), pltpu.HBM)
    anywhere = pl.BlockSpec(memory_space=pl.ANY)
    in_hbm = pl.BlockSpec(memory_space=pltpu.HBM)
    in_vmem = pl.BlockSpec(memory_space=pltpu.VMEM)
    planes, coarse = pl.pallas_call(
        kernel,
        out_shape=(
            jax.ShapeDtypeStruct((PLANES, ROWS, COLS), F32),
            jax.ShapeDtypeStruct((12, 4, 4, 16, 512), F32),
        ),
        in_specs=[in_hbm, in_hbm],
        out_specs=(in_vmem, in_vmem),
        scratch_shapes=[
            pltpu.VMEM((PLANES, ROWS, COLS), F32),
            pltpu.VMEM((2, 2, 4, 7), jnp.int32),
            pltpu.VMEM((512, 256), BF16),
            pltpu.VMEM((PLANES, 80, 128), F32),
            pltpu.VMEM((4, ROWS, 128), F32),
            pltpu.VMEM((4, ROWS, 128), F32),
            pltpu.VMEM((4, 80, 128), F32),
            pltpu.VMEM((4, 80, 128), F32),
            pltpu.VMEM((8, 2, 2, 4, 7), jnp.int32),
            pltpu.VMEM((CLASS * 80, 512), BF16),
            pltpu.VMEM((PLANES, 2, 88, 128), F32),
            pltpu.VMEM((PLANES, 2, 40, 256), F32),
            pltpu.VMEM((2 * CLASS, 40, 128), F32),
            pltpu.VMEM((2 * CLASS, 56, 128), F32),
            pltpu.VMEM((2 * CLASS, 2, 32, 128), F32),
            pltpu.VMEM((2 * CLASS, 56, 128), F32),
            pltpu.VMEM((2, 2, 40, 256), F32),
            pltpu.VMEM((2, 2, 24, 128), F32),
            pltpu.VMEM((CLASS, 16, 128), F32),
            pltpu.VMEM((3, 6, 16, 128), F32),
            pltpu.VMEM((CLASS * 64, 512), BF16),
            pltpu.VMEM((2, 4, 8, 128), F32),
            pltpu.SemaphoreType.DMA((VARS + 1,)),
            pltpu.SemaphoreType.DMA((BATCHES,)),
            pltpu.SemaphoreType.DMA((BATCHES,)),
        ],
        compiler_params=pltpu.CompilerParams(
            collective_id=0, has_side_effects=True, vmem_limit_bytes=VMEM_LIMIT
        ),
        cost_estimate=pl.CostEstimate(flops=2_000_000_000, bytes_accessed=10_000_000, transcendentals=0),
    )(field, mk)
    restored, coarse = pl.pallas_call(
        store,
        out_shape=(
            jax.ShapeDtypeStruct((PLANES, ROWS, COLS), F32),
            jax.ShapeDtypeStruct(coarse.shape, F32),
        ),
        in_specs=[in_vmem, anywhere],
        out_specs=(in_hbm, in_hbm),
        scratch_shapes=[pltpu.VMEM((PLANES, ROWS, COLS), F32), pltpu.SemaphoreType.DMA((12 + VARS,))],
        compiler_params=pltpu.CompilerParams(vmem_limit_bytes=4 * 1024 * 1024),
    )(planes, coarse)
    return restored.reshape(VARS, NZ, ROWS, COLS), coarse.reshape(VARS, 4, 256, 512)


def solution(mesh):
    placed = (P(None, None, "gx", "gy"), P(None, None, "gx", "gy"))
    return jax.shard_map(
        body,
        mesh=mesh,
        in_specs=placed,
        out_specs=(P(None, None, "gx", "gy"), P()),
        check_vma=False,
    )
```

```python
import math

import jax
import jax.numpy as jnp
from jax import lax
from jax.experimental import pallas as pl
from jax.experimental.pallas import tpu as pltpu
from jax.sharding import PartitionSpec as P

MESH = pl.DeviceIdType.MESH
F32 = jnp.float32
BF16 = jnp.bfloat16
VARS, NZ, ROWS, COLS = 3, 16, 64, 128
PLANES = VARS * NZ
CLASS = 12
BATCHES = 32
VMEM_LIMIT = 32 * 1024 * 1024


def by_distance(distance, taps):
    out = jnp.zeros(distance.shape, F32)
    for at, weight in taps.items():
        out = jnp.where(distance == at, weight, out)
    return out


FORWARD_SMOOTH = {0: 0.75, -2: -0.125, 2: -0.125, -1: 0.25, 1: 0.25}
BOTH_SMOOTH = {}
for _a, _v in FORWARD_SMOOTH.items():
    for _b, _w in FORWARD_SMOOTH.items():
        BOTH_SMOOTH[_a + 2 * _b] = BOTH_SMOOTH.get(_a + 2 * _b, 0.0) + _v * _w
FORWARD_DETAIL = {0: -0.5, 1: 1.0, 2: -0.5}
INVERSE_SMOOTH = {0: 1.0, -1: 0.5, 1: 0.5}
INVERSE_DETAIL = {1: 0.75, 0: -0.25, 2: -0.25, -1: -0.125, 3: -0.125}


def write_filters(w_ref, wc_ref):
    row = lax.broadcasted_iota(jnp.int32, (256, 128), 0)
    col = lax.broadcasted_iota(jnp.int32, (256, 128), 1)
    cell = jnp.where(row < 136, row, jnp.where(row < 144, row - 144, 4096))
    w_ref[0:256, 0:128] = by_distance(cell - 2 * (col - 2), FORWARD_SMOOTH).astype(BF16)
    w_ref[0:256, 128:256] = by_distance(cell - 2 * (col - 2), FORWARD_DETAIL).astype(BF16)
    w_ref[256:384, 0:128] = by_distance(col[:128] - 2 * (row[:128] - 2), INVERSE_SMOOTH).astype(BF16)
    w_ref[384:512, 0:128] = by_distance(col[:128] - 2 * (row[:128] - 2), INVERSE_DETAIL).astype(BF16)
    away = jnp.where(col < 32, jnp.abs(cell - 4 * col), 4096)
    wc_ref[...] = by_distance(away, {t: w for t, w in BOTH_SMOOTH.items() if t >= 0}).astype(BF16)
    row, col = row[:128], col[:128]
    ahead = row - 2 - 2 * (jnp.where(col < 64, col, col - 64) - 2)
    w_ref[256:384, 128:256] = jnp.where(
        col < 64, by_distance(ahead, FORWARD_SMOOTH), by_distance(ahead, FORWARD_DETAIL)).astype(BF16)
    ahead = col - 2 - 2 * (jnp.where(row < 64, row, row - 64) - 2)
    w_ref[384:512, 128:256] = jnp.where(
        row < 64, by_distance(ahead, INVERSE_SMOOTH), by_distance(ahead, INVERSE_DETAIL)).astype(BF16)


def halves(x):
    high = x.astype(BF16)
    low = (x - high.astype(F32)).astype(BF16)
    return high, low


def split_dot(x, filters):
    high, low = halves(x)
    return jnp.dot(high, filters, preferred_element_type=F32) + jnp.dot(low, filters, preferred_element_type=F32)


def forward_planes(x):
    count = len(x) // 2
    detail = []
    for k in range(count):
        after = x[2 * k + 2] if k + 1 < count else x[2 * count - 2]
        detail.append(x[2 * k + 1] - 0.5 * (x[2 * k] + after))
    smooth = [x[2 * k] + 0.25 * (detail[max(k - 1, 0)] + detail[k]) for k in range(count)]
    return smooth, detail


def inverse_planes(smooth, detail):
    count = len(smooth)
    even = [smooth[k] - 0.25 * (detail[max(k - 1, 0)] + detail[k]) for k in range(count)]
    out = []
    for k in range(count):
        out += [even[k], detail[k] + 0.5 * (even[k] + even[min(k + 1, count - 1)])]
    return out


def plane_slots(var):
    smooth = [4 * var + k for k in range(4)]
    middle = [12 + 4 * var + k for k in range(4)]
    fine = [24 + 8 * var + k for k in range(8)]
    return smooth, middle, fine


def kernel(
    field_ref, masks_ref, zr_ref, g_ref,
    x_ref, mk_ref, w_ref, wc_ref, yc_ref, t_ref, rp_ref, lp_ref, hl_ref, hr_ref, nk_ref, lhs_ref, y_ref, c_ref, s1_ref, s1l_ref, c2_ref,
    u_ref, m1_ref, m2_ref, own_ref, parts_ref, pack_ref, lhsi_ref, j_ref, load_sem, send_sem, recv_sem,
):
    gx = lax.axis_index("gx")
    gy = lax.axis_index("gy")
    yy, xx = gx // 4, gx % 4
    zz, core = gy // 2, gy % 2
    group, low = gy // 4, zz % 2
    side = 2 * low - 1

    up, down = (gx + 15) % 16, (gx + 1) % 16
    left, right = (gy + 15) % 16, (gy + 1) % 16
    around = [(up, gy), (down, gy), (gx, left), (gx, right), (up, left), (up, right), (down, left), (down, right)]
    flip1 = gy + 1 - 2 * core
    flip2 = gy + 2 - 4 * low
    flip3 = flip2 + 1 - 2 * core
    sibling = (gx, flip1)
    pair = (gx, flip2)
    cross = (gx, (gy + 2 * side + 16) % 16)

    def along_x(k):
        return (yy * 4 + (xx + k) % 4, gy)

    def along_y(k):
        return (((yy + k) % 4) * 4 + xx, gy)

    def in_plane(ky, kx):
        return (((yy + ky) % 4) * 4 + (xx + kx) % 4, gy)

    def along_z(k):
        return (gx, (gy + 2 * side * k + 16) % 16)

    greeted = around + [(gx, flip1), (gx, flip2), (gx, flip3)]
    greeted += [along_x(k) for k in (1, 2, 3)] + [along_y(k) for k in (1, 2, 3)]
    greeted += [along_z(k) for k in (1, 2, -2, 3)]
    greeted += [in_plane(ky, kx) for ky in (1, 2, 3) for kx in (1, 2, 3)]

    loads = [
        pltpu.make_async_copy(field_ref.at[NZ * v:NZ * v + NZ], x_ref.at[NZ * v:NZ * v + NZ], load_sem.at[v])
        for v in range(VARS)
    ]
    loads.append(pltpu.make_async_copy(masks_ref, mk_ref, load_sem.at[VARS]))
    for copy in loads:
        copy.start()
    barrier = pltpu.get_barrier_semaphore()
    for device in greeted:
        pl.semaphore_signal(barrier, inc=1, device_id=device, device_id_type=MESH)

    write_filters(w_ref, wc_ref)
    batches = []

    class Batch:
        def __init__(self, sized=None):
            self.at, self.tiles, self.sized = len(batches), 0, sized
            batches.append(self)

        def send(self, src, dst, device):
            pltpu.make_async_remote_copy(
                src_ref=src, dst_ref=dst, send_sem=send_sem.at[self.at], recv_sem=recv_sem.at[self.at],
                device_id=device, device_id_type=MESH,
            ).start()
            if self.sized is None:
                self.tiles += math.prod(src.shape) // 1024

        def wait(self, sem):
            size = self.sized
            if size is None and self.tiles == 768:
                size = g_ref.at[0:6]
            elif size is None:
                high = max(h for h in range(1, 9) if self.tiles % h == 0)
                size = x_ref.at[0:self.tiles // high, 0:8 * high]
            pltpu.make_async_copy(size, size, sem.at[self.at]).wait()

        def arrived(self):
            self.wait(recv_sem)

    def batch(*copies):
        out = Batch()
        for copy in copies:
            out.send(*copy)
        return out

    lane = lax.broadcasted_iota(jnp.int32, (1, 128), 1)

    for var in range(VARS):
        slots = plane_slots(var)
        loads[var].wait()

        def lift(tile, _, var=var, slots=slots):
            rows = pl.ds(pl.multiple_of(tile * 8, 8), 8)
            x = [x_ref[var * NZ + k, rows, :] for k in range(NZ)]
            smooth, fine = forward_planes(x)
            smooth, middle = forward_planes(smooth)
            ext = pl.ds(pl.multiple_of(tile * 8 + 8, 8), 8)
            for slot, value in zip(slots[0] + slots[1] + slots[2], smooth + middle + fine):
                t_ref[slot, ext, :] = value
            return _

        lax.fori_loop(0, 8, lift, None)

    def pack(q):
        rightward = jnp.zeros((ROWS, 128), F32)
        leftward = jnp.zeros((ROWS, 128), F32)
        for j in range(CLASS):
            plane = t_ref[q * CLASS + j, 8:72, :]
            here = (lane >= 8 * j) & (lane < 8 * j + 8)
            rightward = jnp.where(here, pltpu.roll(plane, (8 * j + 8) % 128, 1), rightward)
            leftward = jnp.where(here, pltpu.roll(plane, 8 * j, 1) if j else plane, leftward)
        rp_ref[q] = rightward
        lp_ref[q] = leftward

    def send_halo(q, n):
        c = pl.ds(q, n)
        full = pl.ds(q * CLASS, CLASS)
        fine = pl.ds((q + 1) * CLASS, (n - 1) * CLASS)
        rows = [
            (t_ref.at[full, 64:72], t_ref.at[full, 0:8], (down, gy)),
            (t_ref.at[full, 8:16], t_ref.at[full, 72:80], (up, gy)),
        ]
        if n > 1:
            rows += [
                (t_ref.at[fine, 68:72], t_ref.at[fine, 4:8], (down, gy)),
                (t_ref.at[fine, 8:12], t_ref.at[fine, 72:76], (up, gy)),
            ]
        return batch(
            *rows,
            (rp_ref.at[c], hl_ref.at[c, 8:72], (gx, right)),
            (lp_ref.at[c], hr_ref.at[c, 8:72], (gx, left)),
            (rp_ref.at[c, 56:64], hl_ref.at[c, 0:8], (down, right)),
            (rp_ref.at[c, 0:8], hl_ref.at[c, 72:80], (up, right)),
            (lp_ref.at[c, 56:64], hr_ref.at[c, 0:8], (down, left)),
            (lp_ref.at[c, 0:8], hr_ref.at[c, 72:80], (up, left)),
        )

    pack(0)
    pl.semaphore_wait(barrier, len(greeted))
    halo0 = send_halo(0, 1)
    loads[VARS].wait()
    for q in (1, 2, 3):
        pack(q)
    halo1 = send_halo(1, 3)
    masks_in = Batch(nk_ref)
    for n, device in enumerate(around):
        masks_in.send(mk_ref, nk_ref.at[n], device)

    def expand_masks():
        below, above, from_right, from_left, below_right, below_left, above_right, above_left = (
            nk_ref.at[n] for n in range(8)
        )
        bands = [(above_left, above, above_right, 1), (from_left, mk_ref, from_right, 0),
                 (from_left, mk_ref, from_right, 1), (below_left, below, below_right, 0)]
        block = lax.broadcasted_iota(jnp.int32, (8, 128), 0)
        place = lax.broadcasted_iota(jnp.int32, (8, 128), 1)
        wide = [[], []]
        for level, spread_out in enumerate(((place + 14) // 16 == block, (place % 64 + 6) // 8 == block)):
            spread_out = jnp.where(spread_out, 1.0, 0.0)
            for n, (a, b, c, i) in enumerate(bands):
                j_ref[level, n] = jnp.zeros((8, 128), F32)
                j_ref[level, n, 0:1, 0:7] = a[level, i, 3:4].astype(F32)
                j_ref[level, n, 1:5, 0:7] = b[level, i].astype(F32)
                j_ref[level, n, 5:6, 0:7] = c[level, i, 0:1].astype(F32)
                wide[level].append(lax.dot_general(
                    j_ref[level, n], spread_out, (((0,), (0,)), ((), ())), preferred_element_type=F32))
        row = lax.broadcasted_iota(jnp.int32, (40, 128), 0)

        def by_rows(values, edges, count):
            out = jnp.broadcast_to(values[0], (count, 128))
            for value, edge in zip(values[1:], edges):
                out = jnp.where(row[:count] >= edge, jnp.broadcast_to(value, (count, 128)), out)
            return out

        for bz in range(2):
            for rd in range(2):
                for ld in range(2):
                    b = 4 * bz + 2 * ld + rd - 1
                    if b >= 0:
                        m1_ref[bz, rd, :, 128 * ld:128 * ld + 128] = by_rows(
                            [v[b:b + 1] for v in wide[0]], (3, 19, 35), 40)
                b = 4 * bz + rd - 1
                values = [jnp.where(lane < 64, v[b:b + 1] if b >= 0 else 1.0, v[b + 2:b + 3]) for v in wide[1]]
                m2_ref[bz, rd] = by_rows(values, (rd, 8 + rd, 16 + rd), 24)

    def sides_and_halves(q):
        for j in range(CLASS):
            sides = jnp.where(
                lane < 8, pltpu.roll(hr_ref[q], (128 - 8 * j) % 128, 1) if j else hr_ref[q],
                pltpu.roll(hl_ref[q], (136 - 8 * j) % 128, 1))
            for col, value in ((0, t_ref[q * CLASS + j]), (128, sides)):
                high, low_part = halves(value)
                lhs_ref[80 * j:80 * j + 80, col:col + 128] = high
                lhs_ref[80 * j:80 * j + 80, 256 + col:384 + col] = low_part

    def lanes1(q, parts=(0, 1)):
        cols = slice(128 * parts[0], 128 * parts[-1] + 128)
        filters = w_ref[0:256, cols]
        both = jnp.concatenate([filters, filters], 0)

        def step(i, _):
            rows = pl.ds(pl.multiple_of(i * 320, 320), 320)
            out = jnp.dot(lhs_ref[rows, :], both, preferred_element_type=F32)
            for n, half in enumerate(parts):
                y_ref[pl.ds(q * CLASS + 4 * i, 4), half, 0:80, :] = out[:, 128 * n:128 * n + 128].reshape(4, 80, 128)
            return _

        lax.fori_loop(0, 3, step, None)

    def coarse_part():
        both = jnp.concatenate([wc_ref[...], wc_ref[...]], 0)

        def step(i, _):
            rows = pl.ds(pl.multiple_of(i * 320, 320), 320)
            yc_ref[pl.ds(4 * i, 4)] = jnp.dot(lhs_ref[rows, :], both, preferred_element_type=F32).reshape(4, 80, 128)
            return _

        lax.fori_loop(0, 3, step, None)

        def lines(i, _):
            for n in range(4):
                p = 4 * i + n
                total = BOTH_SMOOTH[0] * yc_ref[p, pl.ds(8, 16, stride=4), :]
                for t in range(1, 7):
                    total += BOTH_SMOOTH[t] * (yc_ref[p, pl.ds(8 - t, 16, stride=4), :] + yc_ref[p, pl.ds(8 + t, 16, stride=4), :])
                own_ref[p] = total
            return _

        lax.fori_loop(0, 3, lines, None)

    def rows1(q):
        bz = 0 if q < 2 else 1

        def one(p):
            for half in range(2):
                cols = slice(128 * half, 128 * half + 128)
                even0, even1, even2 = (y_ref[p, half, pl.ds(s, 40, stride=2), :] for s in (0, 2, 4))
                odd0, odd1 = (y_ref[p, half, pl.ds(s, 40, stride=2), :] for s in (1, 3))
                detail = odd1 - 0.5 * (even1 + even2)
                before = odd0 - 0.5 * (even0 + even1)
                smooth = even1 + 0.25 * (before + detail)
                c_ref[p, 1, 0:40, cols] = detail * m1_ref[bz, 1, :, cols]
                if q < 2 and half == 0:
                    s1_ref[p] = smooth
                else:
                    c_ref[p, 0, 0:40, cols] = smooth * m1_ref[bz, 0, :, cols]

        def step(i, _):
            one(q * CLASS + 2 * i)
            one(q * CLASS + 2 * i + 1)
            return _

        lax.fori_loop(0, CLASS // 2, step, None)

    def lanes2(q):
        x = s1_ref[q * CLASS:(q + 1) * CLASS].reshape(CLASS * 40, 128)
        s1l_ref[q * CLASS:(q + 1) * CLASS, 0:40, :] = split_dot(x, w_ref[256:384, 128:256]).reshape(CLASS, 40, 128)

    def rows2(q):
        for p in range(q * CLASS, (q + 1) * CLASS):
            even0, even1, even2 = (s1l_ref[p, pl.ds(s, 24, stride=2), :] for s in (1, 3, 5))
            odd0, odd1 = (s1l_ref[p, pl.ds(s, 24, stride=2), :] for s in (2, 4))
            before = odd0 - 0.5 * (even0 + even1)
            detail = odd1 - 0.5 * (even1 + even2)
            smooth = even1 + 0.25 * (before + detail)
            c2_ref[p, 0, 0:24] = smooth * m2_ref[q, 0]
            c2_ref[p, 1, 0:24] = before * m2_ref[q, 1]

    def back2(q):
        for p in range(q * CLASS, (q + 1) * CLASS):
            smooth0, smooth1 = (c2_ref[p, 0, s:s + 24, :] for s in (0, 1))
            detail0, detail1, detail2 = (c2_ref[p, 1, s:s + 24, :] for s in (0, 1, 2))
            even = smooth0 - 0.25 * (detail0 + detail1)
            after = smooth1 - 0.25 * (detail1 + detail2)
            u_ref[p, pl.ds(3, 24, stride=2), :] = even
            u_ref[p, pl.ds(4, 24, stride=2), :] = detail1 + 0.5 * (even + after)
        x = u_ref[q * CLASS:(q + 1) * CLASS, 0:40, :].reshape(CLASS * 40, 128)
        c_ref[q * CLASS:(q + 1) * CLASS, 0, 0:40, 0:128] = split_dot(x, w_ref[384:512, 128:256]).reshape(CLASS, 40, 128)

    def back1(q):
        def one(p, j):
            for half in range(2):
                cols = slice(128 * half, 128 * half + 128)
                smooth0, smooth1 = (c_ref[p, 0, s:s + 32, cols] for s in (3, 4))
                detail0, detail1, detail2 = (c_ref[p, 1, s:s + 32, cols] for s in (2, 3, 4))
                even = smooth0 - 0.25 * (detail0 + detail1)
                after = smooth1 - 0.25 * (detail1 + detail2)
                odd = detail1 + 0.5 * (even + after)
                for which, value in ((0, even), (1, odd)):
                    rows = pl.ds(pl.multiple_of(j * 64 + 32 * which, 32), 32)
                    high, low_part = halves(value)
                    lhsi_ref[rows, cols] = high
                    lhsi_ref[rows, slice(256 + 128 * half, 384 + 128 * half)] = low_part

        def step(i, _):
            one(q * CLASS + 2 * i, 2 * i)
            one(q * CLASS + 2 * i + 1, 2 * i + 1)
            return _

        lax.fori_loop(0, CLASS // 2, step, None)
        filters = w_ref[256:512, 0:128]
        both = jnp.concatenate([filters, filters], 0)

        def multiply(i, _):
            rows = pl.ds(pl.multiple_of(i * 256, 256), 256)
            out = jnp.dot(lhsi_ref[rows, :], both, preferred_element_type=F32)
            zr_ref[pl.ds(q * CLASS + 4 * i, 4)] = out.reshape(4, 64, 128)
            return _

        lax.fori_loop(0, 3, multiply, None)

    def lanes_of(block):
        return pl.ds(pl.multiple_of(128 * ((block + 4) % 4), 128), 128)

    base = 6 * core
    p0, p1, p2 = (pl.ds(base + 2 * r, 2) for r in range(3))
    order = (1, 3, 2)

    def strip0(ky, kz, plane=p0):
        return g_ref.at[plane, (yy + ky + 4) % 4, :, :, lanes_of(group + kz)]

    def strip1(kx, ky=0):
        return g_ref.at[p1, (yy + ky + 4) % 4, (xx + kx + 4) % 4]

    def strip2(ky, kx=0):
        return g_ref.at[p2, (yy + ky + 4) % 4, (xx + kx + 4) % 4]

    def spread(view, axis):
        return batch(*((view, view, axis(k)) for k in order))

    def ship0(ky):
        whole = strip0(ky, 0)
        half = strip0(ky, 0, base + low)
        return batch((whole, whole, cross), (half, half, along_z(3)))

    def relay0(ky, came):
        came.arrived()
        whole = strip0(ky, side)
        half = strip0(ky, 2, base + 1 - low)
        return batch((whole, whole, pair), (half, half, pair))

    def arrived(came):
        came.arrived()

    arrived(halo0)
    sides_and_halves(0)
    coarse_part()
    for tile in range(3):
        packed = own_ref[4 * tile]
        for j in range(1, 4):
            packed += pltpu.roll(own_ref[4 * tile + j], 32 * j, 1)
        pack_ref[tile] = packed
    other = 1 - core
    pre = batch(
        (pack_ref.at[pl.ds(other, 2)], parts_ref.at[0], (gx, flip1)),
        (pack_ref.at[pl.ds(core, 2)], parts_ref.at[1], (gx, flip2)),
        (pack_ref.at[pl.ds(other, 2)], parts_ref.at[2], (gx, flip3)),
    )
    lanes1(0)
    arrived(pre)
    for i in range(6):
        plane = base + i
        block = pltpu.roll(own_ref[plane], 32 * (gy % 4), 1)
        for n, partner in enumerate((flip1, flip2, flip3)):
            place = partner % 4
            came = pltpu.roll(parts_ref[n, plane // 4 - core], (32 * place - 32 * (plane % 4) + 128) % 128, 1)
            block = jnp.where(lane // 32 == place, came, block)
        g_ref[plane, yy, xx, :, lanes_of(group)] = block
    zs = spread(g_ref.at[pl.ds(base + 2, 4), yy, xx, :, lanes_of(group)], along_z)
    source0 = g_ref.at[p0, yy, xx, :, lanes_of(group)]
    mine0 = g_ref.at[p0, yy, xx, :, lanes_of(group)]
    flat0 = {}
    for ky in (0, 1, 3, 2):
        flat0[-ky] = batch(*((source0, mine0, in_plane(ky, kx)) for kx in (0, 1, 3, 2) if kx or ky))
    arrived(masks_in)
    expand_masks()
    rows1(0)
    lanes2(0)
    rows2(0)
    back2(0)
    arrived(flat0[0])
    s0 = {0: ship0(0)}
    arrived(zs)
    xs1 = [batch((strip1(0), strip1(0), along_x(k))) for k in order]
    ys2 = [batch((strip2(0), strip2(0), along_y(k))) for k in order]
    ys1 = {0: spread(strip1(0), along_y)}
    xs2 = {0: spread(strip2(0), along_x)}
    arrived(flat0[-1])
    s0[-1] = ship0(-1)
    arrived(halo1)
    sides_and_halves(1)
    lanes1(1)
    rows1(1)
    arrived(flat0[-3])
    s0[-3] = ship0(-3)
    for n, k in enumerate(order):
        xs1[n].arrived()
        ys1[-k] = spread(strip1(-k), along_y)
        ys2[n].arrived()
        xs2[-k] = spread(strip2(-k), along_x)
    r0 = {}
    sib = Batch()

    def to_sibling(ref):
        sib.send(ref, ref, sibling)

    def complete(which):
        ys1[which].arrived()
        to_sibling(g_ref.at[p1, :, (xx + which + 4) % 4])
        xs2[which].arrived()
        to_sibling(g_ref.at[p2, (yy + which + 4) % 4])

    def complete0(which):
        r0[which].arrived()
        to_sibling(g_ref.at[p0, (yy + which + 4) % 4])

    arrived(flat0[-2])
    s0[-2] = ship0(-2)
    back1(0)
    r0[0] = relay0(0, s0[0])
    lanes2(1)
    rows2(1)
    back2(1)
    back1(1)
    r0[-1] = relay0(-1, s0[-1])
    sides_and_halves(2)
    lanes1(2)
    rows1(2)
    r0[-3] = relay0(-3, s0[-3])
    complete(0)
    back1(2)
    sides_and_halves(3)
    lanes1(3)
    complete0(0)
    complete(-1)
    r0[-2] = relay0(-2, s0[-2])
    rows1(3)
    complete0(-1)
    complete(-3)
    back1(3)
    complete0(-3)
    complete(-2)
    complete0(-2)
    arrived(sib)
    for out in batches:
        out.wait(send_sem)


def store(planes_ref, coarse_ref, restored_out, coarse_out, restored_ref, sem):
    copies = [pltpu.make_async_copy(coarse_ref.at[p], coarse_out.at[p], sem.at[p]) for p in range(12)]
    for copy in copies:
        copy.start()
    for var in range(VARS):
        slots = plane_slots(var)

        def lift(i, _, var=var, slots=slots):
            odd, tile = i // 4, i % 4
            rows = pl.ds(pl.multiple_of(8 * i, 8), 8)
            smooth, middle, fine = ([planes_ref[p, rows, :] for p in part] for part in slots)
            out = inverse_planes(inverse_planes(smooth, middle), fine)
            for k in range(NZ):
                restored_ref[var * NZ + k, pl.ds(16 * tile + odd, 8, stride=2), :] = out[k]
            return _

        lax.fori_loop(0, 8, lift, None)
        planes = pl.ds(NZ * var, NZ)
        copy = pltpu.make_async_copy(restored_ref.at[planes], restored_out.at[planes], sem.at[12 + var])
        copy.start()
        copies.append(copy)
    for copy in copies:
        copy.wait()


def body(field, masks):
    mk = pltpu.with_memory_space_constraint(masks.transpose(0, 2, 3, 1), pltpu.HBM)
    field = pltpu.with_memory_space_constraint(field.reshape(PLANES, ROWS, COLS), pltpu.HBM)
    anywhere = pl.BlockSpec(memory_space=pl.ANY)
    in_hbm = pl.BlockSpec(memory_space=pltpu.HBM)
    in_vmem = pl.BlockSpec(memory_space=pltpu.VMEM)
    planes, coarse = pl.pallas_call(
        kernel,
        out_shape=(
            jax.ShapeDtypeStruct((PLANES, ROWS, COLS), F32),
            jax.ShapeDtypeStruct((12, 4, 4, 16, 512), F32),
        ),
        in_specs=[in_hbm, in_hbm],
        out_specs=(in_vmem, in_vmem),
        scratch_shapes=[
            pltpu.VMEM((PLANES, ROWS, COLS), F32),
            pltpu.VMEM((2, 2, 4, 7), jnp.int32),
            pltpu.VMEM((512, 256), BF16),
            pltpu.VMEM((256, 128), BF16),
            pltpu.VMEM((CLASS, 80, 128), F32),
            pltpu.VMEM((PLANES, 80, 128), F32),
            pltpu.VMEM((4, ROWS, 128), F32),
            pltpu.VMEM((4, ROWS, 128), F32),
            pltpu.VMEM((4, 80, 128), F32),
            pltpu.VMEM((4, 80, 128), F32),
            pltpu.VMEM((8, 2, 2, 4, 7), jnp.int32),
            pltpu.VMEM((CLASS * 80, 512), BF16),
            pltpu.VMEM((PLANES, 2, 88, 128), F32),
            pltpu.VMEM((PLANES, 2, 40, 256), F32),
            pltpu.VMEM((2 * CLASS, 40, 128), F32),
            pltpu.VMEM((2 * CLASS, 56, 128), F32),
            pltpu.VMEM((2 * CLASS, 2, 32, 128), F32),
            pltpu.VMEM((2 * CLASS, 56, 128), F32),
            pltpu.VMEM((2, 2, 40, 256), F32),
            pltpu.VMEM((2, 2, 24, 128), F32),
            pltpu.VMEM((CLASS, 16, 128), F32),
            pltpu.VMEM((3, 2, 16, 128), F32),
            pltpu.VMEM((3, 16, 128), F32),
            pltpu.VMEM((CLASS * 64, 512), BF16),
            pltpu.VMEM((2, 4, 8, 128), F32),
            pltpu.SemaphoreType.DMA((VARS + 1,)),
            pltpu.SemaphoreType.DMA((BATCHES,)),
            pltpu.SemaphoreType.DMA((BATCHES,)),
        ],
        compiler_params=pltpu.CompilerParams(
            collective_id=0, has_side_effects=True, vmem_limit_bytes=VMEM_LIMIT
        ),
        cost_estimate=pl.CostEstimate(flops=2_000_000_000, bytes_accessed=10_000_000, transcendentals=0),
    )(field, mk)
    restored, coarse = pl.pallas_call(
        store,
        out_shape=(
            jax.ShapeDtypeStruct((PLANES, ROWS, COLS), F32),
            jax.ShapeDtypeStruct(coarse.shape, F32),
        ),
        in_specs=[in_vmem, anywhere],
        out_specs=(in_hbm, in_hbm),
        scratch_shapes=[pltpu.VMEM((PLANES, ROWS, COLS), F32), pltpu.SemaphoreType.DMA((12 + VARS,))],
        compiler_params=pltpu.CompilerParams(vmem_limit_bytes=4 * 1024 * 1024),
    )(planes, coarse)
    return restored.reshape(VARS, NZ, ROWS, COLS), coarse.reshape(VARS, 4, 256, 512)


def solution(mesh):
    placed = (P(None, None, "gx", "gy"), P(None, None, "gx", "gy"))
    return jax.shard_map(
        body,
        mesh=mesh,
        in_specs=placed,
        out_specs=(P(None, None, "gx", "gy"), P()),
        check_vma=False,
    )
```

```python
import math

import jax
import jax.numpy as jnp
from jax import lax
from jax.experimental import pallas as pl
from jax.experimental.pallas import tpu as pltpu
from jax.sharding import PartitionSpec as P

MESH = pl.DeviceIdType.MESH
F32 = jnp.float32
BF16 = jnp.bfloat16
VARS, NZ, ROWS, COLS = 3, 16, 64, 128
PLANES = VARS * NZ
CLASS = 12
BATCHES = 32
FAMILIES = 9
VMEM_LIMIT = 32 * 1024 * 1024


def by_distance(distance, taps):
    out = jnp.zeros(distance.shape, F32)
    for at, weight in taps.items():
        out = jnp.where(distance == at, weight, out)
    return out


FORWARD_SMOOTH = {0: 0.75, -2: -0.125, 2: -0.125, -1: 0.25, 1: 0.25}
BOTH_SMOOTH = {}
for _a, _v in FORWARD_SMOOTH.items():
    for _b, _w in FORWARD_SMOOTH.items():
        BOTH_SMOOTH[_a + 2 * _b] = BOTH_SMOOTH.get(_a + 2 * _b, 0.0) + _v * _w
FORWARD_DETAIL = {0: -0.5, 1: 1.0, 2: -0.5}
INVERSE_SMOOTH = {0: 1.0, -1: 0.5, 1: 0.5}
INVERSE_DETAIL = {1: 0.75, 0: -0.25, 2: -0.25, -1: -0.125, 3: -0.125}


def write_filters(w_ref, wc_ref):
    row = lax.broadcasted_iota(jnp.int32, (256, 128), 0)
    col = lax.broadcasted_iota(jnp.int32, (256, 128), 1)
    cell = jnp.where(row < 136, row, jnp.where(row < 144, row - 144, 4096))
    w_ref[0:256, 0:128] = by_distance(cell - 2 * (col - 2), FORWARD_SMOOTH).astype(BF16)
    w_ref[0:256, 128:256] = by_distance(cell - 2 * (col - 2), FORWARD_DETAIL).astype(BF16)
    w_ref[256:384, 0:128] = by_distance(col[:128] - 2 * (row[:128] - 2), INVERSE_SMOOTH).astype(BF16)
    w_ref[384:512, 0:128] = by_distance(col[:128] - 2 * (row[:128] - 2), INVERSE_DETAIL).astype(BF16)
    away = jnp.where(col < 32, jnp.abs(cell - 4 * col), 4096)
    wc_ref[...] = by_distance(away, {t: w for t, w in BOTH_SMOOTH.items() if t >= 0}).astype(BF16)
    row, col = row[:128], col[:128]
    ahead = row - 2 - 2 * (jnp.where(col < 64, col, col - 64) - 2)
    w_ref[256:384, 128:256] = jnp.where(
        col < 64, by_distance(ahead, FORWARD_SMOOTH), by_distance(ahead, FORWARD_DETAIL)).astype(BF16)
    ahead = col - 2 - 2 * (jnp.where(row < 64, row, row - 64) - 2)
    w_ref[384:512, 128:256] = jnp.where(
        row < 64, by_distance(ahead, INVERSE_SMOOTH), by_distance(ahead, INVERSE_DETAIL)).astype(BF16)


def halves(x):
    high = x.astype(BF16)
    low = (x - high.astype(F32)).astype(BF16)
    return high, low


def split_dot(x, filters):
    high, low = halves(x)
    return jnp.dot(high, filters, preferred_element_type=F32) + jnp.dot(low, filters, preferred_element_type=F32)


def forward_planes(x):
    count = len(x) // 2
    detail = []
    for k in range(count):
        after = x[2 * k + 2] if k + 1 < count else x[2 * count - 2]
        detail.append(x[2 * k + 1] - 0.5 * (x[2 * k] + after))
    smooth = [x[2 * k] + 0.25 * (detail[max(k - 1, 0)] + detail[k]) for k in range(count)]
    return smooth, detail


def inverse_planes(smooth, detail):
    count = len(smooth)
    even = [smooth[k] - 0.25 * (detail[max(k - 1, 0)] + detail[k]) for k in range(count)]
    out = []
    for k in range(count):
        out += [even[k], detail[k] + 0.5 * (even[k] + even[min(k + 1, count - 1)])]
    return out


def plane_slots(var):
    smooth = [4 * var + k for k in range(4)]
    middle = [12 + 4 * var + k for k in range(4)]
    fine = [24 + 8 * var + k for k in range(8)]
    return smooth, middle, fine


def kernel(
    field_ref, masks_ref, zr_ref, g_ref,
    x_ref, mk_ref, w_ref, wc_ref, yc_ref, t_ref, rp_ref, lp_ref, hl_ref, hr_ref, nk_ref, lhs_ref, y_ref, c_ref, s1_ref, s1l_ref, c2_ref,
    u_ref, m1_ref, m2_ref, own_ref, parts_ref, pack_ref, lhsi_ref, j_ref, load_sem, send_sem, recv_sem,
):
    gx = lax.axis_index("gx")
    gy = lax.axis_index("gy")
    yy, xx = gx // 4, gx % 4
    zz, core = gy // 2, gy % 2
    group, low = gy // 4, zz % 2
    side = 2 * low - 1

    up, down = (gx + 15) % 16, (gx + 1) % 16
    left, right = (gy + 15) % 16, (gy + 1) % 16
    around = [(up, gy), (down, gy), (gx, left), (gx, right), (up, left), (up, right), (down, left), (down, right)]
    flip1 = gy + 1 - 2 * core
    flip2 = gy + 2 - 4 * low
    flip3 = flip2 + 1 - 2 * core
    sibling = (gx, flip1)
    pair = (gx, flip2)
    cross = (gx, (gy + 2 * side + 16) % 16)

    def along_x(k):
        return (yy * 4 + (xx + k) % 4, gy)

    def along_y(k):
        return (((yy + k) % 4) * 4 + xx, gy)

    def in_plane(ky, kx):
        return (((yy + ky) % 4) * 4 + (xx + kx) % 4, gy)

    def along_z(k):
        return (gx, (gy + 2 * side * k + 16) % 16)

    greeted = around + [(gx, flip1), (gx, flip2), (gx, flip3)]
    greeted += [along_x(k) for k in (1, 2, 3)] + [along_y(k) for k in (1, 2, 3)]
    greeted += [along_z(k) for k in (1, 2, -2, 3)]
    greeted += [in_plane(ky, kx) for ky in (1, 2, 3) for kx in (1, 2, 3)]

    loads = [
        pltpu.make_async_copy(field_ref.at[NZ * v:NZ * v + NZ], x_ref.at[NZ * v:NZ * v + NZ], load_sem.at[v])
        for v in range(VARS)
    ]
    loads.append(pltpu.make_async_copy(masks_ref, mk_ref, load_sem.at[VARS]))
    for copy in loads:
        copy.start()
    barrier = pltpu.get_barrier_semaphore()
    for device in greeted:
        pl.semaphore_signal(barrier, inc=1, device_id=device, device_id_type=MESH)

    write_filters(w_ref, wc_ref)
    batches = []
    families = {}

    def await_tiles(sem, tiles, size=None):
        if size is None and tiles == 768:
            size = g_ref.at[0:6]
        elif size is None and tiles == 576:
            size = g_ref.at[0:9, 0:2]
        elif size is None:
            high = max(h for h in range(1, 9) if tiles % h == 0)
            size = x_ref.at[0:tiles // high, 0:8 * high]
        pltpu.make_async_copy(size, size, sem).wait()

    class Batch:
        def __init__(self, sized=None, family=None):
            self.at, self.tiles, self.sized = len(batches), 0, sized
            batches.append(self)
            self.out = families.setdefault(family or self.at, [len(families), 0, sized])

        def send(self, src, dst, device):
            pltpu.make_async_remote_copy(
                src_ref=src, dst_ref=dst, send_sem=send_sem.at[self.out[0]], recv_sem=recv_sem.at[self.at],
                device_id=device, device_id_type=MESH,
            ).start()
            if self.sized is None:
                self.tiles += math.prod(src.shape) // 1024
                self.out[1] += math.prod(src.shape) // 1024

        def arrived(self):
            await_tiles(recv_sem.at[self.at], self.tiles, self.sized)

    def batch(*copies, family=None):
        out = Batch(family=family)
        for copy in copies:
            out.send(*copy)
        return out

    lane = lax.broadcasted_iota(jnp.int32, (1, 128), 1)

    for var in range(VARS):
        slots = plane_slots(var)
        loads[var].wait()

        def lift(tile, _, var=var, slots=slots):
            rows = pl.ds(pl.multiple_of(tile * 8, 8), 8)
            x = [x_ref[var * NZ + k, rows, :] for k in range(NZ)]
            smooth, fine = forward_planes(x)
            smooth, middle = forward_planes(smooth)
            ext = pl.ds(pl.multiple_of(tile * 8 + 8, 8), 8)
            for slot, value in zip(slots[0] + slots[1] + slots[2], smooth + middle + fine):
                t_ref[slot, ext, :] = value
            return _

        lax.fori_loop(0, 8, lift, None)

    def pack(q):
        rightward = jnp.zeros((ROWS, 128), F32)
        leftward = jnp.zeros((ROWS, 128), F32)
        for j in range(CLASS):
            plane = t_ref[q * CLASS + j, 8:72, :]
            here = (lane >= 8 * j) & (lane < 8 * j + 8)
            rightward = jnp.where(here, pltpu.roll(plane, (8 * j + 8) % 128, 1), rightward)
            leftward = jnp.where(here, pltpu.roll(plane, 8 * j, 1) if j else plane, leftward)
        rp_ref[q] = rightward
        lp_ref[q] = leftward

    def send_halo(q, n):
        c = pl.ds(q, n)
        full = pl.ds(q * CLASS, CLASS)
        fine = pl.ds((q + 1) * CLASS, (n - 1) * CLASS)
        rows = [
            (t_ref.at[full, 64:72], t_ref.at[full, 0:8], (down, gy)),
            (t_ref.at[full, 8:16], t_ref.at[full, 72:80], (up, gy)),
        ]
        if n > 1:
            rows += [
                (t_ref.at[fine, 68:72], t_ref.at[fine, 4:8], (down, gy)),
                (t_ref.at[fine, 8:12], t_ref.at[fine, 72:76], (up, gy)),
            ]
        return batch(
            *rows,
            (rp_ref.at[c], hl_ref.at[c, 8:72], (gx, right)),
            (lp_ref.at[c], hr_ref.at[c, 8:72], (gx, left)),
            (rp_ref.at[c, 56:64], hl_ref.at[c, 0:8], (down, right)),
            (rp_ref.at[c, 0:8], hl_ref.at[c, 72:80], (up, right)),
            (lp_ref.at[c, 56:64], hr_ref.at[c, 0:8], (down, left)),
            (lp_ref.at[c, 0:8], hr_ref.at[c, 72:80], (up, left)),
        )

    pack(0)
    pl.semaphore_wait(barrier, len(greeted))
    halo0 = send_halo(0, 1)
    loads[VARS].wait()
    for q in (1, 2, 3):
        pack(q)
    halo1 = send_halo(1, 3)
    masks_in = Batch(nk_ref)
    for n, device in enumerate(around):
        masks_in.send(mk_ref, nk_ref.at[n], device)

    def expand_masks():
        below, above, from_right, from_left, below_right, below_left, above_right, above_left = (
            nk_ref.at[n] for n in range(8)
        )
        bands = [(above_left, above, above_right, 1), (from_left, mk_ref, from_right, 0),
                 (from_left, mk_ref, from_right, 1), (below_left, below, below_right, 0)]
        block = lax.broadcasted_iota(jnp.int32, (8, 128), 0)
        place = lax.broadcasted_iota(jnp.int32, (8, 128), 1)
        wide = [[], []]
        for level, spread_out in enumerate(((place + 14) // 16 == block, (place % 64 + 6) // 8 == block)):
            spread_out = jnp.where(spread_out, 1.0, 0.0)
            for n, (a, b, c, i) in enumerate(bands):
                j_ref[level, n] = jnp.zeros((8, 128), F32)
                j_ref[level, n, 0:1, 0:7] = a[level, i, 3:4].astype(F32)
                j_ref[level, n, 1:5, 0:7] = b[level, i].astype(F32)
                j_ref[level, n, 5:6, 0:7] = c[level, i, 0:1].astype(F32)
                wide[level].append(lax.dot_general(
                    j_ref[level, n], spread_out, (((0,), (0,)), ((), ())), preferred_element_type=F32))
        row = lax.broadcasted_iota(jnp.int32, (40, 128), 0)

        def by_rows(values, edges, count):
            out = jnp.broadcast_to(values[0], (count, 128))
            for value, edge in zip(values[1:], edges):
                out = jnp.where(row[:count] >= edge, jnp.broadcast_to(value, (count, 128)), out)
            return out

        for bz in range(2):
            for rd in range(2):
                for ld in range(2):
                    b = 4 * bz + 2 * ld + rd - 1
                    if b >= 0:
                        m1_ref[bz, rd, :, 128 * ld:128 * ld + 128] = by_rows(
                            [v[b:b + 1] for v in wide[0]], (3, 19, 35), 40)
                b = 4 * bz + rd - 1
                values = [jnp.where(lane < 64, v[b:b + 1] if b >= 0 else 1.0, v[b + 2:b + 3]) for v in wide[1]]
                m2_ref[bz, rd] = by_rows(values, (rd, 8 + rd, 16 + rd), 24)

    def sides_and_halves(q):
        for j in range(CLASS):
            sides = jnp.where(
                lane < 8, pltpu.roll(hr_ref[q], (128 - 8 * j) % 128, 1) if j else hr_ref[q],
                pltpu.roll(hl_ref[q], (136 - 8 * j) % 128, 1))
            for col, value in ((0, t_ref[q * CLASS + j]), (128, sides)):
                high, low_part = halves(value)
                lhs_ref[80 * j:80 * j + 80, col:col + 128] = high
                lhs_ref[80 * j:80 * j + 80, 256 + col:384 + col] = low_part

    def lanes1(q, parts=(0, 1)):
        cols = slice(128 * parts[0], 128 * parts[-1] + 128)
        filters = w_ref[0:256, cols]
        both = jnp.concatenate([filters, filters], 0)

        def step(i, _):
            rows = pl.ds(pl.multiple_of(i * 320, 320), 320)
            out = jnp.dot(lhs_ref[rows, :], both, preferred_element_type=F32)
            for n, half in enumerate(parts):
                y_ref[pl.ds(q * CLASS + 4 * i, 4), half, 0:80, :] = out[:, 128 * n:128 * n + 128].reshape(4, 80, 128)
            return _

        lax.fori_loop(0, 3, step, None)

    def coarse_part():
        both = jnp.concatenate([wc_ref[...], wc_ref[...]], 0)

        def step(i, _):
            rows = pl.ds(pl.multiple_of(i * 320, 320), 320)
            yc_ref[pl.ds(4 * i, 4)] = jnp.dot(lhs_ref[rows, :], both, preferred_element_type=F32).reshape(4, 80, 128)
            return _

        lax.fori_loop(0, 3, step, None)

        def lines(i, _):
            for n in range(4):
                p = 4 * i + n
                total = BOTH_SMOOTH[0] * yc_ref[p, pl.ds(8, 16, stride=4), :]
                for t in range(1, 7):
                    total += BOTH_SMOOTH[t] * (yc_ref[p, pl.ds(8 - t, 16, stride=4), :] + yc_ref[p, pl.ds(8 + t, 16, stride=4), :])
                own_ref[p] = total
            return _

        lax.fori_loop(0, 3, lines, None)

    def rows1(q):
        bz = 0 if q < 2 else 1

        def one(p):
            for half in range(2):
                cols = slice(128 * half, 128 * half + 128)
                even0, even1, even2 = (y_ref[p, half, pl.ds(s, 40, stride=2), :] for s in (0, 2, 4))
                odd0, odd1 = (y_ref[p, half, pl.ds(s, 40, stride=2), :] for s in (1, 3))
                detail = odd1 - 0.5 * (even1 + even2)
                before = odd0 - 0.5 * (even0 + even1)
                smooth = even1 + 0.25 * (before + detail)
                c_ref[p, 1, 0:40, cols] = detail * m1_ref[bz, 1, :, cols]
                if q < 2 and half == 0:
                    s1_ref[p] = smooth
                else:
                    c_ref[p, 0, 0:40, cols] = smooth * m1_ref[bz, 0, :, cols]

        def step(i, _):
            one(q * CLASS + 2 * i)
            one(q * CLASS + 2 * i + 1)
            return _

        lax.fori_loop(0, CLASS // 2, step, None)

    def lanes2(q):
        x = s1_ref[q * CLASS:(q + 1) * CLASS].reshape(CLASS * 40, 128)
        s1l_ref[q * CLASS:(q + 1) * CLASS, 0:40, :] = split_dot(x, w_ref[256:384, 128:256]).reshape(CLASS, 40, 128)

    def rows2(q):
        for p in range(q * CLASS, (q + 1) * CLASS):
            even0, even1, even2 = (s1l_ref[p, pl.ds(s, 24, stride=2), :] for s in (1, 3, 5))
            odd0, odd1 = (s1l_ref[p, pl.ds(s, 24, stride=2), :] for s in (2, 4))
            before = odd0 - 0.5 * (even0 + even1)
            detail = odd1 - 0.5 * (even1 + even2)
            smooth = even1 + 0.25 * (before + detail)
            c2_ref[p, 0, 0:24] = smooth * m2_ref[q, 0]
            c2_ref[p, 1, 0:24] = before * m2_ref[q, 1]

    def back2(q):
        for p in range(q * CLASS, (q + 1) * CLASS):
            smooth0, smooth1 = (c2_ref[p, 0, s:s + 24, :] for s in (0, 1))
            detail0, detail1, detail2 = (c2_ref[p, 1, s:s + 24, :] for s in (0, 1, 2))
            even = smooth0 - 0.25 * (detail0 + detail1)
            after = smooth1 - 0.25 * (detail1 + detail2)
            u_ref[p, pl.ds(3, 24, stride=2), :] = even
            u_ref[p, pl.ds(4, 24, stride=2), :] = detail1 + 0.5 * (even + after)
        x = u_ref[q * CLASS:(q + 1) * CLASS, 0:40, :].reshape(CLASS * 40, 128)
        c_ref[q * CLASS:(q + 1) * CLASS, 0, 0:40, 0:128] = split_dot(x, w_ref[384:512, 128:256]).reshape(CLASS, 40, 128)

    def back1(q):
        def one(p, j):
            for half in range(2):
                cols = slice(128 * half, 128 * half + 128)
                smooth0, smooth1 = (c_ref[p, 0, s:s + 32, cols] for s in (3, 4))
                detail0, detail1, detail2 = (c_ref[p, 1, s:s + 32, cols] for s in (2, 3, 4))
                even = smooth0 - 0.25 * (detail0 + detail1)
                after = smooth1 - 0.25 * (detail1 + detail2)
                odd = detail1 + 0.5 * (even + after)
                for which, value in ((0, even), (1, odd)):
                    rows = pl.ds(pl.multiple_of(j * 64 + 32 * which, 32), 32)
                    high, low_part = halves(value)
                    lhsi_ref[rows, cols] = high
                    lhsi_ref[rows, slice(256 + 128 * half, 384 + 128 * half)] = low_part

        def step(i, _):
            one(q * CLASS + 2 * i, 2 * i)
            one(q * CLASS + 2 * i + 1, 2 * i + 1)
            return _

        lax.fori_loop(0, CLASS // 2, step, None)
        filters = w_ref[256:512, 0:128]
        both = jnp.concatenate([filters, filters], 0)

        def multiply(i, _):
            rows = pl.ds(pl.multiple_of(i * 256, 256), 256)
            out = jnp.dot(lhsi_ref[rows, :], both, preferred_element_type=F32)
            zr_ref[pl.ds(q * CLASS + 4 * i, 4)] = out.reshape(4, 64, 128)
            return _

        lax.fori_loop(0, 3, multiply, None)

    def lanes_of(block):
        return pl.ds(pl.multiple_of(128 * ((block + 4) % 4), 128), 128)

    base = 6 * core
    p0, p1, p2 = (pl.ds(base + 2 * r, 2) for r in range(3))
    order = (1, 3, 2)

    def strip0(ky, kz, plane=p0):
        return g_ref.at[plane, (yy + ky + 4) % 4, :, :, lanes_of(group + kz)]

    def strip1(kx, ky=0):
        return g_ref.at[p1, (yy + ky + 4) % 4, (xx + kx + 4) % 4]

    def strip2(ky, kx=0):
        return g_ref.at[p2, (yy + ky + 4) % 4, (xx + kx + 4) % 4]

    def spread(view, axis, family="last"):
        return batch(*((view, view, axis(k)) for k in order), family=family)

    def ship0(ky):
        whole = strip0(ky, 0)
        half = strip0(ky, 0, base + low)
        return batch((whole, whole, cross), (half, half, along_z(3)), family="last")

    def relay0(ky, came):
        came.arrived()
        whole = strip0(ky, side)
        half = strip0(ky, 2, base + 1 - low)
        return batch((whole, whole, pair), (half, half, pair), family="last")

    def arrived(came):
        came.arrived()

    arrived(halo0)
    sides_and_halves(0)
    coarse_part()
    for tile in range(3):
        packed = own_ref[4 * tile]
        for j in range(1, 4):
            packed += pltpu.roll(own_ref[4 * tile + j], 32 * j, 1)
        pack_ref[tile] = packed
    other = 1 - core
    pre = batch(
        (pack_ref.at[pl.ds(other, 2)], parts_ref.at[0], (gx, flip1)),
        (pack_ref.at[pl.ds(core, 2)], parts_ref.at[1], (gx, flip2)),
        (pack_ref.at[pl.ds(other, 2)], parts_ref.at[2], (gx, flip3)),
    )
    lanes1(0)
    arrived(pre)
    for i in range(6):
        plane = base + i
        block = pltpu.roll(own_ref[plane], 32 * (gy % 4), 1)
        for n, partner in enumerate((flip1, flip2, flip3)):
            place = partner % 4
            came = pltpu.roll(parts_ref[n, plane // 4 - core], (32 * place - 32 * (plane % 4) + 128) % 128, 1)
            block = jnp.where(lane // 32 == place, came, block)
        g_ref[plane, yy, xx, :, lanes_of(group)] = block
    zs = spread(g_ref.at[pl.ds(base + 2, 4), yy, xx, :, lanes_of(group)], along_z, None)
    source0 = g_ref.at[p0, yy, xx, :, lanes_of(group)]
    mine0 = g_ref.at[p0, yy, xx, :, lanes_of(group)]
    flat0 = {}
    for ky in (0, 1, 3, 2):
        flat0[-ky] = batch(*((source0, mine0, in_plane(ky, kx)) for kx in (0, 1, 3, 2) if kx or ky), family="flat")
    arrived(masks_in)
    expand_masks()
    rows1(0)
    lanes2(0)
    rows2(0)
    back2(0)
    arrived(flat0[0])
    s0 = {0: ship0(0)}
    arrived(zs)
    xs1 = [batch((strip1(0), strip1(0), along_x(k)), family="middle") for k in order]
    ys2 = [batch((strip2(0), strip2(0), along_y(k)), family="middle") for k in order]
    ys1 = {0: spread(strip1(0), along_y)}
    xs2 = {0: spread(strip2(0), along_x)}
    arrived(flat0[-1])
    s0[-1] = ship0(-1)
    arrived(halo1)
    sides_and_halves(1)
    lanes1(1)
    rows1(1)
    arrived(flat0[-3])
    s0[-3] = ship0(-3)
    for n, k in enumerate(order):
        xs1[n].arrived()
        ys1[-k] = spread(strip1(-k), along_y)
        ys2[n].arrived()
        xs2[-k] = spread(strip2(-k), along_x)
    r0 = {}
    sib = Batch()

    def to_sibling(ref):
        sib.send(ref, ref, sibling)

    def complete(which):
        ys1[which].arrived()
        to_sibling(g_ref.at[p1, :, (xx + which + 4) % 4])
        xs2[which].arrived()
        to_sibling(g_ref.at[p2, (yy + which + 4) % 4])

    def complete0(which):
        r0[which].arrived()
        to_sibling(g_ref.at[p0, (yy + which + 4) % 4])

    arrived(flat0[-2])
    s0[-2] = ship0(-2)
    back1(0)
    r0[0] = relay0(0, s0[0])
    lanes2(1)
    rows2(1)
    back2(1)
    back1(1)
    r0[-1] = relay0(-1, s0[-1])
    sides_and_halves(2)
    lanes1(2)
    rows1(2)
    r0[-3] = relay0(-3, s0[-3])
    complete(0)
    back1(2)
    sides_and_halves(3)
    lanes1(3)
    complete0(0)
    complete(-1)
    r0[-2] = relay0(-2, s0[-2])
    rows1(3)
    complete0(-1)
    complete(-3)
    back1(3)
    complete0(-3)
    complete(-2)
    complete0(-2)
    arrived(sib)
    for at, tiles, size in families.values():
        await_tiles(send_sem.at[at], tiles, size)


def store(planes_ref, coarse_ref, restored_out, coarse_out, restored_ref, sem):
    copies = [pltpu.make_async_copy(coarse_ref.at[p], coarse_out.at[p], sem.at[p]) for p in range(12)]
    for copy in copies:
        copy.start()
    for var in range(VARS):
        slots = plane_slots(var)

        def lift(i, _, var=var, slots=slots):
            odd, tile = i // 4, i % 4
            rows = pl.ds(pl.multiple_of(8 * i, 8), 8)
            smooth, middle, fine = ([planes_ref[p, rows, :] for p in part] for part in slots)
            out = inverse_planes(inverse_planes(smooth, middle), fine)
            for k in range(NZ):
                restored_ref[var * NZ + k, pl.ds(16 * tile + odd, 8, stride=2), :] = out[k]
            return _

        lax.fori_loop(0, 8, lift, None)
        planes = pl.ds(NZ * var, NZ)
        copy = pltpu.make_async_copy(restored_ref.at[planes, 0:ROWS], restored_out.at[planes], sem.at[12 + var])
        copy.start()
        copies.append(copy)
    for copy in copies:
        copy.wait()


def body(field, masks):
    mk = pltpu.with_memory_space_constraint(masks.transpose(0, 2, 3, 1), pltpu.HBM)
    field = pltpu.with_memory_space_constraint(field.reshape(PLANES, ROWS, COLS), pltpu.HBM)
    anywhere = pl.BlockSpec(memory_space=pl.ANY)
    in_hbm = pl.BlockSpec(memory_space=pltpu.HBM)
    in_vmem = pl.BlockSpec(memory_space=pltpu.VMEM)
    planes, coarse = pl.pallas_call(
        kernel,
        out_shape=(
            jax.ShapeDtypeStruct((PLANES, ROWS, COLS), F32),
            jax.ShapeDtypeStruct((12, 4, 4, 16, 512), F32),
        ),
        in_specs=[in_hbm, in_hbm],
        out_specs=(in_vmem, in_vmem),
        scratch_shapes=[
            pltpu.VMEM((PLANES, ROWS, COLS), F32),
            pltpu.VMEM((2, 2, 4, 7), jnp.int32),
            pltpu.VMEM((512, 256), BF16),
            pltpu.VMEM((256, 128), BF16),
            pltpu.VMEM((CLASS, 80, 128), F32),
            pltpu.VMEM((PLANES, 80, 128), F32),
            pltpu.VMEM((4, ROWS, 128), F32),
            pltpu.VMEM((4, ROWS, 128), F32),
            pltpu.VMEM((4, 80, 128), F32),
            pltpu.VMEM((4, 80, 128), F32),
            pltpu.VMEM((8, 2, 2, 4, 7), jnp.int32),
            pltpu.VMEM((CLASS * 80, 512), BF16),
            pltpu.VMEM((PLANES, 2, 88, 128), F32),
            pltpu.VMEM((PLANES, 2, 40, 256), F32),
            pltpu.VMEM((2 * CLASS, 40, 128), F32),
            pltpu.VMEM((2 * CLASS, 56, 128), F32),
            pltpu.VMEM((2 * CLASS, 2, 32, 128), F32),
            pltpu.VMEM((2 * CLASS, 56, 128), F32),
            pltpu.VMEM((2, 2, 40, 256), F32),
            pltpu.VMEM((2, 2, 24, 128), F32),
            pltpu.VMEM((CLASS, 16, 128), F32),
            pltpu.VMEM((3, 2, 16, 128), F32),
            pltpu.VMEM((3, 16, 128), F32),
            pltpu.VMEM((CLASS * 64, 512), BF16),
            pltpu.VMEM((2, 4, 8, 128), F32),
            pltpu.SemaphoreType.DMA((VARS + 1,)),
            pltpu.SemaphoreType.DMA((FAMILIES,)),
            pltpu.SemaphoreType.DMA((BATCHES,)),
        ],
        compiler_params=pltpu.CompilerParams(
            collective_id=0, has_side_effects=True, vmem_limit_bytes=VMEM_LIMIT
        ),
        cost_estimate=pl.CostEstimate(flops=2_000_000_000, bytes_accessed=10_000_000, transcendentals=0),
    )(field, mk)
    restored, coarse = pl.pallas_call(
        store,
        out_shape=(
            jax.ShapeDtypeStruct((PLANES, ROWS, COLS), F32),
            jax.ShapeDtypeStruct(coarse.shape, F32),
        ),
        in_specs=[in_vmem, anywhere],
        out_specs=(in_hbm, in_hbm),
        scratch_shapes=[pltpu.VMEM((PLANES, ROWS + 8, COLS), F32), pltpu.SemaphoreType.DMA((12 + VARS,))],
        compiler_params=pltpu.CompilerParams(vmem_limit_bytes=5 * 1024 * 1024),
    )(planes, coarse)
    return restored.reshape(VARS, NZ, ROWS, COLS), coarse.reshape(VARS, 4, 256, 512)


def solution(mesh):
    placed = (P(None, None, "gx", "gy"), P(None, None, "gx", "gy"))
    return jax.shard_map(
        body,
        mesh=mesh,
        in_specs=placed,
        out_specs=(P(None, None, "gx", "gy"), P()),
        check_vma=False,
    )
```

```python
import math

import jax
import jax.numpy as jnp
from jax import lax
from jax.experimental import pallas as pl
from jax.experimental.pallas import tpu as pltpu
from jax.sharding import PartitionSpec as P

MESH = pl.DeviceIdType.MESH
F32 = jnp.float32
BF16 = jnp.bfloat16
VARS, NZ, ROWS, COLS = 3, 16, 64, 128
PLANES = VARS * NZ
CLASS = 12
BATCHES = 32
FAMILIES = 9
VMEM_LIMIT = 32 * 1024 * 1024


def by_distance(distance, taps):
    out = jnp.zeros(distance.shape, F32)
    for at, weight in taps.items():
        out = jnp.where(distance == at, weight, out)
    return out


FORWARD_SMOOTH = {0: 0.75, -2: -0.125, 2: -0.125, -1: 0.25, 1: 0.25}
BOTH_SMOOTH = {}
for _a, _v in FORWARD_SMOOTH.items():
    for _b, _w in FORWARD_SMOOTH.items():
        BOTH_SMOOTH[_a + 2 * _b] = BOTH_SMOOTH.get(_a + 2 * _b, 0.0) + _v * _w
FORWARD_DETAIL = {0: -0.5, 1: 1.0, 2: -0.5}
INVERSE_SMOOTH = {0: 1.0, -1: 0.5, 1: 0.5}
INVERSE_DETAIL = {1: 0.75, 0: -0.25, 2: -0.25, -1: -0.125, 3: -0.125}


def write_filters(w_ref, wc_ref):
    row = lax.broadcasted_iota(jnp.int32, (256, 128), 0)
    col = lax.broadcasted_iota(jnp.int32, (256, 128), 1)
    cell = jnp.where(row < 136, row, jnp.where(row < 144, row - 144, 4096))
    w_ref[0:256, 0:128] = by_distance(cell - 2 * (col - 2), FORWARD_SMOOTH).astype(BF16)
    w_ref[0:256, 128:256] = by_distance(cell - 2 * (col - 2), FORWARD_DETAIL).astype(BF16)
    w_ref[256:384, 0:128] = by_distance(col[:128] - 2 * (row[:128] - 2), INVERSE_SMOOTH).astype(BF16)
    w_ref[384:512, 0:128] = by_distance(col[:128] - 2 * (row[:128] - 2), INVERSE_DETAIL).astype(BF16)
    away = jnp.where(col < 32, jnp.abs(cell - 4 * col), 4096)
    wc_ref[...] = by_distance(away, {t: w for t, w in BOTH_SMOOTH.items() if t >= 0}).astype(BF16)
    row, col = row[:128], col[:128]
    ahead = row - 2 - 2 * (jnp.where(col < 64, col, col - 64) - 2)
    w_ref[256:384, 128:256] = jnp.where(
        col < 64, by_distance(ahead, FORWARD_SMOOTH), by_distance(ahead, FORWARD_DETAIL)).astype(BF16)
    ahead = col - 2 - 2 * (jnp.where(row < 64, row, row - 64) - 2)
    w_ref[384:512, 128:256] = jnp.where(
        row < 64, by_distance(ahead, INVERSE_SMOOTH), by_distance(ahead, INVERSE_DETAIL)).astype(BF16)


def halves(x):
    high = x.astype(BF16)
    low = (x - high.astype(F32)).astype(BF16)
    return high, low


def split_dot(x, filters):
    high, low = halves(x)
    return jnp.dot(high, filters, preferred_element_type=F32) + jnp.dot(low, filters, preferred_element_type=F32)


def forward_planes(x):
    count = len(x) // 2
    detail = []
    for k in range(count):
        after = x[2 * k + 2] if k + 1 < count else x[2 * count - 2]
        detail.append(x[2 * k + 1] - 0.5 * (x[2 * k] + after))
    smooth = [x[2 * k] + 0.25 * (detail[max(k - 1, 0)] + detail[k]) for k in range(count)]
    return smooth, detail


def inverse_planes(smooth, detail):
    count = len(smooth)
    even = [smooth[k] - 0.25 * (detail[max(k - 1, 0)] + detail[k]) for k in range(count)]
    out = []
    for k in range(count):
        out += [even[k], detail[k] + 0.5 * (even[k] + even[min(k + 1, count - 1)])]
    return out


def plane_slots(var):
    smooth = [4 * var + k for k in range(4)]
    middle = [12 + 4 * var + k for k in range(4)]
    fine = [24 + 8 * var + k for k in range(8)]
    return smooth, middle, fine


def kernel(
    field_ref, masks_ref, zr_ref, g_ref,
    x_ref, mk_ref, w_ref, wc_ref, yc_ref, t_ref, rp_ref, lp_ref, hl_ref, hr_ref, nk_ref, lhs_ref, y_ref, c_ref, s1_ref, s1l_ref, c2_ref,
    u_ref, m1_ref, m2_ref, own_ref, parts_ref, pack_ref, lhsi_ref, j_ref, load_sem, send_sem, recv_sem,
):
    gx = lax.axis_index("gx")
    gy = lax.axis_index("gy")
    yy, xx = gx // 4, gx % 4
    zz, core = gy // 2, gy % 2
    group, low = gy // 4, zz % 2
    side = 2 * low - 1

    up, down = (gx + 15) % 16, (gx + 1) % 16
    left, right = (gy + 15) % 16, (gy + 1) % 16
    around = [(up, gy), (down, gy), (gx, left), (gx, right), (up, left), (up, right), (down, left), (down, right)]
    flip1 = gy + 1 - 2 * core
    flip2 = gy + 2 - 4 * low
    flip3 = flip2 + 1 - 2 * core
    sibling = (gx, flip1)
    pair = (gx, flip2)
    cross = (gx, (gy + 2 * side + 16) % 16)

    def along_x(k):
        return (yy * 4 + (xx + k) % 4, gy)

    def along_y(k):
        return (((yy + k) % 4) * 4 + xx, gy)

    def in_plane(ky, kx):
        return (((yy + ky) % 4) * 4 + (xx + kx) % 4, gy)

    def along_z(k):
        return (gx, (gy + 2 * side * k + 16) % 16)

    greeted = around + [(gx, flip1), (gx, flip2), (gx, flip3)]
    greeted += [along_x(k) for k in (1, 2, 3)] + [along_y(k) for k in (1, 2, 3)]
    greeted += [along_z(k) for k in (1, 2, -2, 3)]
    greeted += [in_plane(ky, kx) for ky in (1, 2, 3) for kx in (1, 2, 3)]

    loads = [
        pltpu.make_async_copy(field_ref.at[NZ * v:NZ * v + NZ], x_ref.at[NZ * v:NZ * v + NZ], load_sem.at[v])
        for v in range(VARS)
    ]
    loads.append(pltpu.make_async_copy(masks_ref, mk_ref, load_sem.at[VARS]))
    for copy in loads:
        copy.start()
    barrier = pltpu.get_barrier_semaphore()
    for device in greeted:
        pl.semaphore_signal(barrier, inc=1, device_id=device, device_id_type=MESH)

    write_filters(w_ref, wc_ref)
    batches = []
    families = {}

    def await_tiles(sem, tiles, size=None):
        if size is None and tiles == 768:
            size = g_ref.at[0:6]
        elif size is None and tiles == 576:
            size = g_ref.at[0:9, 0:2]
        elif size is None:
            high = max(h for h in range(1, 9) if tiles % h == 0)
            size = x_ref.at[0:tiles // high, 0:8 * high]
        pltpu.make_async_copy(size, size, sem).wait()

    class Batch:
        def __init__(self, sized=None, family=None):
            self.at, self.tiles, self.sized = len(batches), 0, sized
            batches.append(self)
            self.out = families.setdefault(family or self.at, [len(families), 0, sized])

        def send(self, src, dst, device):
            pltpu.make_async_remote_copy(
                src_ref=src, dst_ref=dst, send_sem=send_sem.at[self.out[0]], recv_sem=recv_sem.at[self.at],
                device_id=device, device_id_type=MESH,
            ).start()
            if self.sized is None:
                self.tiles += math.prod(src.shape) // 1024
                self.out[1] += math.prod(src.shape) // 1024

        def arrived(self):
            await_tiles(recv_sem.at[self.at], self.tiles, self.sized)

    def batch(*copies, family=None):
        out = Batch(family=family)
        for copy in copies:
            out.send(*copy)
        return out

    lane = lax.broadcasted_iota(jnp.int32, (1, 128), 1)

    for var in range(VARS):
        slots = plane_slots(var)
        loads[var].wait()

        def lift(tile, _, var=var, slots=slots):
            rows = pl.ds(pl.multiple_of(tile * 8, 8), 8)
            x = [x_ref[var * NZ + k, rows, :] for k in range(NZ)]
            smooth, fine = forward_planes(x)
            smooth, middle = forward_planes(smooth)
            ext = pl.ds(pl.multiple_of(tile * 8 + 8, 8), 8)
            for slot, value in zip(slots[0] + slots[1] + slots[2], smooth + middle + fine):
                t_ref[slot, ext, :] = value
            return _

        lax.fori_loop(0, 8, lift, None)

    def pack(q):
        rightward = jnp.zeros((ROWS, 128), F32)
        leftward = jnp.zeros((ROWS, 128), F32)
        for j in range(CLASS):
            plane = t_ref[q * CLASS + j, 8:72, :]
            here = (lane >= 8 * j) & (lane < 8 * j + 8)
            rightward = jnp.where(here, pltpu.roll(plane, (8 * j + 8) % 128, 1), rightward)
            leftward = jnp.where(here, pltpu.roll(plane, 8 * j, 1) if j else plane, leftward)
        rp_ref[q] = rightward
        lp_ref[q] = leftward

    def send_halo(q, n):
        c = pl.ds(q, n)
        full = pl.ds(q * CLASS, CLASS)
        fine = pl.ds((q + 1) * CLASS, (n - 1) * CLASS)
        rows = [
            (t_ref.at[full, 64:72], t_ref.at[full, 0:8], (down, gy)),
            (t_ref.at[full, 8:16], t_ref.at[full, 72:80], (up, gy)),
        ]
        if n > 1:
            rows += [
                (t_ref.at[fine, 68:72], t_ref.at[fine, 4:8], (down, gy)),
                (t_ref.at[fine, 8:12], t_ref.at[fine, 72:76], (up, gy)),
            ]
        return batch(
            *rows,
            (rp_ref.at[c], hl_ref.at[c, 8:72], (gx, right)),
            (lp_ref.at[c], hr_ref.at[c, 8:72], (gx, left)),
            (rp_ref.at[c, 56:64], hl_ref.at[c, 0:8], (down, right)),
            (rp_ref.at[c, 0:8], hl_ref.at[c, 72:80], (up, right)),
            (lp_ref.at[c, 56:64], hr_ref.at[c, 0:8], (down, left)),
            (lp_ref.at[c, 0:8], hr_ref.at[c, 72:80], (up, left)),
        )

    pack(0)
    pl.semaphore_wait(barrier, len(greeted))
    halo0 = send_halo(0, 1)
    loads[VARS].wait()
    for q in (1, 2, 3):
        pack(q)
    masks_in = Batch(nk_ref)
    for n, device in enumerate(around):
        masks_in.send(mk_ref, nk_ref.at[n], device)

    def expand_masks():
        below, above, from_right, from_left, below_right, below_left, above_right, above_left = (
            nk_ref.at[n] for n in range(8)
        )
        bands = [(above_left, above, above_right, 1), (from_left, mk_ref, from_right, 0),
                 (from_left, mk_ref, from_right, 1), (below_left, below, below_right, 0)]
        block = lax.broadcasted_iota(jnp.int32, (8, 128), 0)
        place = lax.broadcasted_iota(jnp.int32, (8, 128), 1)
        wide = [[], []]
        for level, spread_out in enumerate(((place + 14) // 16 == block, (place % 64 + 6) // 8 == block)):
            spread_out = jnp.where(spread_out, 1.0, 0.0)
            for n, (a, b, c, i) in enumerate(bands):
                j_ref[level, n] = jnp.zeros((8, 128), F32)
                j_ref[level, n, 0:1, 0:7] = a[level, i, 3:4].astype(F32)
                j_ref[level, n, 1:5, 0:7] = b[level, i].astype(F32)
                j_ref[level, n, 5:6, 0:7] = c[level, i, 0:1].astype(F32)
                wide[level].append(lax.dot_general(
                    j_ref[level, n], spread_out, (((0,), (0,)), ((), ())), preferred_element_type=F32))
        row = lax.broadcasted_iota(jnp.int32, (40, 128), 0)

        def by_rows(values, edges, count):
            out = jnp.broadcast_to(values[0], (count, 128))
            for value, edge in zip(values[1:], edges):
                out = jnp.where(row[:count] >= edge, jnp.broadcast_to(value, (count, 128)), out)
            return out

        for bz in range(2):
            for rd in range(2):
                for ld in range(2):
                    b = 4 * bz + 2 * ld + rd - 1
                    if b >= 0:
                        m1_ref[bz, rd, :, 128 * ld:128 * ld + 128] = by_rows(
                            [v[b:b + 1] for v in wide[0]], (3, 19, 35), 40)
                b = 4 * bz + rd - 1
                values = [jnp.where(lane < 64, v[b:b + 1] if b >= 0 else 1.0, v[b + 2:b + 3]) for v in wide[1]]
                m2_ref[bz, rd] = by_rows(values, (rd, 8 + rd, 16 + rd), 24)

    def sides_and_halves(q):
        for j in range(CLASS):
            sides = jnp.where(
                lane < 8, pltpu.roll(hr_ref[q], (128 - 8 * j) % 128, 1) if j else hr_ref[q],
                pltpu.roll(hl_ref[q], (136 - 8 * j) % 128, 1))
            for col, value in ((0, t_ref[q * CLASS + j]), (128, sides)):
                high, low_part = halves(value)
                lhs_ref[80 * j:80 * j + 80, col:col + 128] = high
                lhs_ref[80 * j:80 * j + 80, 256 + col:384 + col] = low_part

    def lanes1(q, parts=(0, 1)):
        cols = slice(128 * parts[0], 128 * parts[-1] + 128)
        filters = w_ref[0:256, cols]
        both = jnp.concatenate([filters, filters], 0)

        def step(i, _):
            rows = pl.ds(pl.multiple_of(i * 320, 320), 320)
            out = jnp.dot(lhs_ref[rows, :], both, preferred_element_type=F32)
            for n, half in enumerate(parts):
                y_ref[pl.ds(q * CLASS + 4 * i, 4), half, 0:80, :] = out[:, 128 * n:128 * n + 128].reshape(4, 80, 128)
            return _

        lax.fori_loop(0, 3, step, None)

    def coarse_part():
        both = jnp.concatenate([wc_ref[...], wc_ref[...]], 0)

        def step(i, _):
            rows = pl.ds(pl.multiple_of(i * 320, 320), 320)
            yc_ref[pl.ds(4 * i, 4)] = jnp.dot(lhs_ref[rows, :], both, preferred_element_type=F32).reshape(4, 80, 128)
            return _

        lax.fori_loop(0, 3, step, None)

        def lines(i, _):
            for n in range(4):
                p = 4 * i + n
                total = BOTH_SMOOTH[0] * yc_ref[p, pl.ds(8, 16, stride=4), :]
                for t in range(1, 7):
                    total += BOTH_SMOOTH[t] * (yc_ref[p, pl.ds(8 - t, 16, stride=4), :] + yc_ref[p, pl.ds(8 + t, 16, stride=4), :])
                own_ref[p] = total
            return _

        lax.fori_loop(0, 3, lines, None)

    def rows1(q):
        bz = 0 if q < 2 else 1

        def one(p):
            for half in range(2):
                cols = slice(128 * half, 128 * half + 128)
                even0, even1, even2 = (y_ref[p, half, pl.ds(s, 40, stride=2), :] for s in (0, 2, 4))
                odd0, odd1 = (y_ref[p, half, pl.ds(s, 40, stride=2), :] for s in (1, 3))
                detail = odd1 - 0.5 * (even1 + even2)
                before = odd0 - 0.5 * (even0 + even1)
                smooth = even1 + 0.25 * (before + detail)
                c_ref[p, 1, 0:40, cols] = detail * m1_ref[bz, 1, :, cols]
                if q < 2 and half == 0:
                    s1_ref[p] = smooth
                else:
                    c_ref[p, 0, 0:40, cols] = smooth * m1_ref[bz, 0, :, cols]

        def step(i, _):
            one(q * CLASS + 2 * i)
            one(q * CLASS + 2 * i + 1)
            return _

        lax.fori_loop(0, CLASS // 2, step, None)

    def lanes2(q):
        x = s1_ref[q * CLASS:(q + 1) * CLASS].reshape(CLASS * 40, 128)
        s1l_ref[q * CLASS:(q + 1) * CLASS, 0:40, :] = split_dot(x, w_ref[256:384, 128:256]).reshape(CLASS, 40, 128)

    def rows2(q):
        for p in range(q * CLASS, (q + 1) * CLASS):
            even0, even1, even2 = (s1l_ref[p, pl.ds(s, 24, stride=2), :] for s in (1, 3, 5))
            odd0, odd1 = (s1l_ref[p, pl.ds(s, 24, stride=2), :] for s in (2, 4))
            before = odd0 - 0.5 * (even0 + even1)
            detail = odd1 - 0.5 * (even1 + even2)
            smooth = even1 + 0.25 * (before + detail)
            c2_ref[p, 0, 0:24] = smooth * m2_ref[q, 0]
            c2_ref[p, 1, 0:24] = before * m2_ref[q, 1]

    def back2(q):
        for p in range(q * CLASS, (q + 1) * CLASS):
            smooth0, smooth1 = (c2_ref[p, 0, s:s + 24, :] for s in (0, 1))
            detail0, detail1, detail2 = (c2_ref[p, 1, s:s + 24, :] for s in (0, 1, 2))
            even = smooth0 - 0.25 * (detail0 + detail1)
            after = smooth1 - 0.25 * (detail1 + detail2)
            u_ref[p, pl.ds(3, 24, stride=2), :] = even
            u_ref[p, pl.ds(4, 24, stride=2), :] = detail1 + 0.5 * (even + after)
        x = u_ref[q * CLASS:(q + 1) * CLASS, 0:40, :].reshape(CLASS * 40, 128)
        c_ref[q * CLASS:(q + 1) * CLASS, 0, 0:40, 0:128] = split_dot(x, w_ref[384:512, 128:256]).reshape(CLASS, 40, 128)

    def back1(q):
        def one(p, j):
            for half in range(2):
                cols = slice(128 * half, 128 * half + 128)
                smooth0, smooth1 = (c_ref[p, 0, s:s + 32, cols] for s in (3, 4))
                detail0, detail1, detail2 = (c_ref[p, 1, s:s + 32, cols] for s in (2, 3, 4))
                even = smooth0 - 0.25 * (detail0 + detail1)
                after = smooth1 - 0.25 * (detail1 + detail2)
                odd = detail1 + 0.5 * (even + after)
                for which, value in ((0, even), (1, odd)):
                    rows = pl.ds(pl.multiple_of(j * 64 + 32 * which, 32), 32)
                    high, low_part = halves(value)
                    lhsi_ref[rows, cols] = high
                    lhsi_ref[rows, slice(256 + 128 * half, 384 + 128 * half)] = low_part

        def step(i, _):
            one(q * CLASS + 2 * i, 2 * i)
            one(q * CLASS + 2 * i + 1, 2 * i + 1)
            return _

        lax.fori_loop(0, CLASS // 2, step, None)
        filters = w_ref[256:512, 0:128]
        both = jnp.concatenate([filters, filters], 0)

        def multiply(i, _):
            rows = pl.ds(pl.multiple_of(i * 256, 256), 256)
            out = jnp.dot(lhsi_ref[rows, :], both, preferred_element_type=F32)
            zr_ref[pl.ds(q * CLASS + 4 * i, 4)] = out.reshape(4, 64, 128)
            return _

        lax.fori_loop(0, 3, multiply, None)

    def lanes_of(block):
        return pl.ds(pl.multiple_of(128 * ((block + 4) % 4), 128), 128)

    base = 6 * core
    p0, p1, p2 = (pl.ds(base + 2 * r, 2) for r in range(3))
    order = (1, 3, 2)

    def strip0(ky, kz, plane=p0):
        return g_ref.at[plane, (yy + ky + 4) % 4, :, :, lanes_of(group + kz)]

    def strip1(kx, ky=0):
        return g_ref.at[p1, (yy + ky + 4) % 4, (xx + kx + 4) % 4]

    def strip2(ky, kx=0):
        return g_ref.at[p2, (yy + ky + 4) % 4, (xx + kx + 4) % 4]

    def spread(view, axis, family="last"):
        return batch(*((view, view, axis(k)) for k in order), family=family)

    def ship0(ky):
        whole = strip0(ky, 0)
        half = strip0(ky, 0, base + low)
        return batch((whole, whole, cross), (half, half, along_z(3)), family="last")

    def relay0(ky, came):
        came.arrived()
        whole = strip0(ky, side)
        half = strip0(ky, 2, base + 1 - low)
        return batch((whole, whole, pair), (half, half, pair), family="last")

    def arrived(came):
        came.arrived()

    arrived(halo0)
    halo1 = send_halo(1, 3)
    sides_and_halves(0)
    coarse_part()
    for tile in range(3):
        packed = own_ref[4 * tile]
        for j in range(1, 4):
            packed += pltpu.roll(own_ref[4 * tile + j], 32 * j, 1)
        pack_ref[tile] = packed
    other = 1 - core
    pre = batch(
        (pack_ref.at[pl.ds(other, 2)], parts_ref.at[0], (gx, flip1)),
        (pack_ref.at[pl.ds(core, 2)], parts_ref.at[1], (gx, flip2)),
        (pack_ref.at[pl.ds(other, 2)], parts_ref.at[2], (gx, flip3)),
    )
    lanes1(0)
    arrived(pre)
    for i in range(6):
        plane = base + i
        block = pltpu.roll(own_ref[plane], 32 * (gy % 4), 1)
        for n, partner in enumerate((flip1, flip2, flip3)):
            place = partner % 4
            came = pltpu.roll(parts_ref[n, plane // 4 - core], (32 * place - 32 * (plane % 4) + 128) % 128, 1)
            block = jnp.where(lane // 32 == place, came, block)
        g_ref[plane, yy, xx, :, lanes_of(group)] = block
    zs = spread(g_ref.at[pl.ds(base + 2, 4), yy, xx, :, lanes_of(group)], along_z, None)
    source0 = g_ref.at[p0, yy, xx, :, lanes_of(group)]
    mine0 = g_ref.at[p0, yy, xx, :, lanes_of(group)]
    flat0 = {}
    for ky in (0, 1, 3, 2):
        flat0[-ky] = batch(*((source0, mine0, in_plane(ky, kx)) for kx in (0, 1, 3, 2) if kx or ky), family="flat")
    arrived(masks_in)
    expand_masks()
    rows1(0)
    lanes2(0)
    rows2(0)
    back2(0)
    arrived(flat0[0])
    s0 = {0: ship0(0)}
    arrived(zs)
    xs1 = [batch((strip1(0), strip1(0), along_x(k)), family="middle") for k in order]
    ys2 = [batch((strip2(0), strip2(0), along_y(k)), family="middle") for k in order]
    ys1 = {0: spread(strip1(0), along_y)}
    xs2 = {0: spread(strip2(0), along_x)}
    arrived(flat0[-1])
    s0[-1] = ship0(-1)
    arrived(halo1)
    sides_and_halves(1)
    lanes1(1)
    rows1(1)
    arrived(flat0[-3])
    s0[-3] = ship0(-3)
    for n, k in enumerate(order):
        xs1[n].arrived()
        ys1[-k] = spread(strip1(-k), along_y)
        ys2[n].arrived()
        xs2[-k] = spread(strip2(-k), along_x)
    r0 = {}
    sib = Batch()

    def to_sibling(ref):
        sib.send(ref, ref, sibling)

    def complete(which):
        ys1[which].arrived()
        to_sibling(g_ref.at[p1, :, (xx + which + 4) % 4])
        xs2[which].arrived()
        to_sibling(g_ref.at[p2, (yy + which + 4) % 4])

    def complete0(which):
        r0[which].arrived()
        to_sibling(g_ref.at[p0, (yy + which + 4) % 4])

    arrived(flat0[-2])
    s0[-2] = ship0(-2)
    back1(0)
    r0[0] = relay0(0, s0[0])
    lanes2(1)
    rows2(1)
    back2(1)
    back1(1)
    r0[-1] = relay0(-1, s0[-1])
    sides_and_halves(2)
    lanes1(2)
    rows1(2)
    r0[-3] = relay0(-3, s0[-3])
    complete(0)
    back1(2)
    sides_and_halves(3)
    lanes1(3)
    complete0(0)
    complete(-1)
    r0[-2] = relay0(-2, s0[-2])
    rows1(3)
    complete0(-1)
    complete(-3)
    back1(3)
    complete0(-3)
    complete(-2)
    complete0(-2)
    arrived(sib)
    for at, tiles, size in families.values():
        await_tiles(send_sem.at[at], tiles, size)


def store(planes_ref, coarse_ref, restored_out, coarse_out, restored_ref, sem):
    copies = [pltpu.make_async_copy(coarse_ref.at[p], coarse_out.at[p], sem.at[p]) for p in range(12)]
    for copy in copies:
        copy.start()
    for var in range(VARS):
        slots = plane_slots(var)

        def lift(i, _, var=var, slots=slots):
            odd, tile = i // 4, i % 4
            rows = pl.ds(pl.multiple_of(8 * i, 8), 8)
            smooth, middle, fine = ([planes_ref[p, rows, :] for p in part] for part in slots)
            out = inverse_planes(inverse_planes(smooth, middle), fine)
            for k in range(NZ):
                restored_ref[var * NZ + k, pl.ds(16 * tile + odd, 8, stride=2), :] = out[k]
            return _

        lax.fori_loop(0, 8, lift, None)
        planes = pl.ds(NZ * var, NZ)
        copy = pltpu.make_async_copy(restored_ref.at[planes, 0:ROWS], restored_out.at[planes], sem.at[12 + var])
        copy.start()
        copies.append(copy)
    for copy in copies:
        copy.wait()


def body(field, masks):
    mk = pltpu.with_memory_space_constraint(masks.transpose(0, 2, 3, 1), pltpu.HBM)
    field = pltpu.with_memory_space_constraint(field.reshape(PLANES, ROWS, COLS), pltpu.HBM)
    anywhere = pl.BlockSpec(memory_space=pl.ANY)
    in_hbm = pl.BlockSpec(memory_space=pltpu.HBM)
    in_vmem = pl.BlockSpec(memory_space=pltpu.VMEM)
    planes, coarse = pl.pallas_call(
        kernel,
        out_shape=(
            jax.ShapeDtypeStruct((PLANES, ROWS, COLS), F32),
            jax.ShapeDtypeStruct((12, 4, 4, 16, 512), F32),
        ),
        in_specs=[in_hbm, in_hbm],
        out_specs=(in_vmem, in_vmem),
        scratch_shapes=[
            pltpu.VMEM((PLANES, ROWS, COLS), F32),
            pltpu.VMEM((2, 2, 4, 7), jnp.int32),
            pltpu.VMEM((512, 256), BF16),
            pltpu.VMEM((256, 128), BF16),
            pltpu.VMEM((CLASS, 80, 128), F32),
            pltpu.VMEM((PLANES, 80, 128), F32),
            pltpu.VMEM((4, ROWS, 128), F32),
            pltpu.VMEM((4, ROWS, 128), F32),
            pltpu.VMEM((4, 80, 128), F32),
            pltpu.VMEM((4, 80, 128), F32),
            pltpu.VMEM((8, 2, 2, 4, 7), jnp.int32),
            pltpu.VMEM((CLASS * 80, 512), BF16),
            pltpu.VMEM((PLANES, 2, 88, 128), F32),
            pltpu.VMEM((PLANES, 2, 40, 256), F32),
            pltpu.VMEM((2 * CLASS, 40, 128), F32),
            pltpu.VMEM((2 * CLASS, 56, 128), F32),
            pltpu.VMEM((2 * CLASS, 2, 32, 128), F32),
            pltpu.VMEM((2 * CLASS, 56, 128), F32),
            pltpu.VMEM((2, 2, 40, 256), F32),
            pltpu.VMEM((2, 2, 24, 128), F32),
            pltpu.VMEM((CLASS, 16, 128), F32),
            pltpu.VMEM((3, 2, 16, 128), F32),
            pltpu.VMEM((3, 16, 128), F32),
            pltpu.VMEM((CLASS * 64, 512), BF16),
            pltpu.VMEM((2, 4, 8, 128), F32),
            pltpu.SemaphoreType.DMA((VARS + 1,)),
            pltpu.SemaphoreType.DMA((FAMILIES,)),
            pltpu.SemaphoreType.DMA((BATCHES,)),
        ],
        compiler_params=pltpu.CompilerParams(
            collective_id=0, has_side_effects=True, vmem_limit_bytes=VMEM_LIMIT
        ),
        cost_estimate=pl.CostEstimate(flops=2_000_000_000, bytes_accessed=10_000_000, transcendentals=0),
    )(field, mk)
    restored, coarse = pl.pallas_call(
        store,
        out_shape=(
            jax.ShapeDtypeStruct((PLANES, ROWS, COLS), F32),
            jax.ShapeDtypeStruct(coarse.shape, F32),
        ),
        in_specs=[in_vmem, anywhere],
        out_specs=(in_hbm, in_hbm),
        scratch_shapes=[pltpu.VMEM((PLANES, ROWS + 8, COLS), F32), pltpu.SemaphoreType.DMA((12 + VARS,))],
        compiler_params=pltpu.CompilerParams(vmem_limit_bytes=5 * 1024 * 1024),
    )(planes, coarse)
    return restored.reshape(VARS, NZ, ROWS, COLS), coarse.reshape(VARS, 4, 256, 512)


def solution(mesh):
    placed = (P(None, None, "gx", "gy"), P(None, None, "gx", "gy"))
    return jax.shard_map(
        body,
        mesh=mesh,
        in_specs=placed,
        out_specs=(P(None, None, "gx", "gy"), P()),
        check_vma=False,
    )
```
